32 devices in a mesh: grp: 2 (over x), chol: 16 (over z, y, core).
Axes of the slice: x: 2, y: 2, z: 4, core: 2. Of those that a mesh axis runs over, the one named last changes fastest.
Arguments:
- theta: bfloat16 [32, 64, 1280], P(('grp', 'chol')), parts along dimension 0
- chol_tiles: bfloat16 [16, 4, 32, 64, 128], P('chol')
- screen: int32 [16, 4], P('chol'), may hold values 0 or 1
- tile_list: int32 [16, 4], replicated, may hold values from 0 to 9, as said below
Outputs:
- force_bias: float32 [32, 512], P(('grp', 'chol')), parts along dimension 0
- energy: float32 [32], P(('grp', 'chol')), parts along dimension 0
The draws below stay inside these ranges and needn't reach their ends.
There are 2 independent parts, one for each index of `grp`. The reference program is written for one: setup_inputs(seed, part) draws one part's arguments, and reference() takes and returns one part's arrays. A program takes and returns all parts, laid end to end along the dimension named above; an argument that names none is the same for every part. Nothing has to cross between parts.
Inputs may be any that keep to these rules, and one draw needn't show every extreme that they name: `tile_list`: each row holds 4 different tiles.
All inputs are finite; a program needn't handle non-finite values. No bound on the sum of `screen` on one device may be relied on, other than what follows from the above.
Results may differ from the reference program's by a relative error of at most 0.0003.
Values may be sent and summed in bfloat16 or wider, within the bound.
No kernel may reach another device: no remote copies, remote signals or barrier semaphores. Data moves between devices by JAX's collectives and lax.ppermute only.
A program may use at most 128 MiB of HBM per device.

```python
import jax
import jax.numpy as jnp
from jax import lax

NOCC = 64
TILE = 128
NT = 10
MAXT = 4
KB = 32
BLK_DEV = 1
GROUPS = 16
W = 16
NBLK = 16
NORB = 1280


def draw_tile_list(key, part):
    key = jax.random.fold_in(key, 7)
    sub_keys = jax.random.split(key, GROUPS)

    def pick_row(sub_key):
        return jax.random.permutation(sub_key, NT)[:MAXT]
    chosen = jax.vmap(pick_row)(sub_keys)
    return chosen.astype(jnp.int32)


def draw_theta(key, part):
    key = jax.random.fold_in(key, 11)
    noise = jnp.clip(jax.random.normal(key, (W, NOCC, NORB), jnp.float32), -6.0, 6.0)
    rows = lax_iota_rows()
    columns = jnp.arange(NORB, dtype=jnp.int32)[None, :] % TILE
    occupied_part = jnp.where(rows == columns, 1.0, 0.0).astype(jnp.float32)
    return (noise + occupied_part[None, :, :]).astype(jnp.bfloat16)


def lax_iota_rows():
    return jnp.arange(NOCC, dtype=jnp.int32)[:, None]


def draw_chol_tiles(key, part):
    key = jax.random.fold_in(key, 13)
    noise_key, diag_key = jax.random.split(key)
    noise = jnp.clip(jax.random.normal(noise_key, (NBLK, MAXT, KB, NOCC, TILE), jnp.float32), -6.0, 6.0)
    noise = noise * (1.0 / (MAXT * TILE) ** 0.5)
    weights = jax.random.uniform(diag_key, (NBLK, MAXT, KB), jnp.float32, 0.05, 0.15)
    rows = jnp.arange(NOCC, dtype=jnp.int32)[:, None]
    columns = jnp.arange(TILE, dtype=jnp.int32)[None, :]
    density = jnp.where(rows == columns, 1.0, 0.0).astype(jnp.float32)
    return (noise + weights[:, :, :, None, None] * density[None, None, None, :, :]).astype(jnp.bfloat16)


def with_ends(values, own_key, smallest, top_value):
    spot = [jax.random.randint(jax.random.fold_in(own_key, axis), (), 0, length) for axis, length in enumerate(values.shape)]
    longest = values.shape.index(max(values.shape))
    beside = spot[:longest] + [(spot[longest] + 1) % values.shape[longest]] + spot[longest + 1:]
    return values.at[tuple(spot)].set(smallest).at[tuple(beside)].set(top_value)


def setup_inputs(seed: int = 0, part: int = 0) -> dict:
    seeds = jax.random.split(jax.random.key(seed), 5)
    part_keys = jax.random.split(jax.random.fold_in(seeds[4], part), 5)
    return {
        "theta": draw_theta(jax.random.fold_in(jax.random.fold_in(seeds[4], part), 71), part),
        "chol_tiles": draw_chol_tiles(jax.random.fold_in(seeds[4], 71), part),
        "screen": with_ends((jax.random.randint(seeds[2], (NBLK, MAXT), 0, 4) < 3).astype(jnp.int32), jax.random.fold_in(seeds[2], 1), 0, 1),
        "tile_list": draw_tile_list(jax.random.fold_in(seeds[4], 71), part),
    }


def group_terms(theta_tiles, chol_group, screen_group, list_row):
    selected = jnp.take(theta_tiles, list_row.astype(jnp.int32), axis=2).astype(jnp.float32)
    masked = chol_group.astype(jnp.float32) * screen_group[:, :, None, None, None].astype(jnp.float32)
    inner_mat = jnp.einsum("bmkaq,ncmq->nbkac", masked, selected, precision=lax.Precision.HIGHEST)
    bias_rows = jnp.trace(inner_mat, axis1=3, axis2=4)
    cross_sum = jnp.sum(inner_mat * jnp.swapaxes(inner_mat, 3, 4), axis=(3, 4))
    part_sums = jnp.sum(bias_rows * bias_rows - cross_sum, axis=(1, 2))
    return bias_rows.reshape(bias_rows.shape[0], -1), part_sums


def reference(theta, chol_tiles, screen, tile_list):
    walkers = theta.shape[0]
    theta_tiles = theta.reshape(walkers, NOCC, NT, TILE)
    chol_groups = chol_tiles.reshape(GROUPS, BLK_DEV, MAXT, KB, NOCC, TILE)
    screen_groups = screen.reshape(GROUPS, BLK_DEV, MAXT)

    def one_group(group_args):
        return group_terms(theta_tiles, group_args[0], group_args[1], group_args[2])

    bias_all, part_all = lax.map(one_group, (chol_groups, screen_groups, tile_list))
    force_bias = jnp.transpose(bias_all, (1, 0, 2)).reshape(walkers, -1)
    energy = jnp.sum(part_all, axis=0) / (2.0 * NOCC * NOCC)
    return force_bias, energy
```

```python
import functools

import jax
import jax.numpy as jnp
from jax import lax
from jax.experimental import pallas as pl
from jax.experimental.pallas import tpu as pltpu
from jax.sharding import PartitionSpec as P

LANES = 128
VMEM_LIMIT = 48 * 1024 * 1024


def pick_kernel(list_ref, theta_ref, out_ref):
    group = pl.program_id(0)
    listed = list_ref.shape[1]
    width = out_ref.shape[2] // listed
    for m in range(listed):
        start = pl.multiple_of(list_ref[group, m] * width, width)
        out_ref[0, :, m * width:(m + 1) * width] = theta_ref[0, :, pl.ds(start, width)]


def pick_tiles(theta, tile_list, width):
    _, occupied, orbitals = theta.shape
    groups, listed = tile_list.shape
    return pl.pallas_call(
        pick_kernel,
        grid=(groups,),
        in_specs=[
            pl.BlockSpec(memory_space=pltpu.SMEM),
            pl.BlockSpec((1, occupied, orbitals), lambda g: (0, 0, 0)),
        ],
        out_specs=pl.BlockSpec((1, occupied, listed * width), lambda g: (g, 0, 0)),
        out_shape=jax.ShapeDtypeStruct((groups, occupied, listed * width), theta.dtype),
        compiler_params=pltpu.CompilerParams(vmem_limit_bytes=VMEM_LIMIT),
        name="pick_tiles",
    )(tile_list, theta)


def terms_kernel(screen_ref, chol_ref, theta_ref, out_ref, *, k_step):
    _, listed, vectors, occupied, width = chol_ref.shape
    walkers = theta_ref.shape[0]
    columns = walkers * occupied
    depth = listed * width
    tiles = columns // LANES
    per_tile = LANES // occupied

    lane = lax.broadcasted_iota(jnp.int32, (1, depth), 1)
    mask = jnp.zeros((1, depth), jnp.float32)
    for m in range(listed):
        keep = screen_ref[0, m].astype(jnp.float32)
        mask = jnp.where((lane >= m * width) & (lane < (m + 1) * width), keep, mask)
    theta = theta_ref[...].reshape(columns, depth) * mask.astype(theta_ref.dtype)

    row = lax.broadcasted_iota(jnp.int32, (occupied, LANES), 0)
    col = lax.broadcasted_iota(jnp.int32, (occupied, LANES), 1)
    on_diag = (col % occupied) == row
    low = col < occupied

    def one_chunk(chunk_index, cross):
        k0 = chunk_index * k_step
        left = jnp.concatenate(
            [chol_ref[0, m, pl.ds(k0, k_step)].reshape(k_step * occupied, width) for m in range(listed)],
            axis=1,
        )
        inner = lax.dot_general(
            left, theta, (((1,), (1,)), ((), ())), preferred_element_type=jnp.float32
        )
        cross = list(cross)
        diag_rows = []
        for pair in range(k_step // 2):
            parts = []
            for t in range(tiles):
                tile = inner[pair * 2 * occupied:(pair + 1) * 2 * occupied, t * LANES:(t + 1) * LANES]
                flipped = tile.T
                top, bottom = tile[:occupied], tile[occupied:]
                f_top, f_bottom = flipped[:occupied], flipped[occupied:]
                swapped = pltpu.roll(jnp.where(low, f_bottom, f_top), occupied, 1)
                g_top = jnp.where(low, f_top, swapped)
                g_bottom = jnp.where(low, swapped, f_bottom)
                product = top * g_top + bottom * g_bottom
                cross[t] = cross[t] + jnp.sum(product.reshape(occupied // 8, 8, LANES), axis=0)
                d_top = jnp.where(on_diag, top, 0.0)
                d_bottom = jnp.where(on_diag, bottom, 0.0)
                parts.append((jnp.sum(d_top, axis=0, keepdims=True), jnp.sum(d_bottom, axis=0, keepdims=True)))
            diag_rows.append(jnp.concatenate([p[0] for p in parts], axis=1))
            diag_rows.append(jnp.concatenate([p[1] for p in parts], axis=1))
        return tuple(cross), jnp.concatenate(diag_rows, axis=0)

    cross = tuple(jnp.zeros((8, LANES), jnp.float32) for _ in range(tiles))
    diags = []
    for chunk in range(vectors // k_step):
        cross, rows = one_chunk(chunk, cross)
        diags.append(rows)
    cross_row = jnp.concatenate([jnp.sum(c, axis=0, keepdims=True) for c in cross], axis=1)
    rows = jnp.concatenate(diags + [jnp.broadcast_to(cross_row, (8, columns))], axis=0)
    seg_row = lax.broadcasted_iota(jnp.int32, (8, columns), 0)
    seg_col = lax.broadcasted_iota(jnp.int32, (8, columns), 1)
    segment = jnp.where(seg_col // occupied == seg_row, 1.0, 0.0).astype(jnp.float32)
    sums = lax.dot_general(
        segment, rows, (((1,), (1,)), ((), ())),
        precision=lax.Precision.HIGHEST, preferred_element_type=jnp.float32,
    )[:walkers]
    bias = sums[:, :vectors]
    energy = jnp.sum(bias * bias, axis=1, keepdims=True) - sums[:, vectors:vectors + 1]
    out_ref[:, 0, :] = jnp.zeros((walkers, out_ref.shape[2]), jnp.float32)
    out_ref[:, 0, :vectors] = bias
    out_ref[:, 0, vectors:vectors + 1] = energy


def block_terms(screen, chol_tiles, selected, out_width):
    walkers, occupied, depth = selected.shape
    per_step = 4
    _, listed, vectors, _, width = chol_tiles.shape
    return pl.pallas_call(
        functools.partial(terms_kernel, k_step=4),
        grid=(walkers // per_step,),
        in_specs=[
            pl.BlockSpec(memory_space=pltpu.SMEM),
            pl.BlockSpec(chol_tiles.shape, lambda i: (0, 0, 0, 0, 0)),
            pl.BlockSpec((per_step, occupied, depth), lambda i: (i, 0, 0)),
        ],
        out_specs=pl.BlockSpec((per_step, 1, out_width), lambda i: (i, 0, 0)),
        out_shape=jax.ShapeDtypeStruct((walkers, 1, out_width), jnp.float32),
        compiler_params=pltpu.CompilerParams(vmem_limit_bytes=VMEM_LIMIT),
        cost_estimate=pl.CostEstimate(
            flops=2 * walkers * vectors * occupied * occupied * depth,
            bytes_accessed=2 * (chol_tiles.size + selected.size),
            transcendentals=0,
        ),
        name="block_terms",
    )(screen, chol_tiles, selected)


def body(theta, chol_tiles, screen, tile_list):
    groups = lax.axis_size("chol")
    _, occupied, _ = theta.shape
    width = chol_tiles.shape[-1]
    vectors = chol_tiles.shape[2]
    out_width = LANES * ((vectors + 1 + LANES - 1) // LANES)
    outgoing = pick_tiles(theta, tile_list, width)
    selected = lax.all_to_all(outgoing, "chol", split_axis=0, concat_axis=0, tiled=True)
    rows = block_terms(screen, chol_tiles, selected, out_width)
    back = lax.all_to_all(rows, "chol", split_axis=0, concat_axis=0, tiled=True)
    force_bias = back[:, 0, :vectors].reshape(1, groups * vectors)
    energy = jnp.sum(back[:, 0, vectors]).reshape(1) / (2.0 * occupied * occupied)
    return (force_bias, energy)


def solution(mesh):
    in_specs = (
        P(("grp", "chol"), None, None),
        P("chol", None, None, None, None),
        P("chol", None),
        P(),
    )
    out_specs = (P(("grp", "chol"), None), P(("grp", "chol")))
    return jax.shard_map(body, mesh=mesh, in_specs=in_specs, out_specs=out_specs, check_vma=False)
```

```python
import functools

import jax
import jax.numpy as jnp
from jax import lax
from jax.experimental import pallas as pl
from jax.experimental.pallas import tpu as pltpu
from jax.sharding import PartitionSpec as P

LANES = 128
VMEM_LIMIT = 48 * 1024 * 1024
BATCH = 4


def split_axis(groups):
    outer = 1
    while outer * outer * 4 <= groups:
        outer *= 2
    return outer, groups // outer


def pick_kernel(list_ref, theta_ref, *out_refs):
    listed, groups = list_ref.shape
    inner = len(out_refs)
    width = out_refs[0].shape[2] // listed
    me = lax.axis_index("chol")
    first = (me // inner) * inner
    for t, out_ref in enumerate(out_refs):
        group = first + lax.rem(me - first + t, inner)
        for m in range(listed):
            start = pl.multiple_of(list_ref[m, group] * width, width)
            out_ref[0, :, m * width:(m + 1) * width] = theta_ref[0, :, pl.ds(start, width)]


def pick_tiles(theta, listing, width, inner):
    _, occupied, _ = theta.shape
    listed = listing.shape[0]
    piece = jax.ShapeDtypeStruct((1, occupied, listed * width), theta.dtype)
    return pl.pallas_call(
        pick_kernel,
        in_specs=[pl.BlockSpec(memory_space=pltpu.SMEM), pl.BlockSpec(memory_space=pltpu.VMEM)],
        out_specs=[pl.BlockSpec(memory_space=pltpu.VMEM)] * inner,
        out_shape=[piece] * inner,
        compiler_params=pltpu.CompilerParams(vmem_limit_bytes=VMEM_LIMIT),
        cost_estimate=pl.CostEstimate(
            flops=0, bytes_accessed=4 * inner * occupied * listed * width, transcendentals=0
        ),
        name="pick_tiles",
    )(listing, theta)


def batch_terms(chol_ref, theta, k_step):
    _, listed, vectors, occupied, width = chol_ref.shape
    columns = theta.shape[0]
    walkers = columns // occupied
    tiles = columns // LANES

    row = lax.broadcasted_iota(jnp.int32, (occupied, LANES), 0)
    col = lax.broadcasted_iota(jnp.int32, (occupied, LANES), 1)
    on_diag = (col % occupied) == row
    low = col < occupied

    cross = [jnp.zeros((8, LANES), jnp.float32) for _ in range(tiles)]
    diag_rows = []
    for k0 in range(0, vectors, k_step):
        left = jnp.concatenate(
            [chol_ref[0, m, k0:k0 + k_step].reshape(k_step * occupied, width) for m in range(listed)],
            axis=1,
        )
        inner_mat = lax.dot_general(
            left, theta, (((1,), (1,)), ((), ())), preferred_element_type=jnp.float32
        )
        for pair in range(k_step // 2):
            tops, bottoms = [], []
            for t in range(tiles):
                tile = inner_mat[pair * 2 * occupied:(pair + 1) * 2 * occupied, t * LANES:(t + 1) * LANES]
                flipped = tile.T
                top, bottom = tile[:occupied], tile[occupied:]
                f_top, f_bottom = flipped[:occupied], flipped[occupied:]
                swapped = pltpu.roll(jnp.where(low, f_bottom, f_top), occupied, 1)
                product = top * jnp.where(low, f_top, swapped) + bottom * jnp.where(low, swapped, f_bottom)
                cross[t] = cross[t] + jnp.sum(product.reshape(occupied // 8, 8, LANES), axis=0)
                tops.append(jnp.sum(jnp.where(on_diag, top, 0.0), axis=0, keepdims=True))
                bottoms.append(jnp.sum(jnp.where(on_diag, bottom, 0.0), axis=0, keepdims=True))
            diag_rows.append(jnp.concatenate(tops, axis=1))
            diag_rows.append(jnp.concatenate(bottoms, axis=1))
    cross_row = jnp.concatenate([jnp.sum(c, axis=0, keepdims=True) for c in cross], axis=1)
    rows = jnp.concatenate(diag_rows + [jnp.broadcast_to(cross_row, (8, columns))], axis=0)
    seg_row = lax.broadcasted_iota(jnp.int32, (8, columns), 0)
    seg_col = lax.broadcasted_iota(jnp.int32, (8, columns), 1)
    segment = jnp.where(seg_col // occupied == seg_row, 1.0, 0.0).astype(jnp.float32)
    sums = lax.dot_general(
        segment, rows, (((1,), (1,)), ((), ())),
        precision=lax.Precision.HIGHEST, preferred_element_type=jnp.float32,
    )[:walkers]
    bias = sums[:, :vectors]
    energy = jnp.sum(bias * bias, axis=1, keepdims=True) - sums[:, vectors:vectors + 1]
    return bias, energy


def terms_kernel(screen_ref, chol_ref, *refs, shift, inner, carried):
    piece_refs, rest = refs[:inner], refs[inner:]
    out_ref = rest[-1]
    _, listed, vectors, occupied, width = chol_ref.shape
    depth = listed * width
    groups = out_ref.shape[0]
    outer = groups // inner
    me = lax.axis_index("chol")
    zone, spot = me // inner, lax.rem(me, inner)
    owner_zone = lax.rem(zone - shift + outer, outer)

    lane = lax.broadcasted_iota(jnp.int32, (1, depth), 1)
    mask = jnp.zeros((1, depth), jnp.float32)
    for m in range(listed):
        keep = screen_ref[0, m].astype(jnp.float32)
        mask = jnp.where((lane >= m * width) & (lane < (m + 1) * width), keep, mask)
    mask = mask.astype(piece_refs[0].dtype)

    if carried:
        out_ref[...] = rest[0][...]
    else:
        out_ref[...] = jnp.zeros(out_ref.shape, out_ref.dtype)
    for first in range(0, inner, BATCH):
        theta = jnp.concatenate([ref[0] for ref in piece_refs[first:first + BATCH]], axis=0) * mask
        bias, energy = batch_terms(chol_ref, theta, 4)
        for offset in range(BATCH):
            owner = owner_zone * inner + lax.rem(spot - (first + offset) + inner, inner)
            out_ref[pl.ds(owner, 1), 0, :vectors] = bias[offset:offset + 1]
            out_ref[pl.ds(owner, 1), 0, vectors:vectors + 1] = energy[offset:offset + 1]


def block_terms(screen, chol_tiles, pieces, carried, shift, groups, out_width):
    inner = len(pieces)
    _, occupied, depth = pieces[0].shape
    vectors = chol_tiles.shape[2]
    operands = [screen, chol_tiles, *pieces] + ([] if carried is None else [carried])
    return pl.pallas_call(
        functools.partial(terms_kernel, shift=shift, inner=inner, carried=carried is not None),
        in_specs=[pl.BlockSpec(memory_space=pltpu.SMEM)]
        + [pl.BlockSpec(memory_space=pltpu.VMEM)] * (len(operands) - 1),
        out_specs=pl.BlockSpec(memory_space=pltpu.VMEM),
        out_shape=jax.ShapeDtypeStruct((groups, 1, out_width), jnp.float32),
        compiler_params=pltpu.CompilerParams(vmem_limit_bytes=VMEM_LIMIT),
        cost_estimate=pl.CostEstimate(
            flops=2 * inner * vectors * occupied * occupied * depth,
            bytes_accessed=2 * chol_tiles.size,
            transcendentals=0,
        ),
        name="block_terms",
    )(*operands)


def body(theta, chol_tiles, screen, tile_list):
    groups = lax.axis_size("chol")
    outer, inner = split_axis(groups)
    _, occupied, _ = theta.shape
    width = chol_tiles.shape[-1]
    vectors = chol_tiles.shape[2]
    out_width = LANES * ((vectors + 1 + LANES - 1) // LANES)
    listing = tile_list.T

    def moved(zone_step, spot_step):
        return [
            (i, ((i // inner + zone_step) % outer) * inner + (i + spot_step) % inner) for i in range(groups)
        ]

    held = [theta] + [lax.ppermute(theta, "chol", moved(s, 0)) for s in range(1, outer)]
    rows = None
    for s in range(outer):
        picked = pick_tiles(held[s], listing, width, inner)
        pieces = [picked[0]] + [lax.ppermute(picked[t], "chol", moved(0, t)) for t in range(1, inner)]
        rows = block_terms(screen, chol_tiles, pieces, rows, s, groups, out_width)
    back = lax.all_to_all(rows, "chol", split_axis=0, concat_axis=0, tiled=True)
    force_bias = back[:, 0, :vectors].reshape(1, groups * vectors)
    energy = jnp.sum(back[:, 0, vectors]).reshape(1) / (2.0 * occupied * occupied)
    return (force_bias, energy)


def solution(mesh):
    in_specs = (
        P(("grp", "chol"), None, None),
        P("chol", None, None, None, None),
        P("chol", None),
        P(),
    )
    out_specs = (P(("grp", "chol"), None), P(("grp", "chol")))
    return jax.shard_map(body, mesh=mesh, in_specs=in_specs, out_specs=out_specs, check_vma=False)
```

```python
import functools

import jax
import jax.numpy as jnp
from jax import lax
from jax.experimental import pallas as pl
from jax.experimental.pallas import tpu as pltpu
from jax.sharding import PartitionSpec as P

LANES = 128
VMEM_LIMIT = 48 * 1024 * 1024
BATCH = 4
K_STEP = 8
VMEM = pl.BlockSpec(memory_space=pltpu.VMEM)
SMEM = pl.BlockSpec(memory_space=pltpu.SMEM)


def split_axis(groups):
    outer = 1
    while outer * outer * 4 <= groups:
        outer *= 2
    return outer, groups // outer


def pick_kernel(list_ref, *refs, count, inner):
    theta_refs, out_refs = refs[:count], refs[count:]
    listed = list_ref.shape[0]
    width = out_refs[0].shape[2] // listed
    me = lax.axis_index("chol")
    spot = lax.rem(me, inner)
    for t, out_ref in enumerate(out_refs):
        group = me - spot + (spot ^ t)
        for m in range(listed):
            start = pl.multiple_of(list_ref[m, group] * width, width)
            for i, theta_ref in enumerate(theta_refs):
                out_ref[i, :, m * width:(m + 1) * width] = theta_ref[0, :, pl.ds(start, width)]


def pick_tiles(thetas, listing, width, inner):
    count = len(thetas)
    _, occupied, _ = thetas[0].shape
    listed = listing.shape[0]
    piece = jax.ShapeDtypeStruct((count, occupied, listed * width), thetas[0].dtype)
    return pl.pallas_call(
        functools.partial(pick_kernel, count=count, inner=inner),
        in_specs=[SMEM] + [VMEM] * count,
        out_specs=[VMEM] * inner,
        out_shape=[piece] * inner,
        compiler_params=pltpu.CompilerParams(vmem_limit_bytes=VMEM_LIMIT),
        cost_estimate=pl.CostEstimate(
            flops=0, bytes_accessed=4 * count * inner * occupied * listed * width, transcendentals=0
        ),
        name="pick_tiles",
    )(listing, *thetas)


def batch_terms(chol_ref, theta):
    _, listed, vectors, occupied, width = chol_ref.shape
    columns = theta.shape[0]
    walkers = columns // occupied
    tiles = columns // LANES
    contract = (((1,), (1,)), ((), ()))

    lane = lax.broadcasted_iota(jnp.int32, (occupied, LANES), 1)
    low = lane < occupied
    sub8 = lax.broadcasted_iota(jnp.int32, (8, LANES), 0)
    lane8 = lax.broadcasted_iota(jnp.int32, (8, LANES), 1)
    strip = (lane8 % occupied) // 8
    on_diag = lane8 % 8 == sub8

    def diagonal(block):
        merged = block[:8]
        for r in range(1, occupied // 8):
            merged = jnp.where(strip == r, block[8 * r:8 * r + 8], merged)
        return jnp.sum(jnp.where(on_diag, merged, 0.0), axis=0, keepdims=True)

    cross = [jnp.zeros((8, LANES), jnp.float32) for _ in range(tiles)]
    diag_rows = []
    for k0 in range(0, vectors, K_STEP):
        left = jnp.concatenate(
            [chol_ref[0, m, k0:k0 + K_STEP].reshape(K_STEP * occupied, width) for m in range(listed)],
            axis=1,
        )
        inner_mat = lax.dot_general(left, theta, contract, preferred_element_type=jnp.float32)
        flipped = lax.dot_general(theta, left, contract, preferred_element_type=jnp.float32)
        for pair in range(K_STEP // 2):
            tops, bottoms = [], []
            r0 = pair * 2 * occupied
            for t in range(tiles):
                c0 = t * LANES
                top = inner_mat[r0:r0 + occupied, c0:c0 + LANES]
                bottom = inner_mat[r0 + occupied:r0 + 2 * occupied, c0:c0 + LANES]
                f_top = flipped[c0:c0 + occupied, r0:r0 + LANES]
                f_bottom = flipped[c0 + occupied:c0 + 2 * occupied, r0:r0 + LANES]
                swapped = pltpu.roll(jnp.where(low, f_bottom, f_top), occupied, 1)
                product = jnp.where(low, top, bottom) * jnp.where(low, f_top, f_bottom)
                product = product + jnp.where(low, bottom, top) * swapped
                cross[t] = cross[t] + jnp.sum(product.reshape(occupied // 8, 8, LANES), axis=0)
                tops.append(diagonal(top))
                bottoms.append(diagonal(bottom))
            diag_rows.append(jnp.concatenate(tops, axis=1))
            diag_rows.append(jnp.concatenate(bottoms, axis=1))
    cross_row = jnp.concatenate([jnp.sum(c, axis=0, keepdims=True) for c in cross], axis=1)
    rows = jnp.concatenate(diag_rows + [jnp.broadcast_to(cross_row, (8, columns))], axis=0)
    seg_row = lax.broadcasted_iota(jnp.int32, (8, columns), 0)
    seg_col = lax.broadcasted_iota(jnp.int32, (8, columns), 1)
    segment = jnp.where(seg_col // occupied == seg_row, 1.0, 0.0).astype(jnp.float32)
    sums = lax.dot_general(
        segment, rows, contract, precision=lax.Precision.HIGHEST, preferred_element_type=jnp.float32
    )[:walkers]
    bias = sums[:, :vectors]
    energy = jnp.sum(bias * bias, axis=1, keepdims=True) - sums[:, vectors:vectors + 1]
    return bias, energy


def terms_kernel(screen_ref, chol_ref, *refs, shifts, inner, carried):
    piece_refs, rest = refs[:inner], refs[inner:]
    out_ref = rest[-1]
    _, listed, vectors, occupied, width = chol_ref.shape
    depth = listed * width
    me = lax.axis_index("chol")
    spot = lax.rem(me, inner)
    zone = me // inner

    lane = lax.broadcasted_iota(jnp.int32, (1, depth), 1)
    mask = jnp.zeros((1, depth), jnp.float32)
    for m in range(listed):
        keep = screen_ref[0, m].astype(jnp.float32)
        mask = jnp.where((lane >= m * width) & (lane < (m + 1) * width), keep, mask)
    mask = mask.astype(piece_refs[0].dtype)

    if carried:
        out_ref[...] = rest[0][...]
    else:
        out_ref[...] = jnp.zeros(out_ref.shape, out_ref.dtype)
    for i, s in enumerate(shifts):
        for first in range(0, inner, BATCH):
            theta = jnp.concatenate([ref[i] for ref in piece_refs[first:first + BATCH]], axis=0) * mask
            bias, energy = batch_terms(chol_ref, theta)
            for offset in range(BATCH):
                owner = (zone ^ s) * inner + (spot ^ (first + offset))
                out_ref[pl.ds(owner, 1), 0, :vectors] = bias[offset:offset + 1]
                out_ref[pl.ds(owner, 1), 0, vectors:vectors + 1] = energy[offset:offset + 1]


def block_terms(screen, chol_tiles, pieces, carried, shifts, groups, out_width):
    inner = len(pieces)
    count, occupied, depth = pieces[0].shape
    vectors = chol_tiles.shape[2]
    operands = [screen, chol_tiles, *pieces] + ([] if carried is None else [carried])
    return pl.pallas_call(
        functools.partial(terms_kernel, shifts=shifts, inner=inner, carried=carried is not None),
        in_specs=[SMEM] + [VMEM] * (len(operands) - 1),
        out_specs=VMEM,
        out_shape=jax.ShapeDtypeStruct((groups, 1, out_width), jnp.float32),
        compiler_params=pltpu.CompilerParams(vmem_limit_bytes=VMEM_LIMIT),
        cost_estimate=pl.CostEstimate(
            flops=4 * count * inner * vectors * occupied * occupied * depth,
            bytes_accessed=2 * chol_tiles.size,
            transcendentals=0,
        ),
        name="block_terms",
    )(*operands)


def finish_kernel(rows_ref, bias_ref, energy_ref, *, vectors, scale):
    groups = rows_ref.shape[0]
    for d in range(groups):
        bias_ref[:, d * vectors:(d + 1) * vectors] = rows_ref[d, :, :vectors]
    total = jnp.sum(rows_ref[:, 0, :], axis=0, keepdims=True)
    energy_ref[...] = total[:, vectors:vectors + 1] * scale


def finish(rows, vectors, scale):
    groups = rows.shape[0]
    force_bias, energy = pl.pallas_call(
        functools.partial(finish_kernel, vectors=vectors, scale=scale),
        in_specs=[VMEM],
        out_specs=[VMEM, VMEM],
        out_shape=[
            jax.ShapeDtypeStruct((1, groups * vectors), jnp.float32),
            jax.ShapeDtypeStruct((1, 1), jnp.float32),
        ],
        name="finish",
    )(rows)
    return force_bias, energy.reshape(1)


def body(theta, chol_tiles, screen, tile_list):
    groups = lax.axis_size("chol")
    outer, inner = split_axis(groups)
    _, occupied, _ = theta.shape
    width = chol_tiles.shape[-1]
    vectors = chol_tiles.shape[2]
    out_width = LANES * ((vectors + 1 + LANES - 1) // LANES)
    listing = tile_list.T

    def partners(zone_flip, spot_flip):
        return [(i, ((i // inner) ^ zone_flip) * inner + ((i % inner) ^ spot_flip)) for i in range(groups)]

    held = [theta] + [lax.ppermute(theta, "chol", partners(s, 0)) for s in range(1, outer)]
    rows = None
    for first in range(0, outer, outer // 2):
        shifts = list(range(first, first + outer // 2))
        picked = pick_tiles([held[s] for s in shifts], listing, width, inner)
        pieces = [picked[0]] + [lax.ppermute(picked[t], "chol", partners(0, t)) for t in range(1, inner)]
        rows = block_terms(screen, chol_tiles, pieces, rows, shifts, groups, out_width)
    back = lax.all_to_all(rows, "chol", split_axis=0, concat_axis=0, tiled=True)
    return finish(back, vectors, 1.0 / (2.0 * occupied * occupied))


def solution(mesh):
    in_specs = (
        P(("grp", "chol"), None, None),
        P("chol", None, None, None, None),
        P("chol", None),
        P(),
    )
    out_specs = (P(("grp", "chol"), None), P(("grp", "chol")))
    return jax.shard_map(body, mesh=mesh, in_specs=in_specs, out_specs=out_specs, check_vma=False)
```

```python
import functools

import jax
import jax.numpy as jnp
from jax import lax
from jax.experimental import pallas as pl
from jax.experimental.pallas import tpu as pltpu
from jax.sharding import PartitionSpec as P

LANES = 128
CORES = 2
VMEM_LIMIT = 32 * 1024 * 1024
K_STEP = 8
VMEM = pl.BlockSpec(memory_space=pltpu.VMEM)
SMEM = pl.BlockSpec(memory_space=pltpu.SMEM)
PARAMS = pltpu.CompilerParams(vmem_limit_bytes=VMEM_LIMIT)
CONTRACT = (((1,), (1,)), ((), ()))


def screen_kernel(screen_ref, chol_ref, out_ref):
    _, listed, vectors, occupied, width = chol_ref.shape
    for m in range(listed):
        keep = jnp.full((1, width), screen_ref[0, m].astype(jnp.float32)).astype(chol_ref.dtype)
        out_ref[:, m * width:(m + 1) * width] = chol_ref[0, m].reshape(vectors * occupied, width) * keep


def screened_block(screen, chol_tiles):
    _, listed, vectors, occupied, width = chol_tiles.shape
    return pl.pallas_call(
        screen_kernel,
        in_specs=[SMEM, VMEM],
        out_specs=VMEM,
        out_shape=jax.ShapeDtypeStruct((vectors * occupied, listed * width), chol_tiles.dtype),
        compiler_params=PARAMS,
        cost_estimate=pl.CostEstimate(flops=0, bytes_accessed=4 * chol_tiles.size, transcendentals=0),
        name="screen_block",
    )(screen, chol_tiles)


def batch_terms(block_ref, theta, vectors, occupied):
    columns = theta.shape[0]
    walkers = columns // occupied
    tiles = columns // LANES

    lane = lax.broadcasted_iota(jnp.int32, (occupied, LANES), 1)
    low = lane < occupied
    sub8 = lax.broadcasted_iota(jnp.int32, (8, LANES), 0)
    lane8 = lax.broadcasted_iota(jnp.int32, (8, LANES), 1)
    strip = (lane8 % occupied) // 8
    on_diag = lane8 % 8 == sub8

    def diagonal(block):
        merged = block[:8]
        for r in range(1, occupied // 8):
            merged = jnp.where(strip == r, block[8 * r:8 * r + 8], merged)
        return jnp.where(on_diag, merged, 0.0)

    cross = [jnp.zeros((8, LANES), jnp.float32) for _ in range(tiles)]
    diagonals = []
    for k0 in range(0, vectors, K_STEP):
        left = block_ref[k0 * occupied:(k0 + K_STEP) * occupied, :]
        inner_mat = lax.dot_general(left, theta, CONTRACT, preferred_element_type=jnp.float32)
        flipped = lax.dot_general(theta, left, CONTRACT, preferred_element_type=jnp.float32)
        for pair in range(K_STEP // 2):
            tops, bottoms = [], []
            r0 = pair * 2 * occupied
            for t in range(tiles):
                c0 = t * LANES
                top = inner_mat[r0:r0 + occupied, c0:c0 + LANES]
                bottom = inner_mat[r0 + occupied:r0 + 2 * occupied, c0:c0 + LANES]
                f_top = flipped[c0:c0 + occupied, r0:r0 + LANES]
                f_bottom = flipped[c0 + occupied:c0 + 2 * occupied, r0:r0 + LANES]
                swapped = pltpu.roll(jnp.where(low, f_bottom, f_top), occupied, 1)
                product = jnp.where(low, top, bottom) * jnp.where(low, f_top, f_bottom)
                product = product + jnp.where(low, bottom, top) * swapped
                cross[t] = cross[t] + jnp.sum(product.reshape(occupied // 8, 8, LANES), axis=0)
                tops.append(diagonal(top))
                bottoms.append(diagonal(bottom))
            diagonals.append(jnp.concatenate(tops, axis=1))
            diagonals.append(jnp.concatenate(bottoms, axis=1))
    diagonals.append(jnp.concatenate(cross, axis=1))
    stacked = jnp.concatenate(diagonals, axis=0).reshape(vectors + 1, 8, columns)
    rows = jnp.sum(stacked, axis=1)
    seg_row = lax.broadcasted_iota(jnp.int32, (8, columns), 0)
    seg_col = lax.broadcasted_iota(jnp.int32, (8, columns), 1)
    segment = jnp.where(seg_col // occupied == seg_row, 1.0, 0.0).astype(jnp.float32)
    sums = lax.dot_general(
        segment, rows, CONTRACT, precision=lax.Precision.HIGHEST, preferred_element_type=jnp.float32
    )[:walkers]
    return sums[:, :vectors], sums[:, vectors:vectors + 1]


def terms_kernel(list_ref, own_ref, other_ref, *refs, first, pairs, vectors, carried):
    theta_refs, rest = refs[:2 * pairs], refs[2 * pairs:]
    out_ref, picked_ref = rest[-2], rest[-1]
    listed = list_ref.shape[0]
    _, occupied, _ = theta_refs[0].shape
    width = own_ref.shape[1] // listed
    me = lax.axis_index("chol")
    core = lax.rem(me, CORES)
    chip = me // CORES
    spot = lax.rem(chip, 2)
    zone = chip // 2

    for b, group in enumerate((me, me ^ 1)):
        for m in range(listed):
            start = pl.multiple_of(list_ref[m, group] * width, width)
            for i, ref in enumerate(theta_refs):
                picked_ref[b, i * occupied:(i + 1) * occupied, m * width:(m + 1) * width] = ref[0, :, pl.ds(start, width)]

    if carried:
        out_ref[...] = rest[0][...]
    else:
        out_ref[...] = jnp.zeros(out_ref.shape, out_ref.dtype)

    def one_batch(pair, count):
        start = pair * 2 * occupied
        rows = pl.ds(start if isinstance(pair, int) else pl.multiple_of(start, 2 * occupied), count * 2 * occupied)
        own_bias, own_cross = batch_terms(own_ref, picked_ref[0, rows, :], vectors, occupied)
        other_bias, other_cross = batch_terms(other_ref, picked_ref[1, rows, :], vectors, occupied)
        both = jnp.where(
            core == 0,
            jnp.concatenate([own_bias, other_bias], axis=1),
            jnp.concatenate([other_bias, own_bias], axis=1),
        )
        energy = jnp.sum(both * both, axis=1, keepdims=True) - (own_cross + other_cross)
        for i in range(2 * count):
            owner = (zone ^ (first + pair + i // 2)) * 2 + (spot ^ (i % 2))
            out_ref[pl.ds(owner, 1), 0, :CORES * vectors] = both[i:i + 1]
            out_ref[pl.ds(owner, 1), 0, CORES * vectors:CORES * vectors + 1] = energy[i:i + 1]

    if pairs <= 2:
        one_batch(0, pairs)
    else:
        @pl.loop(0, pairs // 2)
        def _(step):
            one_batch(step * 2, 2)


def pair_terms(listing, own, other, thetas, carried, first, vectors, out_width):
    pairs = len(thetas) // 2
    _, occupied, _ = thetas[0].shape
    chips = listing.shape[1] // CORES
    depth = own.shape[1]
    operands = [listing, own, other, *thetas] + ([] if carried is None else [carried])
    return pl.pallas_call(
        functools.partial(terms_kernel, first=first, pairs=pairs, vectors=vectors, carried=carried is not None),
        in_specs=[SMEM] + [VMEM] * (len(operands) - 1),
        out_specs=VMEM,
        out_shape=jax.ShapeDtypeStruct((chips, 1, out_width), jnp.float32),
        scratch_shapes=[pltpu.VMEM((CORES, 2 * pairs * occupied, depth), own.dtype)],
        compiler_params=PARAMS,
        cost_estimate=pl.CostEstimate(
            flops=16 * pairs * vectors * occupied * occupied * depth,
            bytes_accessed=4 * own.size,
            transcendentals=0,
        ),
        name="pair_terms",
    )(*operands)


def finish_kernel(rows_ref, bias_ref, energy_ref, *, used, scale):
    chips = rows_ref.shape[0]
    for d in range(chips):
        bias_ref[:, d * used:(d + 1) * used] = rows_ref[d, :, :used]
    total = jnp.sum(rows_ref[:, 0, :], axis=0, keepdims=True)
    energy_ref[...] = total[:, used:used + 1] * scale


def finish(rows, used, scale):
    chips = rows.shape[0]
    force_bias, energy = pl.pallas_call(
        functools.partial(finish_kernel, used=used, scale=scale),
        in_specs=[VMEM],
        out_specs=[VMEM, VMEM],
        out_shape=[
            jax.ShapeDtypeStruct((1, chips * used), jnp.float32),
            jax.ShapeDtypeStruct((1, 1), jnp.float32),
        ],
        name="finish",
    )(rows)
    return force_bias, energy.reshape(1)


def body(theta, chol_tiles, screen, tile_list):
    groups = lax.axis_size("chol")
    chips = groups // CORES
    zones = chips // 2
    _, occupied, _ = theta.shape
    vectors = chol_tiles.shape[2]
    used = CORES * vectors
    out_width = LANES * ((used + 1 + LANES - 1) // LANES)
    listing = tile_list.T

    def flipped(x, flip):
        return lax.ppermute(x, "chol", [(i, i ^ flip) for i in range(groups)])

    held = {0: theta}
    bit = zones // 2
    while bit:
        for s in sorted(held):
            held[s ^ bit] = flipped(held[s], bit * 2 * CORES)
        bit //= 2
    own = screened_block(screen, chol_tiles)
    other = flipped(own, 1)
    beside = {s: flipped(held[s], CORES) for s in range(zones)}

    rows = None
    for first, last in ((0, 1), (1, zones - 1), (zones - 1, zones)):
        thetas = [x for s in range(first, last) for x in (held[s], beside[s])]
        rows = pair_terms(listing, own, other, thetas, rows, first, vectors, out_width)
    same_core = [list(range(core, groups, CORES)) for core in range(CORES)]
    back = lax.all_to_all(rows, "chol", split_axis=0, concat_axis=0, tiled=True, axis_index_groups=same_core)
    return finish(back, used, 1.0 / (2.0 * occupied * occupied))


def solution(mesh):
    in_specs = (
        P(("grp", "chol"), None, None),
        P("chol", None, None, None, None),
        P("chol", None),
        P(),
    )
    out_specs = (P(("grp", "chol"), None), P(("grp", "chol")))
    return jax.shard_map(body, mesh=mesh, in_specs=in_specs, out_specs=out_specs, check_vma=False)
```

```python
import functools

import jax
import jax.numpy as jnp
from jax import lax
from jax.experimental import pallas as pl
from jax.experimental.pallas import tpu as pltpu
from jax.sharding import PartitionSpec as P

LANES = 128
VMEM_LIMIT = 32 * 1024 * 1024
K_STEP = 8
BATCH = 8
VMEM = pl.BlockSpec(memory_space=pltpu.VMEM)
SMEM = pl.BlockSpec(memory_space=pltpu.SMEM)
ANY = pl.BlockSpec(memory_space=pl.ANY)
PARAMS = pltpu.CompilerParams(vmem_limit_bytes=VMEM_LIMIT)
NT = (((1,), (1,)), ((), ()))
NN = (((1,), (0,)), ((), ()))


def split_axis(groups):
    outer = 1
    while outer * outer * 4 <= groups:
        outer *= 2
    return outer, groups // outer


def prepare_kernel(screen_ref, chol_ref, block_ref, turned_ref):
    _, listed, vectors, occupied, width = chol_ref.shape
    for m in range(listed):
        keep = jnp.full((1, width), screen_ref[0, m].astype(jnp.float32)).astype(chol_ref.dtype)
        tile = chol_ref[0, m].reshape(vectors * occupied, width) * keep
        block_ref[:, m * width:(m + 1) * width] = tile
        turned_ref[m * width:(m + 1) * width, :] = tile.T


def prepare_block(screen, chol_tiles):
    _, listed, vectors, occupied, width = chol_tiles.shape
    rows, depth = vectors * occupied, listed * width
    return pl.pallas_call(
        prepare_kernel,
        in_specs=[SMEM, VMEM],
        out_specs=[VMEM, VMEM],
        out_shape=[
            jax.ShapeDtypeStruct((rows, depth), chol_tiles.dtype),
            jax.ShapeDtypeStruct((depth, rows), chol_tiles.dtype),
        ],
        compiler_params=PARAMS,
        cost_estimate=pl.CostEstimate(flops=0, bytes_accessed=6 * chol_tiles.size, transcendentals=0),
        name="prepare_block",
    )(screen, chol_tiles)


def pick_kernel(list_ref, *refs, count, inner):
    theta_refs, out_refs = refs[:count], refs[count:]
    listed = list_ref.shape[0]
    width = out_refs[0].shape[2] // listed
    me = lax.axis_index("chol")
    for t, out_ref in enumerate(out_refs):
        group = (me // inner) * inner + (lax.rem(me, inner) ^ t)
        for m in range(listed):
            start = pl.multiple_of(list_ref[m, group] * width, width)
            for i, theta_ref in enumerate(theta_refs):
                out_ref[i, :, m * width:(m + 1) * width] = theta_ref[0, :, pl.ds(start, width)]


def pick_tiles(thetas, listing, width, inner):
    count = len(thetas)
    _, occupied, _ = thetas[0].shape
    listed = listing.shape[0]
    piece = jax.ShapeDtypeStruct((count, occupied, listed * width), thetas[0].dtype)
    return pl.pallas_call(
        functools.partial(pick_kernel, count=count, inner=inner),
        in_specs=[SMEM] + [VMEM] * count,
        out_specs=[VMEM] * inner,
        out_shape=[piece] * inner,
        compiler_params=PARAMS,
        cost_estimate=pl.CostEstimate(
            flops=0, bytes_accessed=4 * count * inner * occupied * listed * width, transcendentals=0
        ),
        name="pick_tiles",
    )(listing, *thetas)


def batch_terms(block_ref, turned_ref, theta, vectors, occupied):
    columns = theta.shape[0]
    walkers = columns // occupied
    tiles = columns // LANES

    lane = lax.broadcasted_iota(jnp.int32, (occupied, LANES), 1)
    low = lane < occupied
    sub8 = lax.broadcasted_iota(jnp.int32, (8, LANES), 0)
    lane8 = lax.broadcasted_iota(jnp.int32, (8, LANES), 1)
    strip = (lane8 % occupied) // 8
    on_diag = lane8 % 8 == sub8

    def diagonal(block):
        merged = block[:8]
        for r in range(1, occupied // 8):
            merged = jnp.where(strip == r, block[8 * r:8 * r + 8], merged)
        return jnp.where(on_diag, merged, 0.0)

    cross = [jnp.zeros((8, LANES), jnp.float32) for _ in range(tiles)]
    diagonals = []
    for k0 in range(0, vectors, K_STEP):
        span = slice(k0 * occupied, (k0 + K_STEP) * occupied)
        inner_mat = lax.dot_general(block_ref[span, :], theta, NT, preferred_element_type=jnp.float32)
        flipped = lax.dot_general(theta, turned_ref[:, span], NN, preferred_element_type=jnp.float32)
        for pair in range(K_STEP // 2):
            tops, bottoms = [], []
            r0 = pair * 2 * occupied
            for t in range(tiles):
                c0 = t * LANES
                top = inner_mat[r0:r0 + occupied, c0:c0 + LANES]
                bottom = inner_mat[r0 + occupied:r0 + 2 * occupied, c0:c0 + LANES]
                f_top = flipped[c0:c0 + occupied, r0:r0 + LANES]
                f_bottom = flipped[c0 + occupied:c0 + 2 * occupied, r0:r0 + LANES]
                swapped = pltpu.roll(jnp.where(low, f_bottom, f_top), occupied, 1)
                product = jnp.where(low, top, bottom) * jnp.where(low, f_top, f_bottom)
                product = product + jnp.where(low, bottom, top) * swapped
                cross[t] = cross[t] + jnp.sum(product.reshape(occupied // 8, 8, LANES), axis=0)
                tops.append(diagonal(top))
                bottoms.append(diagonal(bottom))
            diagonals.append(jnp.concatenate(tops, axis=1))
            diagonals.append(jnp.concatenate(bottoms, axis=1))
    diagonals.append(jnp.concatenate(cross, axis=1))
    stacked = jnp.concatenate(diagonals, axis=0).reshape(vectors + 1, 8, columns)
    rows = jnp.sum(stacked, axis=1)
    seg_row = lax.broadcasted_iota(jnp.int32, (8, columns), 0)
    seg_col = lax.broadcasted_iota(jnp.int32, (8, columns), 1)
    segment = jnp.where(seg_col // occupied == seg_row, 1.0, 0.0).astype(jnp.float32)
    sums = lax.dot_general(
        segment, rows, NT, precision=lax.Precision.HIGHEST, preferred_element_type=jnp.float32
    )[:walkers]
    bias = sums[:, :vectors]
    return bias, jnp.sum(bias * bias, axis=1, keepdims=True) - sums[:, vectors:vectors + 1]


def terms_kernel(block_ref, turned_ref, *refs, parts, inner, vectors, carried):
    piece_refs, rest = refs[:inner * len(parts)], refs[inner * len(parts):]
    out_ref, theta_ref = rest[-2], rest[-1]
    _, occupied, _ = piece_refs[0].shape
    me = lax.axis_index("chol")
    spot = lax.rem(me, inner)
    zone = me // inner
    shifts = [s for part in parts for s in part]
    walkers = len(shifts) * inner

    row = 0
    for p, part in enumerate(parts):
        for i in range(len(part)):
            for ref in piece_refs[p * inner:(p + 1) * inner]:
                theta_ref[row:row + occupied, :] = ref[i]
                row += occupied
    if carried:
        out_ref[...] = rest[0][...]
    else:
        out_ref[...] = jnp.zeros(out_ref.shape, out_ref.dtype)

    def one_batch(first, count):
        start = first * occupied
        rows = pl.ds(start if isinstance(first, int) else pl.multiple_of(start, count * occupied), count * occupied)
        bias, energy = batch_terms(block_ref, turned_ref, theta_ref[rows, :], vectors, occupied)
        for j in range(count):
            index = first + j
            owner = (zone ^ (shifts[0] + index // inner)) * inner + (spot ^ lax.rem(index, inner))
            out_ref[pl.ds(owner, 1), 0, :vectors] = bias[j:j + 1]
            out_ref[pl.ds(owner, 1), 0, vectors:vectors + 1] = energy[j:j + 1]

    if walkers <= BATCH:
        one_batch(0, walkers)
    else:
        @pl.loop(0, walkers // BATCH)
        def _(step):
            one_batch(step * BATCH, BATCH)


def block_terms(block, turned, pieces, carried, parts, vectors, groups, out_width):
    inner = len(pieces[0])
    count = sum(len(part) for part in parts)
    _, occupied, depth = pieces[0][0].shape
    operands = [block, turned] + [p for part in pieces for p in part] + ([] if carried is None else [carried])
    return pl.pallas_call(
        functools.partial(
            terms_kernel, parts=parts, inner=inner, vectors=vectors, carried=carried is not None
        ),
        in_specs=[VMEM] * len(operands),
        out_specs=VMEM,
        out_shape=jax.ShapeDtypeStruct((groups, 1, out_width), jnp.float32),
        scratch_shapes=[pltpu.VMEM((count * inner * occupied, depth), block.dtype)],
        compiler_params=PARAMS,
        cost_estimate=pl.CostEstimate(
            flops=4 * count * inner * vectors * occupied * occupied * depth,
            bytes_accessed=4 * block.size,
            transcendentals=0,
        ),
        name="block_terms",
    )(*operands)


def finish_kernel(rows_ref, bias_ref, energy_ref, bias_buf, energy_buf, sems, *, vectors, scale):
    groups = rows_ref.shape[0]
    total = jnp.sum(rows_ref[:, 0, :], axis=0, keepdims=True)
    energy_buf[...] = total[:, vectors:vectors + 1] * scale
    energy_copy = pltpu.make_async_copy(energy_buf, energy_ref, sems.at[1])
    energy_copy.start()
    for d in range(groups):
        bias_buf[:, d * vectors:(d + 1) * vectors] = rows_ref[d, :, :vectors]
    bias_copy = pltpu.make_async_copy(bias_buf, bias_ref, sems.at[0])
    bias_copy.start()
    energy_copy.wait()
    bias_copy.wait()


def finish(rows, vectors, scale):
    groups = rows.shape[0]
    shapes = [(1, groups * vectors), (1, 1)]
    force_bias, energy = pl.pallas_call(
        functools.partial(finish_kernel, vectors=vectors, scale=scale),
        in_specs=[VMEM],
        out_specs=[ANY, ANY],
        out_shape=[jax.ShapeDtypeStruct(s, jnp.float32) for s in shapes],
        scratch_shapes=[pltpu.VMEM(s, jnp.float32) for s in shapes] + [pltpu.SemaphoreType.DMA((2,))],
        name="finish",
    )(rows)
    return force_bias, energy.reshape(1)


def body(theta, chol_tiles, screen, tile_list):
    groups = lax.axis_size("chol")
    outer, inner = split_axis(groups)
    _, occupied, _ = theta.shape
    width = chol_tiles.shape[-1]
    vectors = chol_tiles.shape[2]
    out_width = LANES * ((vectors + 1 + LANES - 1) // LANES)
    listing = tile_list.T

    def partners(zone_flip, spot_flip):
        return [(i, ((i // inner) ^ zone_flip) * inner + ((i % inner) ^ spot_flip)) for i in range(groups)]

    def flipped(x, zone_flip, spot_flip=0):
        return lax.ppermute(x, "chol", partners(zone_flip, spot_flip))

    held = [theta] + [None] * (outer - 1)
    bit = outer // 2
    while bit:
        for s in range(0, outer, 2 * bit):
            held[s + bit] = flipped(held[s], bit)
        bit //= 2
    block, turned = prepare_block(screen, chol_tiles)

    def neighbourhood(shifts):
        picked = pick_tiles([held[s] for s in shifts], listing, width, inner)
        return [picked[0]] + [flipped(picked[t], 0, t) for t in range(1, inner)]

    rows = None
    for parts in ([[0, 1]], [list(range(2, outer - 1)), [outer - 1]]):
        pieces = [neighbourhood(shifts) for shifts in parts]
        rows = block_terms(block, turned, pieces, rows, parts, vectors, groups, out_width)
    back = lax.all_to_all(rows, "chol", split_axis=0, concat_axis=0, tiled=True)
    return finish(back, vectors, 1.0 / (2.0 * occupied * occupied))


def solution(mesh):
    in_specs = (
        P(("grp", "chol"), None, None),
        P("chol", None, None, None, None),
        P("chol", None),
        P(),
    )
    out_specs = (P(("grp", "chol"), None), P(("grp", "chol")))
    return jax.shard_map(body, mesh=mesh, in_specs=in_specs, out_specs=out_specs, check_vma=False)
```

```python
import functools

import jax
import jax.numpy as jnp
from jax import lax
from jax.experimental import pallas as pl
from jax.experimental.pallas import tpu as pltpu
from jax.sharding import PartitionSpec as P

LANES = 128
CORES = 2
VMEM_LIMIT = 32 * 1024 * 1024
K_STEP = 8
BATCH = 4
VMEM = pl.BlockSpec(memory_space=pltpu.VMEM)
SMEM = pl.BlockSpec(memory_space=pltpu.SMEM)
PARAMS = pltpu.CompilerParams(vmem_limit_bytes=VMEM_LIMIT)
NT = (((1,), (1,)), ((), ()))
NN = (((1,), (0,)), ((), ()))


def prepare_kernel(screen_ref, chol_ref, block_ref, turned_ref):
    _, listed, vectors, occupied, width = chol_ref.shape
    for m in range(listed):
        keep = jnp.full((1, width), screen_ref[0, m].astype(jnp.float32)).astype(chol_ref.dtype)
        tile = chol_ref[0, m].reshape(vectors * occupied, width) * keep
        block_ref[:, m * width:(m + 1) * width] = tile
        turned_ref[m * width:(m + 1) * width, :] = tile.T


def prepare_block(screen, chol_tiles):
    _, listed, vectors, occupied, width = chol_tiles.shape
    rows, depth = vectors * occupied, listed * width
    return pl.pallas_call(
        prepare_kernel,
        in_specs=[SMEM, VMEM],
        out_specs=[VMEM, VMEM],
        out_shape=[
            jax.ShapeDtypeStruct((rows, depth), chol_tiles.dtype),
            jax.ShapeDtypeStruct((depth, rows), chol_tiles.dtype),
        ],
        compiler_params=PARAMS,
        cost_estimate=pl.CostEstimate(flops=0, bytes_accessed=6 * chol_tiles.size, transcendentals=0),
        name="prepare_block",
    )(screen, chol_tiles)


def batch_terms(block_ref, turned_ref, theta, vectors, occupied):
    columns = theta.shape[0]
    walkers = columns // occupied
    tiles = columns // LANES

    lane = lax.broadcasted_iota(jnp.int32, (occupied, LANES), 1)
    low = lane < occupied
    sub8 = lax.broadcasted_iota(jnp.int32, (8, LANES), 0)
    lane8 = lax.broadcasted_iota(jnp.int32, (8, LANES), 1)
    strip = (lane8 % occupied) // 8
    on_diag = lane8 % 8 == sub8

    def diagonal(block):
        merged = block[:8]
        for r in range(1, occupied // 8):
            merged = jnp.where(strip == r, block[8 * r:8 * r + 8], merged)
        return jnp.where(on_diag, merged, 0.0)

    cross = [jnp.zeros((8, LANES), jnp.float32) for _ in range(tiles)]
    diagonals = []
    for k0 in range(0, vectors, K_STEP):
        span = slice(k0 * occupied, (k0 + K_STEP) * occupied)
        inner_mat = lax.dot_general(block_ref[span, :], theta, NT, preferred_element_type=jnp.float32)
        flipped = lax.dot_general(theta, turned_ref[:, span], NN, preferred_element_type=jnp.float32)
        for pair in range(K_STEP // 2):
            tops, bottoms = [], []
            r0 = pair * 2 * occupied
            for t in range(tiles):
                c0 = t * LANES
                top = inner_mat[r0:r0 + occupied, c0:c0 + LANES]
                bottom = inner_mat[r0 + occupied:r0 + 2 * occupied, c0:c0 + LANES]
                f_top = flipped[c0:c0 + occupied, r0:r0 + LANES]
                f_bottom = flipped[c0 + occupied:c0 + 2 * occupied, r0:r0 + LANES]
                swapped = pltpu.roll(jnp.where(low, f_bottom, f_top), occupied, 1)
                product = jnp.where(low, top, bottom) * jnp.where(low, f_top, f_bottom)
                product = product + jnp.where(low, bottom, top) * swapped
                cross[t] = cross[t] + jnp.sum(product.reshape(occupied // 8, 8, LANES), axis=0)
                tops.append(diagonal(top))
                bottoms.append(diagonal(bottom))
            diagonals.append(jnp.concatenate(tops, axis=1))
            diagonals.append(jnp.concatenate(bottoms, axis=1))
    diagonals.append(jnp.concatenate(cross, axis=1))
    stacked = jnp.concatenate(diagonals, axis=0).reshape(vectors + 1, 8, columns)
    rows = jnp.sum(stacked, axis=1)
    seg_row = lax.broadcasted_iota(jnp.int32, (8, columns), 0)
    seg_col = lax.broadcasted_iota(jnp.int32, (8, columns), 1)
    segment = jnp.where(seg_col // occupied == seg_row, 1.0, 0.0).astype(jnp.float32)
    sums = lax.dot_general(
        segment, rows, NT, precision=lax.Precision.HIGHEST, preferred_element_type=jnp.float32
    )[:walkers]
    return sums[:, :vectors], sums[:, vectors:vectors + 1]


def terms_kernel(list_ref, own_ref, own_turned_ref, other_ref, other_turned_ref, *refs, first, count, vectors, carried):
    theta_refs, rest = refs[:count], refs[count:]
    out_ref, picked_ref = rest[-2], rest[-1]
    listed = list_ref.shape[0]
    _, occupied, _ = theta_refs[0].shape
    width = own_ref.shape[1] // listed
    me = lax.axis_index("chol")
    core = lax.rem(me, CORES)
    chip = me // CORES

    for b, group in enumerate((me, me ^ 1)):
        for m in range(listed):
            start = pl.multiple_of(list_ref[m, group] * width, width)
            for i, ref in enumerate(theta_refs):
                picked_ref[b, i * occupied:(i + 1) * occupied, m * width:(m + 1) * width] = ref[0, :, pl.ds(start, width)]

    if carried:
        out_ref[...] = rest[0][...]
    else:
        out_ref[...] = jnp.zeros(out_ref.shape, out_ref.dtype)

    def one_batch(index, walkers):
        start = index * occupied
        rows = pl.ds(start if isinstance(index, int) else pl.multiple_of(start, walkers * occupied), walkers * occupied)
        own_bias, own_cross = batch_terms(own_ref, own_turned_ref, picked_ref[0, rows, :], vectors, occupied)
        other_bias, other_cross = batch_terms(other_ref, other_turned_ref, picked_ref[1, rows, :], vectors, occupied)
        both = jnp.where(
            core == 0,
            jnp.concatenate([own_bias, other_bias], axis=1),
            jnp.concatenate([other_bias, own_bias], axis=1),
        )
        energy = jnp.sum(both * both, axis=1, keepdims=True) - (own_cross + other_cross)
        for i in range(walkers):
            owner = chip ^ (first + index + i)
            out_ref[pl.ds(owner, 1), 0, :CORES * vectors] = both[i:i + 1]
            out_ref[pl.ds(owner, 1), 0, CORES * vectors:CORES * vectors + 1] = energy[i:i + 1]

    if count <= BATCH:
        one_batch(0, count)
    else:
        @pl.loop(0, count // BATCH)
        def _(step):
            one_batch(step * BATCH, BATCH)


def chip_terms(listing, blocks, thetas, carried, first, vectors, out_width):
    count = len(thetas)
    _, occupied, _ = thetas[0].shape
    chips = listing.shape[1] // CORES
    depth = blocks[0].shape[1]
    operands = [listing, *blocks, *thetas] + ([] if carried is None else [carried])
    return pl.pallas_call(
        functools.partial(terms_kernel, first=first, count=count, vectors=vectors, carried=carried is not None),
        in_specs=[SMEM] + [VMEM] * (len(operands) - 1),
        out_specs=VMEM,
        out_shape=jax.ShapeDtypeStruct((chips, 1, out_width), jnp.float32),
        scratch_shapes=[pltpu.VMEM((CORES, count * occupied, depth), thetas[0].dtype)],
        compiler_params=PARAMS,
        cost_estimate=pl.CostEstimate(
            flops=8 * count * vectors * occupied * occupied * depth,
            bytes_accessed=8 * blocks[0].size,
            transcendentals=0,
        ),
        name="chip_terms",
    )(*operands)


def finish_kernel(rows_ref, bias_ref, energy_ref, *, used, scale):
    chips, _, width = rows_ref.shape
    total = rows_ref[0]
    for d in range(1, chips):
        total = total + rows_ref[d]
    energy_ref[...] = total[:, used:used + 1] * scale
    lane = lax.broadcasted_iota(jnp.int32, (1, width), 1)
    fit = LANES // used if width == LANES else 0
    if fit and chips % fit == 0:
        for d in range(0, chips, fit):
            packed = rows_ref[d]
            for i in range(1, fit):
                packed = jnp.where(lane < i * used, packed, pltpu.roll(rows_ref[d + i], i * used, 1))
            bias_ref[:, d * used:(d + fit) * used] = packed
    else:
        for d in range(chips):
            bias_ref[:, d * used:(d + 1) * used] = rows_ref[d, :, :used]


def finish(rows, used, scale):
    chips = rows.shape[0]
    force_bias, energy = pl.pallas_call(
        functools.partial(finish_kernel, used=used, scale=scale),
        in_specs=[VMEM],
        out_specs=[VMEM, VMEM],
        out_shape=[
            jax.ShapeDtypeStruct((1, chips * used), jnp.float32),
            jax.ShapeDtypeStruct((1, 1), jnp.float32),
        ],
        name="finish",
    )(rows)
    return force_bias, energy.reshape(1)


def body(theta, chol_tiles, screen, tile_list):
    groups = lax.axis_size("chol")
    chips = groups // CORES
    half = chips // 2
    _, occupied, _ = theta.shape
    vectors = chol_tiles.shape[2]
    used = CORES * vectors
    out_width = LANES * ((used + 1 + LANES - 1) // LANES)
    listing = tile_list.T

    def to_chip(x, offset):
        return lax.ppermute(x, "chol", [(i, i ^ (offset * CORES)) for i in range(groups)])

    def to_core(x):
        return lax.ppermute(x, "chol", [(i, i ^ 1) for i in range(groups)])

    far = to_chip(theta, half)
    near = [theta] + [to_chip(theta, offset) for offset in range(1, half)]
    beyond = [far] + [to_chip(far, offset) for offset in range(1, half)]
    blocks = [*prepare_block(screen, chol_tiles), *prepare_block(to_core(screen), to_core(chol_tiles))]

    rows = chip_terms(listing, blocks, near, None, 0, vectors, out_width)
    rows = chip_terms(listing, blocks, beyond, rows, half, vectors, out_width)
    same_core = [list(range(core, groups, CORES)) for core in range(CORES)]
    back = lax.all_to_all(rows, "chol", split_axis=0, concat_axis=0, tiled=True, axis_index_groups=same_core)
    return finish(back, used, 1.0 / (2.0 * occupied * occupied))


def solution(mesh):
    in_specs = (
        P(("grp", "chol"), None, None),
        P("chol", None, None, None, None),
        P("chol", None),
        P(),
    )
    out_specs = (P(("grp", "chol"), None), P(("grp", "chol")))
    return jax.shard_map(body, mesh=mesh, in_specs=in_specs, out_specs=out_specs, check_vma=False)
```

```python
import functools

import jax
import jax.numpy as jnp
from jax import lax
from jax.experimental import pallas as pl
from jax.experimental.pallas import tpu as pltpu
from jax.sharding import PartitionSpec as P

LANES = 128
CORES = 2
VMEM_LIMIT = 32 * 1024 * 1024
K_STEP = 16
BATCH = 4
VMEM = pl.BlockSpec(memory_space=pltpu.VMEM)
SMEM = pl.BlockSpec(memory_space=pltpu.SMEM)
PARAMS = pltpu.CompilerParams(vmem_limit_bytes=VMEM_LIMIT)
SMALL = pl.CostEstimate(flops=0, bytes_accessed=0, transcendentals=0)
NT = (((1,), (1,)), ((), ()))
NN = (((1,), (0,)), ((), ()))


def prepare_kernel(chol_ref, block_ref, turned_ref):
    _, listed, vectors, occupied, width = chol_ref.shape
    for m in range(listed):
        tile = chol_ref[0, m].reshape(vectors * occupied, width)
        block_ref[:, m * width:(m + 1) * width] = tile
        turned_ref[m * width:(m + 1) * width, :] = tile.T


def prepare_block(chol_tiles):
    _, listed, vectors, occupied, width = chol_tiles.shape
    rows, depth = vectors * occupied, listed * width
    return pl.pallas_call(
        prepare_kernel,
        in_specs=[VMEM],
        out_specs=[VMEM, VMEM],
        out_shape=[
            jax.ShapeDtypeStruct((rows, depth), chol_tiles.dtype),
            jax.ShapeDtypeStruct((depth, rows), chol_tiles.dtype),
        ],
        compiler_params=PARAMS,
        cost_estimate=SMALL,
        name="prepare_block",
    )(chol_tiles)


def fold_rows(blocks, sub):
    high = sub < 4
    pairs = []
    for i in range(4):
        a, b = blocks[i], blocks[i + 4]
        pairs.append(jnp.where(high, a, b) + pltpu.roll(jnp.where(high, b, a), 4, 0))
    for shift in (2, 1):
        first = sub % (2 * shift) < shift
        half = len(pairs) // 2
        pairs = [
            jnp.where(
                first,
                pairs[i] + pltpu.roll(pairs[i], 8 - shift, 0),
                pairs[i + half] + pltpu.roll(pairs[i + half], shift, 0),
            )
            for i in range(half)
        ]
    return pairs[0]


def batch_terms(block_ref, turned_ref, theta, cross, store_rows, vectors, occupied):
    columns = theta.shape[0]
    tiles = columns // LANES

    low = lax.broadcasted_iota(jnp.int32, (occupied, LANES), 1) < occupied
    sub8 = lax.broadcasted_iota(jnp.int32, (8, LANES), 0)
    lane8 = lax.broadcasted_iota(jnp.int32, (8, LANES), 1)
    strip = (lane8 % occupied) // 8
    on_diag = lane8 % 8 == sub8

    def diagonal(block):
        merged = block[:8]
        for r in range(1, occupied // 8):
            merged = jnp.where(strip == r, block[8 * r:8 * r + 8], merged)
        return jnp.where(on_diag, merged, 0.0)

    for k0 in range(0, vectors, K_STEP):
        span = slice(k0 * occupied, (k0 + K_STEP) * occupied)
        inner_mat = lax.dot_general(block_ref[span, :], theta, NT, preferred_element_type=jnp.float32)
        flipped = lax.dot_general(theta, turned_ref[:, span], NN, preferred_element_type=jnp.float32)
        for k8 in range(0, K_STEP, 8):
            for t in range(tiles):
                c0 = t * LANES
                diagonals = []
                for k in range(k8, k8 + 8, 2):
                    r0 = k * occupied
                    top = inner_mat[r0:r0 + occupied, c0:c0 + LANES]
                    bottom = inner_mat[r0 + occupied:r0 + 2 * occupied, c0:c0 + LANES]
                    f_top = flipped[c0:c0 + occupied, r0:r0 + LANES]
                    f_bottom = flipped[c0 + occupied:c0 + 2 * occupied, r0:r0 + LANES]
                    swapped = pltpu.roll(jnp.where(low, f_bottom, f_top), occupied, 1)
                    product = jnp.where(low, top, bottom) * jnp.where(low, f_top, f_bottom)
                    product = product + jnp.where(low, bottom, top) * swapped
                    cross[t] = cross[t] + jnp.sum(product.reshape(occupied // 8, 8, LANES), axis=0)
                    diagonals.append(diagonal(top))
                    diagonals.append(diagonal(bottom))
                store_rows(k0 + k8, t, fold_rows(diagonals, sub8))


def terms_kernel(list_ref, *refs, first, count, vectors, batch, carried):
    screen_refs, block_refs, theta_refs, rest = refs[:2], refs[2:6], refs[6:6 + count], refs[6 + count:]
    out_ref, picked_ref, rows_ref = rest[-3:]
    listed = list_ref.shape[0]
    _, occupied, _ = theta_refs[0].shape
    width = block_refs[0].shape[1] // listed
    used = CORES * vectors
    columns = batch * occupied
    tiles = columns // LANES
    out_width = out_ref.shape[2]
    me = lax.axis_index("chol")
    core = lax.rem(me, CORES)
    chip = me // CORES

    for b, group in enumerate((me, me ^ 1)):
        for m in range(listed):
            start = pl.multiple_of(list_ref[m, group] * width, width)
            keep = jnp.full((1, width), screen_refs[b][0, m].astype(jnp.float32)).astype(picked_ref.dtype)
            for i, ref in enumerate(theta_refs):
                picked_ref[b, i * occupied:(i + 1) * occupied, m * width:(m + 1) * width] = (
                    ref[0, :, pl.ds(start, width)] * keep
                )

    if carried:
        out_ref[...] = rest[0][...]
    else:
        out_ref[...] = jnp.zeros(out_ref.shape, out_ref.dtype)

    def one_batch(index):
        start = index * occupied
        rows = pl.ds(start if isinstance(index, int) else pl.multiple_of(start, columns), columns)
        cross = [jnp.zeros((8, LANES), jnp.float32) for _ in range(tiles)]
        for b in range(CORES):
            place = (core ^ b) * vectors

            def store_rows(k, t, value, place=place):
                rows_ref[pl.ds(pl.multiple_of(place + k, 8), 8), t * LANES:(t + 1) * LANES] = value

            batch_terms(
                block_refs[2 * b], block_refs[2 * b + 1], picked_ref[b, rows, :], cross, store_rows, vectors, occupied
            )
        for t in range(tiles):
            rows_ref[used:used + 8, t * LANES:(t + 1) * LANES] = cross[t]
        values = rows_ref[...]
        parts = []
        for _ in range(3):
            part = values.astype(jnp.bfloat16)
            parts.append(part)
            values = values - part.astype(jnp.float32)
        seg_row = lax.broadcasted_iota(jnp.int32, (8, columns), 0)
        seg_col = lax.broadcasted_iota(jnp.int32, (8, columns), 1)
        segment = jnp.where(seg_col // occupied == seg_row, 1.0, 0.0).astype(jnp.bfloat16)
        sums = sum(
            lax.dot_general(segment, part, NT, preferred_element_type=jnp.float32) for part in parts
        )
        bias = sums[:, :used]
        energy = jnp.sum(bias * bias, axis=1, keepdims=True) - jnp.sum(
            sums[:, used:used + 8], axis=1, keepdims=True
        )
        for i in range(batch):
            owner = chip ^ (first + index + i)
            out_ref[pl.ds(owner, 1), 0, :used] = bias[i:i + 1]
            out_ref[pl.ds(owner, 1), 0, used:used + 1] = energy[i:i + 1]

    if count == batch:
        one_batch(0)
    else:
        @pl.loop(0, count // batch)
        def _(step):
            one_batch(step * batch)


def chip_terms(listing, screens, blocks, thetas, carried, first, vectors, out_width):
    count = len(thetas)
    batch = min(count, BATCH)
    _, occupied, _ = thetas[0].shape
    chips = listing.shape[1] // CORES
    depth = blocks[0].shape[1]
    operands = [listing, *screens, *blocks, *thetas] + ([] if carried is None else [carried])
    return pl.pallas_call(
        functools.partial(
            terms_kernel, first=first, count=count, vectors=vectors, batch=batch, carried=carried is not None
        ),
        in_specs=[SMEM] * 3 + [VMEM] * (len(operands) - 3),
        out_specs=VMEM,
        out_shape=jax.ShapeDtypeStruct((chips, 1, out_width), jnp.float32),
        scratch_shapes=[
            pltpu.VMEM((CORES, count * occupied, depth), thetas[0].dtype),
            pltpu.VMEM((CORES * vectors + 8, batch * occupied), jnp.float32),
        ],
        compiler_params=PARAMS,
        cost_estimate=SMALL,
        name="chip_terms",
    )(*operands)


def finish_kernel(rows_ref, bias_ref, energy_ref, bias_buf, energy_buf, sems, *, used, scale):
    chips, _, width = rows_ref.shape
    fit = LANES // used if width == LANES else 0
    lane = lax.broadcasted_iota(jnp.int32, (1, width), 1)
    if fit and chips % fit == 0:
        for d in range(0, chips, fit):
            packed = rows_ref[d]
            for i in range(1, fit):
                packed = jnp.where(lane < i * used, packed, pltpu.roll(rows_ref[d + i], i * used, 1))
            bias_buf[:, d * used:(d + fit) * used] = packed
    else:
        for d in range(chips):
            bias_buf[:, d * used:(d + 1) * used] = rows_ref[d, :, :used]
    bias_copy = pltpu.make_async_copy(bias_buf, bias_ref, sems.at[0])
    bias_copy.start()
    total = rows_ref[0]
    for d in range(1, chips):
        total = total + rows_ref[d]
    energy_buf[...] = total[:, used:used + 1] * scale
    energy_copy = pltpu.make_async_copy(energy_buf, energy_ref, sems.at[1])
    energy_copy.start()
    bias_copy.wait()
    energy_copy.wait()


def finish(rows, used, scale):
    chips = rows.shape[0]
    shapes = [(1, chips * used), (1, 1)]
    force_bias, energy = pl.pallas_call(
        functools.partial(finish_kernel, used=used, scale=scale),
        in_specs=[VMEM],
        out_specs=[pl.BlockSpec(memory_space=pl.ANY)] * 2,
        out_shape=[jax.ShapeDtypeStruct(s, jnp.float32) for s in shapes],
        scratch_shapes=[pltpu.VMEM(s, jnp.float32) for s in shapes] + [pltpu.SemaphoreType.DMA((2,))],
        name="finish",
    )(rows)
    return force_bias, energy.reshape(1)


def body(theta, chol_tiles, screen, tile_list):
    groups = lax.axis_size("chol")
    chips = groups // CORES
    half = chips // 2
    _, occupied, _ = theta.shape
    vectors = chol_tiles.shape[2]
    used = CORES * vectors
    out_width = LANES * ((used + 1 + LANES - 1) // LANES)
    listing = tile_list.T

    def to_chip(x, offset):
        return lax.ppermute(x, "chol", [(i, i ^ (offset * CORES)) for i in range(groups)])

    def to_core(x):
        return lax.ppermute(x, "chol", [(i, i ^ 1) for i in range(groups)])

    far = to_chip(theta, half)
    near = [theta] + [to_chip(theta, offset) for offset in range(1, half)]
    own, own_turned = prepare_block(chol_tiles)
    far, own = lax.optimization_barrier((far, own))
    beyond = [far] + [to_chip(far, offset) for offset in range(1, half)]
    other, other_turned = prepare_block(to_core(chol_tiles))
    other, late_screen = lax.optimization_barrier((other, screen))
    screens = [screen, to_core(late_screen)]
    blocks = [own, own_turned, other, other_turned]

    rows = chip_terms(listing, screens, blocks, near, None, 0, vectors, out_width)
    rows = chip_terms(listing, screens, blocks, beyond, rows, half, vectors, out_width)
    same_core = [list(range(core, groups, CORES)) for core in range(CORES)]
    back = lax.all_to_all(rows, "chol", split_axis=0, concat_axis=0, tiled=True, axis_index_groups=same_core)
    return finish(back, used, 1.0 / (2.0 * occupied * occupied))


def solution(mesh):
    in_specs = (
        P(("grp", "chol"), None, None),
        P("chol", None, None, None, None),
        P("chol", None),
        P(),
    )
    out_specs = (P(("grp", "chol"), None), P(("grp", "chol")))
    return jax.shard_map(body, mesh=mesh, in_specs=in_specs, out_specs=out_specs, check_vma=False)
```

```python
import functools

import jax
import jax.numpy as jnp
from jax import lax
from jax.experimental import pallas as pl
from jax.experimental.pallas import tpu as pltpu
from jax.sharding import PartitionSpec as P

LANES = 128
CORES = 2
VMEM_LIMIT = 32 * 1024 * 1024
K_STEP = 16
TURNED = 8
BATCH = 4
VMEM = pl.BlockSpec(memory_space=pltpu.VMEM)
SMEM = pl.BlockSpec(memory_space=pltpu.SMEM)
PARAMS = pltpu.CompilerParams(vmem_limit_bytes=VMEM_LIMIT)
SMALL = pl.CostEstimate(flops=0, bytes_accessed=0, transcendentals=0)
NT = (((1,), (1,)), ((), ()))
NN = (((1,), (0,)), ((), ()))


def prepare_kernel(screen_ref, chol_ref, block_ref, turned_ref):
    _, listed, vectors, occupied, width = chol_ref.shape
    span = TURNED * occupied
    for m in range(listed):
        keep = jnp.full((1, width), screen_ref[0, m].astype(jnp.float32)).astype(chol_ref.dtype)
        tile = chol_ref[0, m].reshape(vectors * occupied, width) * keep
        block_ref[:, m * width:(m + 1) * width] = tile
        for c in range(vectors // K_STEP):
            start = c * K_STEP * occupied
            turned_ref[m * width:(m + 1) * width, c * span:(c + 1) * span] = tile[start:start + span].T


def prepare_block(screen, chol_tiles):
    _, listed, vectors, occupied, width = chol_tiles.shape
    rows, depth = vectors * occupied, listed * width
    return pl.pallas_call(
        prepare_kernel,
        in_specs=[SMEM, VMEM],
        out_specs=[VMEM, VMEM],
        out_shape=[
            jax.ShapeDtypeStruct((rows, depth), chol_tiles.dtype),
            jax.ShapeDtypeStruct((depth, rows // K_STEP * TURNED), chol_tiles.dtype),
        ],
        compiler_params=PARAMS,
        cost_estimate=SMALL,
        name="prepare_block",
    )(screen, chol_tiles)


def fold_rows(blocks, sub):
    high = sub < 4
    pairs = []
    for i in range(4):
        a, b = blocks[i], blocks[i + 4]
        pairs.append(jnp.where(high, a, b) + pltpu.roll(jnp.where(high, b, a), 4, 0))
    for shift in (2, 1):
        first = sub % (2 * shift) < shift
        half = len(pairs) // 2
        pairs = [
            jnp.where(
                first,
                pairs[i] + pltpu.roll(pairs[i], 8 - shift, 0),
                pairs[i + half] + pltpu.roll(pairs[i + half], shift, 0),
            )
            for i in range(half)
        ]
    return pairs[0]


def batch_terms(block_ref, turned_ref, theta, cross, store_rows, vectors, occupied):
    columns = theta.shape[0]
    tiles = columns // LANES

    low = lax.broadcasted_iota(jnp.int32, (occupied, LANES), 1) < occupied
    sub8 = lax.broadcasted_iota(jnp.int32, (8, LANES), 0)
    lane8 = lax.broadcasted_iota(jnp.int32, (8, LANES), 1)
    strip = (lane8 % occupied) // 8
    on_diag = lane8 % 8 == sub8

    def diagonal(block):
        merged = block[:8]
        for r in range(1, occupied // 8):
            merged = jnp.where(strip == r, block[8 * r:8 * r + 8], merged)
        return jnp.where(on_diag, merged, 0.0)

    for k0 in range(0, vectors, K_STEP):
        span = slice(k0 * occupied, (k0 + K_STEP) * occupied)
        inner_mat = lax.dot_general(block_ref[span, :], theta, NT, preferred_element_type=jnp.float32)
        turned = slice(k0 // K_STEP * TURNED * occupied, (k0 // K_STEP + 1) * TURNED * occupied)
        flipped = lax.dot_general(theta, turned_ref[:, turned], NN, preferred_element_type=jnp.float32)
        for k8 in range(0, K_STEP, 8):
            for t in range(tiles):
                c0 = t * LANES
                diagonals = []
                for k in range(k8, k8 + 8, 2):
                    r0 = k * occupied
                    top = inner_mat[r0:r0 + occupied, c0:c0 + LANES]
                    bottom = inner_mat[r0 + occupied:r0 + 2 * occupied, c0:c0 + LANES]
                    if k < TURNED:
                        other = flipped[c0:c0 + LANES, r0:r0 + LANES]
                    else:
                        other = inner_mat[r0:r0 + LANES, c0:c0 + LANES].T
                    f_top, f_bottom = other[:occupied], other[occupied:]
                    swapped = pltpu.roll(jnp.where(low, f_bottom, f_top), occupied, 1)
                    product = jnp.where(low, top, bottom) * jnp.where(low, f_top, f_bottom)
                    product = product + jnp.where(low, bottom, top) * swapped
                    cross[t] = cross[t] + jnp.sum(product.reshape(occupied // 8, 8, LANES), axis=0)
                    diagonals.append(diagonal(top))
                    diagonals.append(diagonal(bottom))
                store_rows(k0 + k8, t, fold_rows(diagonals, sub8))


def terms_kernel(list_ref, *refs, first, count, falling, vectors, batch, carried):
    block_refs, theta_refs, rest = refs[:4], refs[4:4 + count], refs[4 + count:]
    out_ref, picked_ref, rows_ref = rest[-3:]
    listed = list_ref.shape[0]
    _, occupied, _ = theta_refs[0].shape
    width = block_refs[0].shape[1] // listed
    used = CORES * vectors
    columns = batch * occupied
    tiles = columns // LANES
    out_width = out_ref.shape[2]
    me = lax.axis_index("chol")
    core = lax.rem(me, CORES)
    chip = me // CORES

    for b, group in enumerate((me, me ^ 1)):
        for m in range(listed):
            start = pl.multiple_of(list_ref[m, group] * width, width)
            for i, ref in enumerate(theta_refs):
                picked_ref[b, i * occupied:(i + 1) * occupied, m * width:(m + 1) * width] = ref[0, :, pl.ds(start, width)]

    if carried:
        out_ref[...] = rest[0][...]
    else:
        out_ref[...] = jnp.zeros(out_ref.shape, out_ref.dtype)

    def one_batch(index):
        start = index * occupied
        rows = pl.ds(start if isinstance(index, int) else pl.multiple_of(start, columns), columns)
        cross = [jnp.zeros((8, LANES), jnp.float32) for _ in range(tiles)]
        for b in range(CORES):
            place = (core ^ b) * vectors

            def store_rows(k, t, value, place=place):
                rows_ref[pl.ds(pl.multiple_of(place + k, 8), 8), t * LANES:(t + 1) * LANES] = value

            batch_terms(
                block_refs[2 * b], block_refs[2 * b + 1], picked_ref[b, rows, :], cross, store_rows, vectors, occupied
            )
        for t in range(tiles):
            rows_ref[used:used + 8, t * LANES:(t + 1) * LANES] = cross[t]
        values = rows_ref[...]
        parts = []
        for _ in range(3):
            part = values.astype(jnp.bfloat16)
            parts.append(part)
            values = values - part.astype(jnp.float32)
        seg_row = lax.broadcasted_iota(jnp.int32, (8, columns), 0)
        seg_col = lax.broadcasted_iota(jnp.int32, (8, columns), 1)
        segment = jnp.where(seg_col // occupied == seg_row, 1.0, 0.0).astype(jnp.bfloat16)
        sums = sum(
            lax.dot_general(segment, part, NT, preferred_element_type=jnp.float32) for part in parts
        )
        bias = sums[:, :used]
        energy = jnp.sum(bias * bias, axis=1, keepdims=True) - jnp.sum(
            sums[:, used:used + 8], axis=1, keepdims=True
        )
        for i in range(batch):
            place = lax.rem(count - index - i, count) if falling else index + i
            owner = chip ^ (first + place)
            out_ref[pl.ds(owner, 1), 0, :used] = bias[i:i + 1]
            out_ref[pl.ds(owner, 1), 0, used:used + 1] = energy[i:i + 1]

    if count == batch:
        one_batch(0)
    else:
        @pl.loop(0, count // batch)
        def _(step):
            one_batch(step * batch)


def chip_terms(listing, blocks, thetas, carried, first, falling, vectors, out_width):
    count = len(thetas)
    if falling:
        thetas = thetas[:1] + thetas[:0:-1]
    batch = min(count, BATCH)
    _, occupied, _ = thetas[0].shape
    chips = listing.shape[1] // CORES
    depth = blocks[0].shape[1]
    operands = [listing, *blocks, *thetas] + ([] if carried is None else [carried])
    return pl.pallas_call(
        functools.partial(
            terms_kernel, first=first, count=count, falling=falling, vectors=vectors, batch=batch,
            carried=carried is not None,
        ),
        in_specs=[SMEM] + [VMEM] * (len(operands) - 1),
        out_specs=VMEM,
        out_shape=jax.ShapeDtypeStruct((chips, 1, out_width), jnp.float32),
        scratch_shapes=[
            pltpu.VMEM((CORES, count * occupied, depth), thetas[0].dtype),
            pltpu.VMEM((CORES * vectors + 8, batch * occupied), jnp.float32),
        ],
        compiler_params=PARAMS,
        cost_estimate=SMALL,
        name="chip_terms",
    )(*operands)


def finish_kernel(rows_ref, bias_ref, energy_ref, bias_buf, energy_buf, sems, *, used, scale):
    chips, _, width = rows_ref.shape
    fit = LANES // used if width == LANES else 0
    lane = lax.broadcasted_iota(jnp.int32, (1, width), 1)
    if fit and chips % fit == 0:
        for d in range(0, chips, fit):
            packed = rows_ref[d]
            for i in range(1, fit):
                packed = jnp.where(lane < i * used, packed, pltpu.roll(rows_ref[d + i], i * used, 1))
            bias_buf[:, d * used:(d + fit) * used] = packed
    else:
        for d in range(chips):
            bias_buf[:, d * used:(d + 1) * used] = rows_ref[d, :, :used]
    bias_copy = pltpu.make_async_copy(bias_buf, bias_ref, sems.at[0])
    bias_copy.start()
    total = rows_ref[0]
    for d in range(1, chips):
        total = total + rows_ref[d]
    energy_buf[...] = total[:, used:used + 1] * scale
    energy_copy = pltpu.make_async_copy(energy_buf, energy_ref, sems.at[1])
    energy_copy.start()
    bias_copy.wait()
    energy_copy.wait()


def finish(rows, used, scale):
    chips = rows.shape[0]
    shapes = [(1, chips * used), (1, 1)]
    force_bias, energy = pl.pallas_call(
        functools.partial(finish_kernel, used=used, scale=scale),
        in_specs=[VMEM],
        out_specs=[pl.BlockSpec(memory_space=pl.ANY)] * 2,
        out_shape=[jax.ShapeDtypeStruct(s, jnp.float32) for s in shapes],
        scratch_shapes=[pltpu.VMEM(s, jnp.float32) for s in shapes] + [pltpu.SemaphoreType.DMA((2,))],
        name="finish",
    )(rows)
    return force_bias, energy.reshape(1)


def body(theta, chol_tiles, screen, tile_list):
    groups = lax.axis_size("chol")
    chips = groups // CORES
    half = chips // 2
    _, occupied, _ = theta.shape
    vectors = chol_tiles.shape[2]
    used = CORES * vectors
    out_width = LANES * ((used + 1 + LANES - 1) // LANES)
    listing = tile_list.T

    def to_chip(x, offset):
        return lax.ppermute(x, "chol", [(i, i ^ (offset * CORES)) for i in range(groups)])

    def to_core(x):
        return lax.ppermute(x, "chol", [(i, i ^ 1) for i in range(groups)])

    far = to_chip(theta, half)
    near = [theta] + [to_chip(theta, offset) for offset in range(1, half)]
    own, own_turned = prepare_block(screen, chol_tiles)
    near[1], near[2], own, far = lax.optimization_barrier((near[1], near[2], own, far))
    beyond = [far] + [to_chip(far, offset) for offset in range(1, half)]
    other_chol, late_screen, near[-1] = lax.optimization_barrier((to_core(chol_tiles), screen, near[-1]))
    other, other_turned = prepare_block(to_core(late_screen), other_chol)
    blocks = [own, own_turned, other, other_turned]

    rows = chip_terms(listing, blocks, near, None, 0, False, vectors, out_width)
    rows = chip_terms(listing, blocks, beyond, rows, half, True, vectors, out_width)
    same_core = [list(range(core, groups, CORES)) for core in range(CORES)]
    back = lax.all_to_all(rows, "chol", split_axis=0, concat_axis=0, tiled=True, axis_index_groups=same_core)
    return finish(back, used, 1.0 / (2.0 * occupied * occupied))


def solution(mesh):
    in_specs = (
        P(("grp", "chol"), None, None),
        P("chol", None, None, None, None),
        P("chol", None),
        P(),
    )
    out_specs = (P(("grp", "chol"), None), P(("grp", "chol")))
    return jax.shard_map(body, mesh=mesh, in_specs=in_specs, out_specs=out_specs, check_vma=False)
```

```python
import functools

import jax
import jax.numpy as jnp
from jax import lax
from jax.experimental import pallas as pl
from jax.experimental.pallas import tpu as pltpu
from jax.sharding import PartitionSpec as P

LANES = 128
CORES = 2
VMEM_LIMIT = 32 * 1024 * 1024
K_STEP = 32
TURNED = 16
BATCH = 4
VMEM = pl.BlockSpec(memory_space=pltpu.VMEM)
SMEM = pl.BlockSpec(memory_space=pltpu.SMEM)
PARAMS = pltpu.CompilerParams(vmem_limit_bytes=VMEM_LIMIT)
SMALL = pl.CostEstimate(flops=0, bytes_accessed=0, transcendentals=0)
NT = (((1,), (1,)), ((), ()))
NN = (((1,), (0,)), ((), ()))


def prepare_kernel(screen_ref, chol_ref, block_ref, turned_ref):
    _, listed, vectors, occupied, width = chol_ref.shape
    span = TURNED * occupied
    for m in range(listed):
        keep = jnp.full((1, width), screen_ref[0, m].astype(jnp.float32)).astype(chol_ref.dtype)
        tile = chol_ref[0, m].reshape(vectors * occupied, width) * keep
        block_ref[:, m * width:(m + 1) * width] = tile
        for c in range(vectors // K_STEP):
            start = c * K_STEP * occupied
            turned_ref[m * width:(m + 1) * width, c * span:(c + 1) * span] = tile[start:start + span].T


def prepare_block(screen, chol_tiles):
    _, listed, vectors, occupied, width = chol_tiles.shape
    rows, depth = vectors * occupied, listed * width
    return pl.pallas_call(
        prepare_kernel,
        in_specs=[SMEM, VMEM],
        out_specs=[VMEM, VMEM],
        out_shape=[
            jax.ShapeDtypeStruct((rows, depth), chol_tiles.dtype),
            jax.ShapeDtypeStruct((depth, rows // K_STEP * TURNED), chol_tiles.dtype),
        ],
        compiler_params=PARAMS,
        cost_estimate=SMALL,
        name="prepare_block",
    )(screen, chol_tiles)


def fold_rows(blocks, sub):
    high = sub < 4
    pairs = []
    for i in range(4):
        a, b = blocks[i], blocks[i + 4]
        pairs.append(jnp.where(high, a, b) + pltpu.roll(jnp.where(high, b, a), 4, 0))
    for shift in (2, 1):
        first = sub % (2 * shift) < shift
        half = len(pairs) // 2
        pairs = [
            jnp.where(
                first,
                pairs[i] + pltpu.roll(pairs[i], 8 - shift, 0),
                pairs[i + half] + pltpu.roll(pairs[i + half], shift, 0),
            )
            for i in range(half)
        ]
    return pairs[0]


def batch_terms(block_ref, turned_ref, theta, cross, store_rows, vectors, occupied):
    columns = theta.shape[0]
    tiles = columns // LANES

    low = lax.broadcasted_iota(jnp.int32, (occupied, LANES), 1) < occupied
    sub8 = lax.broadcasted_iota(jnp.int32, (8, LANES), 0)
    lane8 = lax.broadcasted_iota(jnp.int32, (8, LANES), 1)
    strip = (lane8 % occupied) // 8
    on_diag = lane8 % 8 == sub8

    def diagonal(block):
        merged = block[:8]
        for r in range(1, occupied // 8):
            merged = jnp.where(strip == r, block[8 * r:8 * r + 8], merged)
        return jnp.where(on_diag, merged, 0.0)

    for k0 in range(0, vectors, K_STEP):
        span = slice(k0 * occupied, (k0 + K_STEP) * occupied)
        inner_mat = lax.dot_general(block_ref[span, :], theta, NT, preferred_element_type=jnp.float32)
        turned = slice(k0 // K_STEP * TURNED * occupied, (k0 // K_STEP + 1) * TURNED * occupied)
        flipped = lax.dot_general(theta, turned_ref[:, turned], NN, preferred_element_type=jnp.float32)
        for k8 in range(0, K_STEP, 8):
            for t in range(tiles):
                c0 = t * LANES
                diagonals = []
                for k in range(k8, k8 + 8, 2):
                    r0 = k * occupied
                    top = inner_mat[r0:r0 + occupied, c0:c0 + LANES]
                    bottom = inner_mat[r0 + occupied:r0 + 2 * occupied, c0:c0 + LANES]
                    if k < TURNED:
                        other = flipped[c0:c0 + LANES, r0:r0 + LANES]
                    else:
                        other = inner_mat[r0:r0 + LANES, c0:c0 + LANES].T
                    f_top, f_bottom = other[:occupied], other[occupied:]
                    swapped = pltpu.roll(jnp.where(low, f_bottom, f_top), occupied, 1)
                    product = jnp.where(low, top, bottom) * jnp.where(low, f_top, f_bottom)
                    product = product + jnp.where(low, bottom, top) * swapped
                    cross[t] = cross[t] + jnp.sum(product.reshape(occupied // 8, 8, LANES), axis=0)
                    diagonals.append(diagonal(top))
                    diagonals.append(diagonal(bottom))
                store_rows(k0 + k8, t, fold_rows(diagonals, sub8))


def terms_kernel(list_ref, *refs, first, count, falling, vectors, batch, carried):
    block_refs, theta_refs, rest = refs[:4], refs[4:4 + count], refs[4 + count:]
    out_ref, picked_ref, rows_ref = rest[-3:]
    listed = list_ref.shape[0]
    _, occupied, _ = theta_refs[0].shape
    width = block_refs[0].shape[1] // listed
    used = CORES * vectors
    columns = batch * occupied
    tiles = columns // LANES
    out_width = out_ref.shape[2]
    me = lax.axis_index("chol")
    core = lax.rem(me, CORES)
    chip = me // CORES

    for b, group in enumerate((me, me ^ 1)):
        for m in range(listed):
            start = pl.multiple_of(list_ref[m, group] * width, width)
            for i, ref in enumerate(theta_refs):
                picked_ref[b, i * occupied:(i + 1) * occupied, m * width:(m + 1) * width] = ref[0, :, pl.ds(start, width)]

    if carried:
        out_ref[...] = rest[0][...]
    else:
        out_ref[...] = jnp.zeros(out_ref.shape, out_ref.dtype)

    def one_batch(index):
        start = index * occupied
        rows = pl.ds(start if isinstance(index, int) else pl.multiple_of(start, columns), columns)
        cross = [jnp.zeros((8, LANES), jnp.float32) for _ in range(tiles)]
        for b in range(CORES):
            place = (core ^ b) * vectors

            def store_rows(k, t, value, place=place):
                rows_ref[pl.ds(pl.multiple_of(place + k, 8), 8), t * LANES:(t + 1) * LANES] = value

            batch_terms(
                block_refs[2 * b], block_refs[2 * b + 1], picked_ref[b, rows, :], cross, store_rows, vectors, occupied
            )
        for t in range(tiles):
            rows_ref[used:used + 8, t * LANES:(t + 1) * LANES] = cross[t]
        values = rows_ref[...]
        parts = []
        for _ in range(3):
            part = values.astype(jnp.bfloat16)
            parts.append(part)
            values = values - part.astype(jnp.float32)
        seg_row = lax.broadcasted_iota(jnp.int32, (8, columns), 0)
        seg_col = lax.broadcasted_iota(jnp.int32, (8, columns), 1)
        segment = jnp.where(seg_col // occupied == seg_row, 1.0, 0.0).astype(jnp.bfloat16)
        sums = sum(
            lax.dot_general(segment, part, NT, preferred_element_type=jnp.float32) for part in parts
        )
        bias = sums[:, :used]
        energy = jnp.sum(bias * bias, axis=1, keepdims=True) - jnp.sum(
            sums[:, used:used + 8], axis=1, keepdims=True
        )
        for i in range(batch):
            place = lax.rem(count - index - i, count) if falling else index + i
            owner = chip ^ (first + place)
            out_ref[pl.ds(owner, 1), 0, :used] = bias[i:i + 1]
            out_ref[pl.ds(owner, 1), 0, used:used + 1] = energy[i:i + 1]

    if count == batch:
        one_batch(0)
    else:
        @pl.loop(0, count // batch)
        def _(step):
            one_batch(step * batch)


def chip_terms(listing, blocks, thetas, carried, first, falling, vectors, out_width):
    count = len(thetas)
    if falling:
        thetas = thetas[:1] + thetas[:0:-1]
    batch = min(count, BATCH)
    _, occupied, _ = thetas[0].shape
    chips = listing.shape[1] // CORES
    depth = blocks[0].shape[1]
    operands = [listing, *blocks, *thetas] + ([] if carried is None else [carried])
    return pl.pallas_call(
        functools.partial(
            terms_kernel, first=first, count=count, falling=falling, vectors=vectors, batch=batch,
            carried=carried is not None,
        ),
        in_specs=[SMEM] + [VMEM] * (len(operands) - 1),
        out_specs=VMEM,
        out_shape=jax.ShapeDtypeStruct((chips, 1, out_width), jnp.float32),
        scratch_shapes=[
            pltpu.VMEM((CORES, count * occupied, depth), thetas[0].dtype),
            pltpu.VMEM((CORES * vectors + 8, batch * occupied), jnp.float32),
        ],
        compiler_params=PARAMS,
        cost_estimate=SMALL,
        name="chip_terms",
    )(*operands)


def finish_kernel(rows_ref, bias_ref, energy_ref, bias_buf, energy_buf, sems, *, used, scale):
    chips, _, width = rows_ref.shape
    fit = LANES // used if width == LANES else 0
    lane = lax.broadcasted_iota(jnp.int32, (1, width), 1)
    if fit and chips % fit == 0:
        for d in range(0, chips, fit):
            packed = rows_ref[d]
            for i in range(1, fit):
                packed = jnp.where(lane < i * used, packed, pltpu.roll(rows_ref[d + i], i * used, 1))
            bias_buf[:, d * used:(d + fit) * used] = packed
    else:
        for d in range(chips):
            bias_buf[:, d * used:(d + 1) * used] = rows_ref[d, :, :used]
    bias_copy = pltpu.make_async_copy(bias_buf, bias_ref, sems.at[0])
    bias_copy.start()
    total = rows_ref[0]
    for d in range(1, chips):
        total = total + rows_ref[d]
    energy_buf[...] = total[:, used:used + 1] * scale
    energy_copy = pltpu.make_async_copy(energy_buf, energy_ref, sems.at[1])
    energy_copy.start()
    bias_copy.wait()
    energy_copy.wait()


def finish(rows, used, scale):
    chips = rows.shape[0]
    shapes = [(1, chips * used), (1, 1)]
    force_bias, energy = pl.pallas_call(
        functools.partial(finish_kernel, used=used, scale=scale),
        in_specs=[VMEM],
        out_specs=[pl.BlockSpec(memory_space=pl.ANY)] * 2,
        out_shape=[jax.ShapeDtypeStruct(s, jnp.float32) for s in shapes],
        scratch_shapes=[pltpu.VMEM(s, jnp.float32) for s in shapes] + [pltpu.SemaphoreType.DMA((2,))],
        name="finish",
    )(rows)
    return force_bias, energy.reshape(1)


def body(theta, chol_tiles, screen, tile_list):
    groups = lax.axis_size("chol")
    chips = groups // CORES
    half = chips // 2
    _, occupied, _ = theta.shape
    vectors = chol_tiles.shape[2]
    used = CORES * vectors
    out_width = LANES * ((used + 1 + LANES - 1) // LANES)
    listing = tile_list.T

    def to_chip(x, offset):
        return lax.ppermute(x, "chol", [(i, i ^ (offset * CORES)) for i in range(groups)])

    def to_core(x):
        return lax.ppermute(x, "chol", [(i, i ^ 1) for i in range(groups)])

    far = to_chip(theta, half)
    near = [theta] + [to_chip(theta, offset) for offset in range(1, half - 1)]
    own, own_turned = prepare_block(screen, chol_tiles)
    near[1], own, late_theta = lax.optimization_barrier((near[1], own, theta))
    near.append(to_chip(late_theta, half - 1))
    far, near[2] = lax.optimization_barrier((far, near[2]))
    beyond = [far] + [to_chip(far, offset) for offset in range(1, half)]
    other_chol, late_screen, near[-1] = lax.optimization_barrier((to_core(chol_tiles), screen, near[-1]))
    other, other_turned = prepare_block(to_core(late_screen), other_chol)
    blocks = [own, own_turned, other, other_turned]

    rows = chip_terms(listing, blocks, near, None, 0, False, vectors, out_width)
    rows = chip_terms(listing, blocks, beyond, rows, half, False, vectors, out_width)
    same_core = [list(range(core, groups, CORES)) for core in range(CORES)]
    back = lax.all_to_all(rows, "chol", split_axis=0, concat_axis=0, tiled=True, axis_index_groups=same_core)
    return finish(back, used, 1.0 / (2.0 * occupied * occupied))


def solution(mesh):
    in_specs = (
        P(("grp", "chol"), None, None),
        P("chol", None, None, None, None),
        P("chol", None),
        P(),
    )
    out_specs = (P(("grp", "chol"), None), P(("grp", "chol")))
    return jax.shard_map(body, mesh=mesh, in_specs=in_specs, out_specs=out_specs, check_vma=False)
```

```python
import functools

import jax
import jax.numpy as jnp
from jax import lax
from jax.experimental import pallas as pl
from jax.experimental.pallas import tpu as pltpu
from jax.sharding import PartitionSpec as P

LANES = 128
CORES = 2
VMEM_LIMIT = 32 * 1024 * 1024
K_STEP = 16
TURNED = 8
BATCH = 4
VMEM = pl.BlockSpec(memory_space=pltpu.VMEM)
SMEM = pl.BlockSpec(memory_space=pltpu.SMEM)
PARAMS = pltpu.CompilerParams(vmem_limit_bytes=VMEM_LIMIT)
SMALL = pl.CostEstimate(flops=0, bytes_accessed=0, transcendentals=0)
NT = (((1,), (1,)), ((), ()))
NN = (((1,), (0,)), ((), ()))


def prepare_kernel(screen_ref, chol_ref, block_ref, turned_ref):
    _, listed, vectors, occupied, width = chol_ref.shape
    span = TURNED * occupied
    for m in range(listed):
        keep = jnp.full((1, width), screen_ref[0, m].astype(jnp.float32)).astype(chol_ref.dtype)
        tile = chol_ref[0, m].reshape(vectors * occupied, width) * keep
        block_ref[:, m * width:(m + 1) * width] = tile
        for c in range(vectors // K_STEP):
            start = c * K_STEP * occupied
            turned_ref[m * width:(m + 1) * width, c * span:(c + 1) * span] = tile[start:start + span].T


def prepare_block(screen, chol_tiles):
    _, listed, vectors, occupied, width = chol_tiles.shape
    rows, depth = vectors * occupied, listed * width
    return pl.pallas_call(
        prepare_kernel,
        in_specs=[SMEM, VMEM],
        out_specs=[VMEM, VMEM],
        out_shape=[
            jax.ShapeDtypeStruct((rows, depth), chol_tiles.dtype),
            jax.ShapeDtypeStruct((depth, rows // K_STEP * TURNED), chol_tiles.dtype),
        ],
        compiler_params=PARAMS,
        cost_estimate=SMALL,
        name="prepare_block",
    )(screen, chol_tiles)


def fold_rows(blocks, sub):
    high = sub < 4
    pairs = []
    for i in range(4):
        a, b = blocks[i], blocks[i + 4]
        pairs.append(jnp.where(high, a, b) + pltpu.roll(jnp.where(high, b, a), 4, 0))
    for shift in (2, 1):
        first = sub % (2 * shift) < shift
        half = len(pairs) // 2
        pairs = [
            jnp.where(
                first,
                pairs[i] + pltpu.roll(pairs[i], 8 - shift, 0),
                pairs[i + half] + pltpu.roll(pairs[i + half], shift, 0),
            )
            for i in range(half)
        ]
    return pairs[0]


def batch_terms(block_ref, turned_ref, theta, cross, store_rows, vectors, occupied):
    columns = theta.shape[0]
    tiles = columns // LANES

    low = lax.broadcasted_iota(jnp.int32, (occupied, LANES), 1) < occupied
    sub8 = lax.broadcasted_iota(jnp.int32, (8, LANES), 0)
    lane8 = lax.broadcasted_iota(jnp.int32, (8, LANES), 1)
    strip = (lane8 % occupied) // 8
    on_diag = lane8 % 8 == sub8

    def diagonal(block):
        merged = block[:8]
        for r in range(1, occupied // 8):
            merged = jnp.where(strip == r, block[8 * r:8 * r + 8], merged)
        return jnp.where(on_diag, merged, 0.0)

    for k0 in range(0, vectors, K_STEP):
        span = slice(k0 * occupied, (k0 + K_STEP) * occupied)
        inner_mat = lax.dot_general(block_ref[span, :], theta, NT, preferred_element_type=jnp.float32)
        turned = slice(k0 // K_STEP * TURNED * occupied, (k0 // K_STEP + 1) * TURNED * occupied)
        flipped = lax.dot_general(theta, turned_ref[:, turned], NN, preferred_element_type=jnp.float32)
        for k8 in range(0, K_STEP, 8):
            for t in range(tiles):
                c0 = t * LANES
                diagonals = []
                for k in range(k8, k8 + 8, 2):
                    r0 = k * occupied
                    top = inner_mat[r0:r0 + occupied, c0:c0 + LANES]
                    bottom = inner_mat[r0 + occupied:r0 + 2 * occupied, c0:c0 + LANES]
                    if k < TURNED:
                        other = flipped[c0:c0 + LANES, r0:r0 + LANES]
                    else:
                        other = inner_mat[r0:r0 + LANES, c0:c0 + LANES].T
                    f_top, f_bottom = other[:occupied], other[occupied:]
                    swapped = pltpu.roll(jnp.where(low, f_bottom, f_top), occupied, 1)
                    product = jnp.where(low, top, bottom) * jnp.where(low, f_top, f_bottom)
                    product = product + jnp.where(low, bottom, top) * swapped
                    cross[t] = cross[t] + jnp.sum(product.reshape(occupied // 8, 8, LANES), axis=0)
                    diagonals.append(diagonal(top))
                    diagonals.append(diagonal(bottom))
                store_rows(k0 + k8, t, fold_rows(diagonals, sub8))


def terms_kernel(list_ref, *refs, first, jump, count, places, vectors, batch, carried):
    held = len(places)
    block_refs, theta_refs, rest = refs[:4], refs[4:4 + held], refs[4 + held:]
    out_ref, picked_ref, rows_ref = rest[-3:]
    listed = list_ref.shape[0]
    occupied = block_refs[0].shape[0] // vectors
    width = block_refs[0].shape[1] // listed
    used = CORES * vectors
    columns = batch * occupied
    tiles = columns // LANES
    out_width = out_ref.shape[2]
    me = lax.axis_index("chol")
    core = lax.rem(me, CORES)
    chip = me // CORES

    for b, group in enumerate((me, me ^ 1)):
        for m in range(listed):
            start = pl.multiple_of(list_ref[m, group] * width, width)
            for row, ref in zip(places, theta_refs):
                picked_ref[b, row:row + ref.shape[1], m * width:(m + 1) * width] = ref[0, :, pl.ds(start, width)]

    if carried:
        out_ref[...] = rest[0][...]
    else:
        out_ref[...] = jnp.zeros(out_ref.shape, out_ref.dtype)

    def one_batch(index):
        start = index * occupied
        rows = pl.ds(start if isinstance(index, int) else pl.multiple_of(start, columns), columns)
        cross = [jnp.zeros((8, LANES), jnp.float32) for _ in range(tiles)]
        for b in range(CORES):
            place = (core ^ b) * vectors

            def store_rows(k, t, value, place=place):
                rows_ref[pl.ds(pl.multiple_of(place + k, 8), 8), t * LANES:(t + 1) * LANES] = value

            batch_terms(
                block_refs[2 * b], block_refs[2 * b + 1], picked_ref[b, rows, :], cross, store_rows, vectors, occupied
            )
        for t in range(tiles):
            rows_ref[used:used + 8, t * LANES:(t + 1) * LANES] = cross[t]
        values = rows_ref[...]
        parts = []
        for _ in range(3):
            part = values.astype(jnp.bfloat16)
            parts.append(part)
            values = values - part.astype(jnp.float32)
        seg_row = lax.broadcasted_iota(jnp.int32, (8, columns), 0)
        seg_col = lax.broadcasted_iota(jnp.int32, (8, columns), 1)
        segment = jnp.where(seg_col // occupied == seg_row, 1.0, 0.0).astype(jnp.bfloat16)
        sums = sum(
            lax.dot_general(segment, part, NT, preferred_element_type=jnp.float32) for part in parts
        )
        bias = sums[:, :used]
        energy = jnp.sum(bias * bias, axis=1, keepdims=True) - jnp.sum(
            sums[:, used:used + 8], axis=1, keepdims=True
        )
        for i in range(batch):
            place = jnp.int32(index + i)
            owner = chip ^ (first + place + (place >= jump).astype(jnp.int32))
            out_ref[pl.ds(owner, 1), 0, :used] = bias[i:i + 1]
            out_ref[pl.ds(owner, 1), 0, used:used + 1] = energy[i:i + 1]

    if count == batch:
        one_batch(0)
    else:
        @pl.loop(0, count // batch)
        def _(step):
            one_batch(step * batch)


def chip_terms(listing, blocks, thetas, carried, first, jump, vectors, out_width):
    count = len(thetas)
    occupied = sum(part.shape[1] for part in thetas[0])
    pieces = []
    for walker, parts in enumerate(thetas):
        row = walker * occupied
        for index, part in enumerate(parts):
            pieces.append((index, row, part))
            row += part.shape[1]
    pieces.sort(key=lambda piece: piece[0])
    places, thetas = [piece[1] for piece in pieces], [piece[2] for piece in pieces]
    batch = min(count, BATCH)
    chips = listing.shape[1] // CORES
    depth = blocks[0].shape[1]
    operands = [listing, *blocks, *thetas] + ([] if carried is None else [carried])
    return pl.pallas_call(
        functools.partial(
            terms_kernel, first=first, jump=jump, count=count, places=places, vectors=vectors, batch=batch,
            carried=carried is not None,
        ),
        in_specs=[SMEM] + [VMEM] * (len(operands) - 1),
        out_specs=VMEM,
        out_shape=jax.ShapeDtypeStruct((chips, 1, out_width), jnp.float32),
        scratch_shapes=[
            pltpu.VMEM((CORES, count * occupied, depth), thetas[0].dtype),
            pltpu.VMEM((CORES * vectors + 8, batch * occupied), jnp.float32),
        ],
        compiler_params=PARAMS,
        cost_estimate=SMALL,
        name="chip_terms",
    )(*operands)


def finish_kernel(rows_ref, bias_ref, energy_ref, bias_buf, energy_buf, sems, *, used, scale):
    chips, _, width = rows_ref.shape
    fit = LANES // used if width == LANES else 0
    lane = lax.broadcasted_iota(jnp.int32, (1, width), 1)
    if fit and chips % fit == 0:
        for d in range(0, chips, fit):
            packed = rows_ref[d]
            for i in range(1, fit):
                packed = jnp.where(lane < i * used, packed, pltpu.roll(rows_ref[d + i], i * used, 1))
            bias_buf[:, d * used:(d + fit) * used] = packed
    else:
        for d in range(chips):
            bias_buf[:, d * used:(d + 1) * used] = rows_ref[d, :, :used]
    bias_copy = pltpu.make_async_copy(bias_buf, bias_ref, sems.at[0])
    bias_copy.start()
    total = rows_ref[0]
    for d in range(1, chips):
        total = total + rows_ref[d]
    energy_buf[...] = total[:, used:used + 1] * scale
    energy_copy = pltpu.make_async_copy(energy_buf, energy_ref, sems.at[1])
    energy_copy.start()
    bias_copy.wait()
    energy_copy.wait()


def finish(rows, used, scale):
    chips = rows.shape[0]
    shapes = [(1, chips * used), (1, 1)]
    force_bias, energy = pl.pallas_call(
        functools.partial(finish_kernel, used=used, scale=scale),
        in_specs=[VMEM],
        out_specs=[pl.BlockSpec(memory_space=pl.ANY)] * 2,
        out_shape=[jax.ShapeDtypeStruct(s, jnp.float32) for s in shapes],
        scratch_shapes=[pltpu.VMEM(s, jnp.float32) for s in shapes] + [pltpu.SemaphoreType.DMA((2,))],
        name="finish",
    )(rows)
    return force_bias, energy.reshape(1)


def body(theta, chol_tiles, screen, tile_list):
    groups = lax.axis_size("chol")
    chips = groups // CORES
    half = chips // 2
    _, occupied, _ = theta.shape
    vectors = chol_tiles.shape[2]
    used = CORES * vectors
    out_width = LANES * ((used + 1 + LANES - 1) // LANES)
    listing = tile_list.T

    def to_chip(x, offset):
        return lax.ppermute(x, "chol", [(i, i ^ (offset * CORES)) for i in range(groups)])

    def to_core(x):
        return lax.ppermute(x, "chol", [(i, i ^ 1) for i in range(groups)])

    middle = occupied // 2
    far = [to_chip(theta[:, :middle], half), to_chip(theta[:, middle:], half)]
    near = [theta] + [to_chip(theta, offset) for offset in range(1, half - 1)]
    own, own_turned = prepare_block(screen, chol_tiles)
    near[1], own, late_screen = lax.optimization_barrier((near[1], own, screen))
    far[0], near[2], other_screen, other_chol, late_theta = lax.optimization_barrier(
        (far[0], near[2], to_core(late_screen), to_core(chol_tiles), theta)
    )
    sent = [to_chip(far[0], offset) for offset in range(1, half)]
    far[1], far[0] = lax.optimization_barrier((far[1], far[0]))
    beyond = [[sent[offset - 1], to_chip(far[1], offset)] for offset in range(1, half)]
    last = to_chip(late_theta, half - 1)
    other, other_turned = prepare_block(other_screen, other_chol)
    blocks = [own, own_turned, other, other_turned]

    rows = chip_terms(listing, blocks, [[x] for x in near] + [far], None, 0, half - 1, vectors, out_width)
    rows = chip_terms(listing, blocks, [[last]] + beyond, rows, half - 1, 1, vectors, out_width)
    same_core = [list(range(core, groups, CORES)) for core in range(CORES)]
    back = lax.all_to_all(rows, "chol", split_axis=0, concat_axis=0, tiled=True, axis_index_groups=same_core)
    return finish(back, used, 1.0 / (2.0 * occupied * occupied))


def solution(mesh):
    in_specs = (
        P(("grp", "chol"), None, None),
        P("chol", None, None, None, None),
        P("chol", None),
        P(),
    )
    out_specs = (P(("grp", "chol"), None), P(("grp", "chol")))
    return jax.shard_map(body, mesh=mesh, in_specs=in_specs, out_specs=out_specs, check_vma=False)
```

```python
import functools

import jax
import jax.numpy as jnp
from jax import lax
from jax.experimental import pallas as pl
from jax.experimental.pallas import tpu as pltpu
from jax.sharding import PartitionSpec as P

LANES = 128
CORES = 2
VMEM_LIMIT = 32 * 1024 * 1024
K_STEP = 16
TURNED = 8
BATCH = 4
VMEM = pl.BlockSpec(memory_space=pltpu.VMEM)
SMEM = pl.BlockSpec(memory_space=pltpu.SMEM)
PARAMS = pltpu.CompilerParams(vmem_limit_bytes=VMEM_LIMIT)
SMALL = pl.CostEstimate(flops=0, bytes_accessed=0, transcendentals=0)
NT = (((1,), (1,)), ((), ()))
NN = (((1,), (0,)), ((), ()))


def prepare_kernel(screen_ref, chol_ref, block_ref, turned_ref):
    _, listed, vectors, occupied, width = chol_ref.shape
    span = TURNED * occupied
    for m in range(listed):
        keep = jnp.full((1, width), screen_ref[0, m].astype(jnp.float32)).astype(chol_ref.dtype)
        tile = chol_ref[0, m].reshape(vectors * occupied, width) * keep
        block_ref[:, m * width:(m + 1) * width] = tile
        for c in range(vectors // K_STEP):
            start = c * K_STEP * occupied
            turned_ref[m * width:(m + 1) * width, c * span:(c + 1) * span] = tile[start:start + span].T


def prepare_block(screen, chol_tiles):
    _, listed, vectors, occupied, width = chol_tiles.shape
    rows, depth = vectors * occupied, listed * width
    return pl.pallas_call(
        prepare_kernel,
        in_specs=[SMEM, VMEM],
        out_specs=[VMEM, VMEM],
        out_shape=[
            jax.ShapeDtypeStruct((rows, depth), chol_tiles.dtype),
            jax.ShapeDtypeStruct((depth, rows // K_STEP * TURNED), chol_tiles.dtype),
        ],
        compiler_params=PARAMS,
        cost_estimate=SMALL,
        name="prepare_block",
    )(screen, chol_tiles)


def fold_rows(blocks, sub):
    high = sub < 4
    pairs = []
    for i in range(4):
        a, b = blocks[i], blocks[i + 4]
        pairs.append(jnp.where(high, a, b) + pltpu.roll(jnp.where(high, b, a), 4, 0))
    for shift in (2, 1):
        first = sub % (2 * shift) < shift
        half = len(pairs) // 2
        pairs = [
            jnp.where(
                first,
                pairs[i] + pltpu.roll(pairs[i], 8 - shift, 0),
                pairs[i + half] + pltpu.roll(pairs[i + half], shift, 0),
            )
            for i in range(half)
        ]
    return pairs[0]


def batch_terms(block_ref, turned_ref, theta, cross, store_rows, vectors, occupied):
    columns = theta.shape[0]
    tiles = columns // LANES

    low = lax.broadcasted_iota(jnp.int32, (occupied, LANES), 1) < occupied
    sub8 = lax.broadcasted_iota(jnp.int32, (8, LANES), 0)
    lane8 = lax.broadcasted_iota(jnp.int32, (8, LANES), 1)
    strip = (lane8 % occupied) // 8
    on_diag = lane8 % 8 == sub8

    def diagonal(block):
        merged = block[:8]
        for r in range(1, occupied // 8):
            merged = jnp.where(strip == r, block[8 * r:8 * r + 8], merged)
        return jnp.where(on_diag, merged, 0.0)

    for k0 in range(0, vectors, K_STEP):
        span = slice(k0 * occupied, (k0 + K_STEP) * occupied)
        inner_mat = lax.dot_general(block_ref[span, :], theta, NT, preferred_element_type=jnp.float32)
        turned = slice(k0 // K_STEP * TURNED * occupied, (k0 // K_STEP + 1) * TURNED * occupied)
        flipped = lax.dot_general(theta, turned_ref[:, turned], NN, preferred_element_type=jnp.float32)
        for k8 in range(0, K_STEP, 8):
            for t in range(tiles):
                c0 = t * LANES
                diagonals = []
                for k in range(k8, k8 + 8, 2):
                    r0 = k * occupied
                    top = inner_mat[r0:r0 + occupied, c0:c0 + LANES]
                    bottom = inner_mat[r0 + occupied:r0 + 2 * occupied, c0:c0 + LANES]
                    if k < TURNED:
                        other = flipped[c0:c0 + LANES, r0:r0 + LANES]
                    else:
                        other = inner_mat[r0:r0 + LANES, c0:c0 + LANES].T
                    f_top, f_bottom = other[:occupied], other[occupied:]
                    swapped = pltpu.roll(jnp.where(low, f_bottom, f_top), occupied, 1)
                    product = jnp.where(low, top, bottom) * jnp.where(low, f_top, f_bottom)
                    product = product + jnp.where(low, bottom, top) * swapped
                    cross[t] = cross[t] + jnp.sum(product.reshape(occupied // 8, 8, LANES), axis=0)
                    diagonals.append(diagonal(top))
                    diagonals.append(diagonal(bottom))
                store_rows(k0 + k8, t, fold_rows(diagonals, sub8))


def terms_kernel(list_ref, *refs, first, count, falling, vectors, batch, carried):
    block_refs, theta_refs, rest = refs[:4], refs[4:4 + count], refs[4 + count:]
    out_ref, picked_ref, rows_ref = rest[-3:]
    listed = list_ref.shape[0]
    _, occupied, _ = theta_refs[0].shape
    width = block_refs[0].shape[1] // listed
    used = CORES * vectors
    columns = batch * occupied
    tiles = columns // LANES
    out_width = out_ref.shape[2]
    me = lax.axis_index("chol")
    core = lax.rem(me, CORES)
    chip = me // CORES

    for b, group in enumerate((me, me ^ 1)):
        for m in range(listed):
            start = pl.multiple_of(list_ref[m, group] * width, width)
            for i, ref in enumerate(theta_refs):
                picked_ref[b, i * occupied:(i + 1) * occupied, m * width:(m + 1) * width] = ref[0, :, pl.ds(start, width)]

    if carried:
        out_ref[...] = rest[0][...]
    else:
        out_ref[...] = jnp.zeros(out_ref.shape, out_ref.dtype)

    def one_batch(index):
        start = index * occupied
        rows = pl.ds(start if isinstance(index, int) else pl.multiple_of(start, columns), columns)
        cross = [jnp.zeros((8, LANES), jnp.float32) for _ in range(tiles)]
        for b in range(CORES):
            place = (core ^ b) * vectors

            def store_rows(k, t, value, place=place):
                rows_ref[pl.ds(pl.multiple_of(place + k, 8), 8), t * LANES:(t + 1) * LANES] = value

            batch_terms(
                block_refs[2 * b], block_refs[2 * b + 1], picked_ref[b, rows, :], cross, store_rows, vectors, occupied
            )
        for t in range(tiles):
            rows_ref[used:used + 8, t * LANES:(t + 1) * LANES] = cross[t]
        values = rows_ref[...]
        parts = []
        for _ in range(3):
            part = values.astype(jnp.bfloat16)
            parts.append(part)
            values = values - part.astype(jnp.float32)
        seg_row = lax.broadcasted_iota(jnp.int32, (8, columns), 0)
        seg_col = lax.broadcasted_iota(jnp.int32, (8, columns), 1)
        segment = jnp.where(seg_col // occupied == seg_row, 1.0, 0.0).astype(jnp.bfloat16)
        sums = sum(
            lax.dot_general(segment, part, NT, preferred_element_type=jnp.float32) for part in parts
        )
        for i in range(batch):
            place = lax.rem(count - index - i, count) if falling else index + i
            owner = chip ^ (first + place)
            out_ref[pl.ds(owner, 1), 0, :used + 8] = sums[i:i + 1]

    if count == batch:
        one_batch(0)
    else:
        @pl.loop(0, count // batch)
        def _(step):
            one_batch(step * batch)


def chip_terms(listing, blocks, thetas, carried, first, falling, vectors, out_width):
    count = len(thetas)
    if falling:
        thetas = thetas[:1] + thetas[:0:-1]
    batch = min(count, BATCH)
    _, occupied, _ = thetas[0].shape
    chips = listing.shape[1] // CORES
    depth = blocks[0].shape[1]
    operands = [listing, *blocks, *thetas] + ([] if carried is None else [carried])
    return pl.pallas_call(
        functools.partial(
            terms_kernel, first=first, count=count, falling=falling, vectors=vectors, batch=batch,
            carried=carried is not None,
        ),
        in_specs=[SMEM] + [VMEM] * (len(operands) - 1),
        out_specs=VMEM,
        out_shape=jax.ShapeDtypeStruct((chips, 1, out_width), jnp.float32),
        scratch_shapes=[
            pltpu.VMEM((CORES, count * occupied, depth), thetas[0].dtype),
            pltpu.VMEM((CORES * vectors + 8, batch * occupied), jnp.float32),
        ],
        compiler_params=PARAMS,
        cost_estimate=SMALL,
        name="chip_terms",
    )(*operands)


def own_kernel(rows_ref, out_ref, *, used):
    chip = lax.axis_index("chol") // CORES
    out_ref[...] = energy_terms(rows_ref[pl.ds(chip, 1), 0, :], used)


def energy_terms(rows, used):
    lane = lax.broadcasted_iota(jnp.int32, rows.shape, 1)
    return jnp.where(lane < used, rows * rows, jnp.where(lane < used + 8, -rows, 0.0))


def finish_kernel(rows_ref, own_ref, bias_ref, energy_ref, bias_buf, energy_buf, sems, *, used, scale):
    chips, _, width = rows_ref.shape
    chip = lax.axis_index("chol") // CORES
    fit = LANES // used if width == LANES else 0
    lane = lax.broadcasted_iota(jnp.int32, (1, width), 1)
    if fit and chips % fit == 0:
        for d in range(0, chips, fit):
            packed = rows_ref[d]
            for i in range(1, fit):
                packed = jnp.where(lane < i * used, packed, pltpu.roll(rows_ref[d + i], i * used, 1))
            bias_buf[:, d * used:(d + fit) * used] = packed
    else:
        for d in range(chips):
            bias_buf[:, d * used:(d + 1) * used] = rows_ref[d, :, :used]
    bias_copy = pltpu.make_async_copy(bias_buf, bias_ref, sems.at[0])
    bias_copy.start()
    total = own_ref[...]
    for d in range(chips):
        total = total + jnp.where(chip == d, 0.0, energy_terms(rows_ref[d], used))
    energy_buf[...] = jnp.sum(total, axis=1, keepdims=True) * scale
    energy_copy = pltpu.make_async_copy(energy_buf, energy_ref, sems.at[1])
    energy_copy.start()
    bias_copy.wait()
    energy_copy.wait()


def finish(back, rows, used, scale):
    chips, _, width = rows.shape
    own = pl.pallas_call(
        functools.partial(own_kernel, used=used),
        in_specs=[VMEM],
        out_specs=VMEM,
        out_shape=jax.ShapeDtypeStruct((1, width), jnp.float32),
        cost_estimate=pl.CostEstimate(flops=0, bytes_accessed=1 << 20, transcendentals=0),
        name="own_terms",
    )(rows)
    shapes = [(1, chips * used), (1, 1)]
    force_bias, energy = pl.pallas_call(
        functools.partial(finish_kernel, used=used, scale=scale),
        in_specs=[VMEM, VMEM],
        out_specs=[pl.BlockSpec(memory_space=pl.ANY)] * 2,
        out_shape=[jax.ShapeDtypeStruct(s, jnp.float32) for s in shapes],
        scratch_shapes=[pltpu.VMEM(s, jnp.float32) for s in shapes] + [pltpu.SemaphoreType.DMA((2,))],
        name="finish",
    )(back, own)
    return force_bias, energy.reshape(1)


def body(theta, chol_tiles, screen, tile_list):
    groups = lax.axis_size("chol")
    chips = groups // CORES
    half = chips // 2
    _, occupied, _ = theta.shape
    vectors = chol_tiles.shape[2]
    used = CORES * vectors
    out_width = LANES * ((used + 8 + LANES - 1) // LANES)
    listing = tile_list.T

    def to_chip(x, offset):
        return lax.ppermute(x, "chol", [(i, i ^ (offset * CORES)) for i in range(groups)])

    def to_core(x):
        return lax.ppermute(x, "chol", [(i, i ^ 1) for i in range(groups)])

    far = to_chip(theta, half)
    near = [theta] + [to_chip(theta, offset) for offset in range(1, half)]
    own, own_turned = prepare_block(screen, chol_tiles)
    near[1], near[2], own, far = lax.optimization_barrier((near[1], near[2], own, far))
    beyond = [far] + [to_chip(far, offset) for offset in range(1, half)]
    other_chol, late_screen, near[-1] = lax.optimization_barrier((to_core(chol_tiles), screen, near[-1]))
    other, other_turned = prepare_block(to_core(late_screen), other_chol)
    blocks = [own, own_turned, other, other_turned]

    rows = chip_terms(listing, blocks, near, None, 0, False, vectors, out_width)
    rows = chip_terms(listing, blocks, beyond, rows, half, True, vectors, out_width)
    same_core = [list(range(core, groups, CORES)) for core in range(CORES)]
    back = lax.all_to_all(rows, "chol", split_axis=0, concat_axis=0, tiled=True, axis_index_groups=same_core)
    return finish(back, rows, used, 1.0 / (2.0 * occupied * occupied))


def solution(mesh):
    in_specs = (
        P(("grp", "chol"), None, None),
        P("chol", None, None, None, None),
        P("chol", None),
        P(),
    )
    out_specs = (P(("grp", "chol"), None), P(("grp", "chol")))
    return jax.shard_map(body, mesh=mesh, in_specs=in_specs, out_specs=out_specs, check_vma=False)
```

```python
import functools

import jax
import jax.numpy as jnp
from jax import lax
from jax.experimental import pallas as pl
from jax.experimental.pallas import tpu as pltpu
from jax.sharding import PartitionSpec as P

LANES = 128
CORES = 2
VMEM_LIMIT = 32 * 1024 * 1024
WIDE = ((16, 8),)
NARROW = ((8, 8), (8, 0))
BATCH = 4
VMEM = pl.BlockSpec(memory_space=pltpu.VMEM)
SMEM = pl.BlockSpec(memory_space=pltpu.SMEM)
PARAMS = pltpu.CompilerParams(vmem_limit_bytes=VMEM_LIMIT)
SMALL = pl.CostEstimate(flops=0, bytes_accessed=0, transcendentals=0)
NT = (((1,), (1,)), ((), ()))
NN = (((1,), (0,)), ((), ()))


def prepare_kernel(screen_ref, chol_ref, block_ref, turned_ref):
    _, listed, vectors, occupied, width = chol_ref.shape
    for m in range(listed):
        keep = jnp.full((1, width), screen_ref[0, m].astype(jnp.float32)).astype(chol_ref.dtype)
        tile = chol_ref[0, m].reshape(vectors * occupied, width) * keep
        block_ref[:, m * width:(m + 1) * width] = tile
        turned_ref[m * width:(m + 1) * width, :] = tile.T


def prepare_block(screen, chol_tiles):
    _, listed, vectors, occupied, width = chol_tiles.shape
    rows, depth = vectors * occupied, listed * width
    return pl.pallas_call(
        prepare_kernel,
        in_specs=[SMEM, VMEM],
        out_specs=[VMEM, VMEM],
        out_shape=[
            jax.ShapeDtypeStruct((rows, depth), chol_tiles.dtype),
            jax.ShapeDtypeStruct((depth, rows), chol_tiles.dtype),
        ],
        compiler_params=PARAMS,
        cost_estimate=SMALL,
        name="prepare_block",
    )(screen, chol_tiles)


def pick_kernel(list_ref, theta_ref, *out_refs):
    listed = list_ref.shape[0]
    width = out_refs[0].shape[2] // listed
    me = lax.axis_index("chol")
    for offset, out_ref in enumerate(out_refs):
        device = me ^ (offset * CORES)
        for b, group in enumerate((device, device ^ 1)):
            for m in range(listed):
                start = pl.multiple_of(list_ref[m, group] * width, width)
                out_ref[b, :, m * width:(m + 1) * width] = theta_ref[0, :, pl.ds(start, width)]


def pick_tiles(listing, theta, depth, count):
    piece = jax.ShapeDtypeStruct((CORES, theta.shape[1], depth), theta.dtype)
    return pl.pallas_call(
        pick_kernel,
        in_specs=[SMEM, VMEM],
        out_specs=[VMEM] * count,
        out_shape=[piece] * count,
        compiler_params=PARAMS,
        cost_estimate=SMALL,
        name="pick_tiles",
    )(listing, theta)


def fold_rows(blocks, sub):
    high = sub < 4
    pairs = []
    for i in range(4):
        a, b = blocks[i], blocks[i + 4]
        pairs.append(jnp.where(high, a, b) + pltpu.roll(jnp.where(high, b, a), 4, 0))
    for shift in (2, 1):
        first = sub % (2 * shift) < shift
        half = len(pairs) // 2
        pairs = [
            jnp.where(
                first,
                pairs[i] + pltpu.roll(pairs[i], 8 - shift, 0),
                pairs[i + half] + pltpu.roll(pairs[i + half], shift, 0),
            )
            for i in range(half)
        ]
    return pairs[0]


def batch_terms(block_ref, turned_ref, theta, cross, store_rows, chunks, vectors, occupied):
    columns = theta.shape[0]
    tiles = columns // LANES

    low = lax.broadcasted_iota(jnp.int32, (occupied, LANES), 1) < occupied
    sub8 = lax.broadcasted_iota(jnp.int32, (8, LANES), 0)
    lane8 = lax.broadcasted_iota(jnp.int32, (8, LANES), 1)
    strip = (lane8 % occupied) // 8
    on_diag = lane8 % 8 == sub8

    def diagonal(block):
        merged = block[:8]
        for r in range(1, occupied // 8):
            merged = jnp.where(strip == r, block[8 * r:8 * r + 8], merged)
        return jnp.where(on_diag, merged, 0.0)

    k0 = 0
    while k0 < vectors:
        for size, by_matmul in chunks:
            span = slice(k0 * occupied, (k0 + size) * occupied)
            inner_mat = lax.dot_general(block_ref[span, :], theta, NT, preferred_element_type=jnp.float32)
            if by_matmul:
                turned = slice(k0 * occupied, (k0 + by_matmul) * occupied)
                flipped = lax.dot_general(theta, turned_ref[:, turned], NN, preferred_element_type=jnp.float32)
            for k8 in range(0, size, 8):
                for t in range(tiles):
                    c0 = t * LANES
                    diagonals = []
                    for k in range(k8, k8 + 8, 2):
                        r0 = k * occupied
                        top = inner_mat[r0:r0 + occupied, c0:c0 + LANES]
                        bottom = inner_mat[r0 + occupied:r0 + 2 * occupied, c0:c0 + LANES]
                        if k < by_matmul:
                            other = flipped[c0:c0 + LANES, r0:r0 + LANES]
                        else:
                            other = inner_mat[r0:r0 + LANES, c0:c0 + LANES].T
                        f_top, f_bottom = other[:occupied], other[occupied:]
                        swapped = pltpu.roll(jnp.where(low, f_bottom, f_top), occupied, 1)
                        product = jnp.where(low, top, bottom) * jnp.where(low, f_top, f_bottom)
                        product = product + jnp.where(low, bottom, top) * swapped
                        cross[t] = cross[t] + jnp.sum(product.reshape(occupied // 8, 8, LANES), axis=0)
                        diagonals.append(diagonal(top))
                        diagonals.append(diagonal(bottom))
                    store_rows(k0 + k8, t, fold_rows(diagonals, sub8))
            k0 += size


def terms_kernel(*refs, first, count, picked, chunks, vectors, batch, carried):
    if not picked:
        list_ref, refs = refs[0], refs[1:]
    block_refs, theta_refs, rest = refs[:4], refs[4:4 + count], refs[4 + count:]
    out_ref, picked_ref, rows_ref = rest[-3:]
    occupied = block_refs[0].shape[0] // vectors
    depth = block_refs[0].shape[1]
    used = CORES * vectors
    columns = batch * occupied
    tiles = columns // LANES
    me = lax.axis_index("chol")
    core = lax.rem(me, CORES)
    chip = me // CORES

    for b, group in enumerate((me, me ^ 1)):
        if picked:
            for i, ref in enumerate(theta_refs):
                picked_ref[b, i * occupied:(i + 1) * occupied, :] = ref[b]
        else:
            listed = list_ref.shape[0]
            width = depth // listed
            for m in range(listed):
                start = pl.multiple_of(list_ref[m, group] * width, width)
                for i, ref in enumerate(theta_refs):
                    picked_ref[b, i * occupied:(i + 1) * occupied, m * width:(m + 1) * width] = (
                        ref[0, :, pl.ds(start, width)]
                    )

    if carried:
        out_ref[...] = rest[0][...]
    else:
        out_ref[...] = jnp.zeros(out_ref.shape, out_ref.dtype)

    def one_batch(index):
        start = index * occupied
        rows = pl.ds(start if isinstance(index, int) else pl.multiple_of(start, columns), columns)
        cross = [jnp.zeros((8, LANES), jnp.float32) for _ in range(tiles)]
        for b in range(CORES):
            place = (core ^ b) * vectors

            def store_rows(k, t, value, place=place):
                rows_ref[pl.ds(pl.multiple_of(place + k, 8), 8), t * LANES:(t + 1) * LANES] = value

            batch_terms(
                block_refs[2 * b], block_refs[2 * b + 1], picked_ref[b, rows, :], cross, store_rows, chunks,
                vectors, occupied,
            )
        for t in range(tiles):
            rows_ref[used:used + 8, t * LANES:(t + 1) * LANES] = cross[t]
        values = rows_ref[...]
        parts = []
        for _ in range(3):
            part = values.astype(jnp.bfloat16)
            parts.append(part)
            values = values - part.astype(jnp.float32)
        seg_row = lax.broadcasted_iota(jnp.int32, (8, columns), 0)
        seg_col = lax.broadcasted_iota(jnp.int32, (8, columns), 1)
        segment = jnp.where(seg_col // occupied == seg_row, 1.0, 0.0).astype(jnp.bfloat16)
        sums = sum(
            lax.dot_general(segment, part, NT, preferred_element_type=jnp.float32) for part in parts
        )
        for i in range(batch):
            owner = chip ^ (first + index + i)
            out_ref[pl.ds(owner, 1), 0, :used + 8] = sums[i:i + 1]

    if count == batch:
        one_batch(0)
    else:
        @pl.loop(0, count // batch)
        def _(step):
            one_batch(step * batch)


def chip_terms(listing, blocks, thetas, carried, first, chunks, vectors, chips, out_width):
    count = len(thetas)
    batch = min(count, BATCH)
    rows, depth = blocks[0].shape
    occupied = rows // vectors
    operands = [*blocks, *thetas] + ([] if carried is None else [carried])
    in_specs = [VMEM] * len(operands)
    if listing is not None:
        operands, in_specs = [listing, *operands], [SMEM, *in_specs]
    return pl.pallas_call(
        functools.partial(
            terms_kernel, first=first, count=count, picked=listing is None, chunks=chunks, vectors=vectors, batch=batch,
            carried=carried is not None,
        ),
        in_specs=in_specs,
        out_specs=VMEM,
        out_shape=jax.ShapeDtypeStruct((chips, 1, out_width), jnp.float32),
        scratch_shapes=[
            pltpu.VMEM((CORES, count * occupied, depth), thetas[0].dtype),
            pltpu.VMEM((CORES * vectors + 8, batch * occupied), jnp.float32),
        ],
        compiler_params=PARAMS,
        cost_estimate=SMALL,
        name="chip_terms",
    )(*operands)


def energy_terms(rows, used):
    lane = lax.broadcasted_iota(jnp.int32, rows.shape, 1)
    return jnp.where(lane < used, rows * rows, jnp.where(lane < used + 8, -rows, 0.0))


def finish_kernel(rows_ref, bias_ref, energy_ref, bias_buf, energy_buf, sems, *, used, scale):
    chips, _, width = rows_ref.shape
    fit = LANES // used if width == LANES else 0
    lane = lax.broadcasted_iota(jnp.int32, (1, width), 1)
    if fit and chips % fit == 0:
        for d in range(0, chips, fit):
            packed = rows_ref[d]
            for i in range(1, fit):
                packed = jnp.where(lane < i * used, packed, pltpu.roll(rows_ref[d + i], i * used, 1))
            bias_buf[:, d * used:(d + fit) * used] = packed
    else:
        for d in range(chips):
            bias_buf[:, d * used:(d + 1) * used] = rows_ref[d, :, :used]
    bias_copy = pltpu.make_async_copy(bias_buf, bias_ref, sems.at[0])
    bias_copy.start()
    total = energy_terms(rows_ref[0], used)
    for d in range(1, chips):
        total = total + energy_terms(rows_ref[d], used)
    energy_buf[...] = jnp.sum(total, axis=1, keepdims=True) * scale
    energy_copy = pltpu.make_async_copy(energy_buf, energy_ref, sems.at[1])
    energy_copy.start()
    bias_copy.wait()
    energy_copy.wait()


def finish(rows, used, scale):
    chips = rows.shape[0]
    shapes = [(1, chips * used), (1, 1)]
    force_bias, energy = pl.pallas_call(
        functools.partial(finish_kernel, used=used, scale=scale),
        in_specs=[VMEM],
        out_specs=[pl.BlockSpec(memory_space=pl.ANY)] * 2,
        out_shape=[jax.ShapeDtypeStruct(s, jnp.float32) for s in shapes],
        scratch_shapes=[pltpu.VMEM(s, jnp.float32) for s in shapes] + [pltpu.SemaphoreType.DMA((2,))],
        name="finish",
    )(rows)
    return force_bias, energy.reshape(1)


def body(theta, chol_tiles, screen, tile_list):
    groups = lax.axis_size("chol")
    chips = groups // CORES
    half = chips // 2
    _, occupied, _ = theta.shape
    vectors = chol_tiles.shape[2]
    used = CORES * vectors
    out_width = LANES * ((used + 8 + LANES - 1) // LANES)
    listing = tile_list.T

    def to_chip(x, offset):
        return lax.ppermute(x, "chol", [(i, i ^ (offset * CORES)) for i in range(groups)])

    def to_core(x):
        return lax.ppermute(x, "chol", [(i, i ^ 1) for i in range(groups)])

    far = to_chip(theta, half)
    near = [theta] + [to_chip(theta, offset) for offset in range(1, half)]
    own, own_turned = prepare_block(screen, chol_tiles)
    near[1], near[2], own, far = lax.optimization_barrier((near[1], near[2], own, far))
    pieces = pick_tiles(listing, far, own.shape[1], half)
    beyond = [pieces[0]] + [to_chip(pieces[offset], offset) for offset in range(1, half)]
    other_chol, late_screen, near[-1] = lax.optimization_barrier((to_core(chol_tiles), screen, near[-1]))
    other, other_turned = prepare_block(to_core(late_screen), other_chol)
    blocks = [own, own_turned, other, other_turned]

    rows = chip_terms(listing, blocks, near, None, 0, WIDE, vectors, chips, out_width)
    rows = chip_terms(None, blocks, beyond, rows, half, NARROW, vectors, chips, out_width)
    same_core = [list(range(core, groups, CORES)) for core in range(CORES)]
    back = lax.all_to_all(rows, "chol", split_axis=0, concat_axis=0, tiled=True, axis_index_groups=same_core)
    return finish(back, used, 1.0 / (2.0 * occupied * occupied))


def solution(mesh):
    in_specs = (
        P(("grp", "chol"), None, None),
        P("chol", None, None, None, None),
        P("chol", None),
        P(),
    )
    out_specs = (P(("grp", "chol"), None), P(("grp", "chol")))
    return jax.shard_map(body, mesh=mesh, in_specs=in_specs, out_specs=out_specs, check_vma=False)
```

```python
import functools

import jax
import jax.numpy as jnp
from jax import lax
from jax.experimental import pallas as pl
from jax.experimental.pallas import tpu as pltpu
from jax.sharding import PartitionSpec as P

LANES = 128
CORES = 2
VMEM_LIMIT = 32 * 1024 * 1024
NEAR = ((8, 4),)
BEYOND = ((8, 8), (8, 0))
BATCH = 4
VMEM = pl.BlockSpec(memory_space=pltpu.VMEM)
SMEM = pl.BlockSpec(memory_space=pltpu.SMEM)
PARAMS = pltpu.CompilerParams(vmem_limit_bytes=VMEM_LIMIT)
SMALL = pl.CostEstimate(flops=0, bytes_accessed=0, transcendentals=0)
NT = (((1,), (1,)), ((), ()))
NN = (((1,), (0,)), ((), ()))


def prepare_kernel(chol_ref, block_ref, turned_ref):
    _, listed, vectors, occupied, width = chol_ref.shape
    for m in range(listed):
        tile = chol_ref[0, m].reshape(vectors * occupied, width)
        block_ref[:, m * width:(m + 1) * width] = tile
        turned_ref[m * width:(m + 1) * width, :] = tile.T


def prepare_block(chol_tiles):
    _, listed, vectors, occupied, width = chol_tiles.shape
    rows, depth = vectors * occupied, listed * width
    return pl.pallas_call(
        prepare_kernel,
        in_specs=[VMEM],
        out_specs=[VMEM, VMEM],
        out_shape=[
            jax.ShapeDtypeStruct((rows, depth), chol_tiles.dtype),
            jax.ShapeDtypeStruct((depth, rows), chol_tiles.dtype),
        ],
        compiler_params=PARAMS,
        cost_estimate=SMALL,
        name="prepare_block",
    )(chol_tiles)


def pick_kernel(list_ref, theta_ref, *out_refs):
    listed = list_ref.shape[0]
    width = out_refs[0].shape[2] // listed
    me = lax.axis_index("chol")
    for offset, out_ref in enumerate(out_refs):
        device = me ^ (offset * CORES)
        for b, group in enumerate((device, device ^ 1)):
            for m in range(listed):
                start = pl.multiple_of(list_ref[m, group] * width, width)
                out_ref[b, :, m * width:(m + 1) * width] = theta_ref[0, :, pl.ds(start, width)]


def pick_tiles(listing, theta, depth, count):
    piece = jax.ShapeDtypeStruct((CORES, theta.shape[1], depth), theta.dtype)
    return pl.pallas_call(
        pick_kernel,
        in_specs=[SMEM, VMEM],
        out_specs=[VMEM] * count,
        out_shape=[piece] * count,
        compiler_params=PARAMS,
        cost_estimate=SMALL,
        name="pick_tiles",
    )(listing, theta)


def fold_rows(blocks, sub):
    high = sub < 4
    pairs = []
    for i in range(4):
        a, b = blocks[i], blocks[i + 4]
        pairs.append(jnp.where(high, a, b) + pltpu.roll(jnp.where(high, b, a), 4, 0))
    for shift in (2, 1):
        first = sub % (2 * shift) < shift
        half = len(pairs) // 2
        pairs = [
            jnp.where(
                first,
                pairs[i] + pltpu.roll(pairs[i], 8 - shift, 0),
                pairs[i + half] + pltpu.roll(pairs[i + half], shift, 0),
            )
            for i in range(half)
        ]
    return pairs[0]


def chunk_products(block_ref, turned_ref, theta, occupied, k0, size, by_matmul):
    span = slice(k0 * occupied, (k0 + size) * occupied)
    inner_mat = lax.dot_general(block_ref[span, :], theta, NT, preferred_element_type=jnp.float32)
    if not by_matmul:
        return inner_mat, None
    turned = slice(k0 * occupied, (k0 + by_matmul) * occupied)
    return inner_mat, lax.dot_general(theta, turned_ref[:, turned], NN, preferred_element_type=jnp.float32)


def chunk_terms(inner_mat, flipped, cross, store_rows, occupied, k0, size, by_matmul):
    tiles = inner_mat.shape[1] // LANES

    low = lax.broadcasted_iota(jnp.int32, (occupied, LANES), 1) < occupied
    sub8 = lax.broadcasted_iota(jnp.int32, (8, LANES), 0)
    lane8 = lax.broadcasted_iota(jnp.int32, (8, LANES), 1)
    strip = (lane8 % occupied) // 8
    on_diag = lane8 % 8 == sub8

    def diagonal(block):
        merged = block[:8]
        for r in range(1, occupied // 8):
            merged = jnp.where(strip == r, block[8 * r:8 * r + 8], merged)
        return jnp.where(on_diag, merged, 0.0)

    for k8 in range(0, size, 8):
        for t in range(tiles):
            c0 = t * LANES
            diagonals = []
            for k in range(k8, k8 + 8, 2):
                r0 = k * occupied
                top = inner_mat[r0:r0 + occupied, c0:c0 + LANES]
                bottom = inner_mat[r0 + occupied:r0 + 2 * occupied, c0:c0 + LANES]
                if k < by_matmul:
                    other = flipped[c0:c0 + LANES, r0:r0 + LANES]
                else:
                    other = inner_mat[r0:r0 + LANES, c0:c0 + LANES].T
                f_top, f_bottom = other[:occupied], other[occupied:]
                swapped = pltpu.roll(jnp.where(low, f_bottom, f_top), occupied, 1)
                product = jnp.where(low, top, bottom) * jnp.where(low, f_top, f_bottom)
                product = product + jnp.where(low, bottom, top) * swapped
                cross[t] = cross[t] + jnp.sum(product.reshape(occupied // 8, 8, LANES), axis=0)
                diagonals.append(diagonal(top))
                diagonals.append(diagonal(bottom))
            store_rows(k0 + k8, t, fold_rows(diagonals, sub8))


def mask_kernel_rows(screen_refs, listed, width):
    return [
        jnp.concatenate(
            [jnp.full((1, width), ref[0, m].astype(jnp.float32)) for m in range(listed)], axis=1
        )
        for ref in screen_refs
    ]


def terms_kernel(*refs, first, count, picked, chunks, vectors, batch):
    if picked:
        mask_ref, carried_ref, refs = refs[0], refs[1], refs[2:]
    else:
        list_ref, screen_refs, refs = refs[0], refs[1:3], refs[3:]
    block_refs, theta_refs, rest = refs[:4], refs[4:4 + count], refs[4 + count:]
    out_ref, picked_ref, rows_ref = rest[0], rest[-2], rest[-1]
    occupied = block_refs[0].shape[0] // vectors
    depth = block_refs[0].shape[1]
    used = CORES * vectors
    columns = batch * occupied
    tiles = columns // LANES
    me = lax.axis_index("chol")
    core = lax.rem(me, CORES)
    chip = me // CORES

    if picked:
        masks = [mask_ref[b:b + 1, :] for b in range(CORES)]
        out_ref[...] = carried_ref[...]
    else:
        listed = list_ref.shape[0]
        width = depth // listed
        masks = mask_kernel_rows(screen_refs, listed, width)
        mask_ref = rest[1]
        for b in range(CORES):
            mask_ref[b:b + 1, :] = masks[b]
        out_ref[...] = jnp.zeros(out_ref.shape, out_ref.dtype)
    for b, group in enumerate((me, me ^ 1)):
        mask = masks[b].astype(picked_ref.dtype)
        if picked:
            for i, ref in enumerate(theta_refs):
                picked_ref[b, i * occupied:(i + 1) * occupied, :] = ref[b] * mask
        else:
            for m in range(listed):
                start = pl.multiple_of(list_ref[m, group] * width, width)
                tile_mask = mask[:, m * width:(m + 1) * width]
                for i, ref in enumerate(theta_refs):
                    picked_ref[b, i * occupied:(i + 1) * occupied, m * width:(m + 1) * width] = (
                        ref[0, :, pl.ds(start, width)] * tile_mask
                    )

    def one_batch(index):
        start = index * occupied
        rows = pl.ds(start if isinstance(index, int) else pl.multiple_of(start, columns), columns)
        cross = [jnp.zeros((8, LANES), jnp.float32) for _ in range(tiles)]
        tasks = []
        for b in range(CORES):
            theta, k0 = picked_ref[b, rows, :], 0
            while k0 < vectors:
                for size, by_matmul in chunks:
                    tasks.append((b, theta, k0, size, by_matmul))
                    k0 += size

        def products(task):
            b, theta, k0, size, by_matmul = task
            return chunk_products(block_refs[2 * b], block_refs[2 * b + 1], theta, occupied, k0, size, by_matmul)

        ahead = products(tasks[0])
        for i, (b, _, k0, size, by_matmul) in enumerate(tasks):
            now, ahead = ahead, products(tasks[i + 1]) if i + 1 < len(tasks) else None
            place = (core ^ b) * vectors

            def store_rows(k, t, value, place=place):
                rows_ref[pl.ds(pl.multiple_of(place + k, 8), 8), t * LANES:(t + 1) * LANES] = value

            chunk_terms(*now, cross, store_rows, occupied, k0, size, by_matmul)
        for t in range(tiles):
            rows_ref[used:used + 8, t * LANES:(t + 1) * LANES] = cross[t]
        values = rows_ref[...]
        parts = []
        for _ in range(3):
            part = values.astype(jnp.bfloat16)
            parts.append(part)
            values = values - part.astype(jnp.float32)
        seg_row = lax.broadcasted_iota(jnp.int32, (8, columns), 0)
        seg_col = lax.broadcasted_iota(jnp.int32, (8, columns), 1)
        segment = jnp.where(seg_col // occupied == seg_row, 1.0, 0.0).astype(jnp.bfloat16)
        sums = sum(
            lax.dot_general(segment, part, NT, preferred_element_type=jnp.float32) for part in parts
        )
        for i in range(batch):
            owner = chip ^ (first + index + i)
            out_ref[pl.ds(owner, 1), 0, :used + 8] = sums[i:i + 1]

    if count == batch:
        one_batch(0)
    else:
        @pl.loop(0, count // batch)
        def _(step):
            one_batch(step * batch)


def chip_terms(scalars, so_far, blocks, thetas, first, chunks, vectors, chips, out_width):
    count = len(thetas)
    batch = min(count, BATCH)
    rows, depth = blocks[0].shape
    occupied = rows // vectors
    vector_operands = [*so_far, *blocks, *thetas]
    out_shape = [jax.ShapeDtypeStruct((chips, 1, out_width), jnp.float32)]
    if scalars:
        out_shape.append(jax.ShapeDtypeStruct((CORES, depth), jnp.float32))
    return pl.pallas_call(
        functools.partial(
            terms_kernel, first=first, count=count, picked=not scalars, chunks=chunks, vectors=vectors, batch=batch
        ),
        in_specs=[SMEM] * len(scalars) + [VMEM] * len(vector_operands),
        out_specs=[VMEM] * len(out_shape),
        out_shape=out_shape,
        scratch_shapes=[
            pltpu.VMEM((CORES, count * occupied, depth), thetas[0].dtype),
            pltpu.VMEM((CORES * vectors + 8, batch * occupied), jnp.float32),
        ],
        compiler_params=PARAMS,
        cost_estimate=SMALL,
        name="chip_terms",
    )(*scalars, *vector_operands)


def energy_terms(rows, used):
    lane = lax.broadcasted_iota(jnp.int32, rows.shape, 1)
    return jnp.where(lane < used, rows * rows, jnp.where(lane < used + 8, -rows, 0.0))


def finish_kernel(rows_ref, bias_ref, energy_ref, bias_buf, energy_buf, sems, *, used, scale):
    chips, _, width = rows_ref.shape
    fit = LANES // used if width == LANES else 0
    lane = lax.broadcasted_iota(jnp.int32, (1, width), 1)
    if fit and chips % fit == 0:
        for d in range(0, chips, fit):
            packed = rows_ref[d]
            for i in range(1, fit):
                packed = jnp.where(lane < i * used, packed, pltpu.roll(rows_ref[d + i], i * used, 1))
            bias_buf[:, d * used:(d + fit) * used] = packed
    else:
        for d in range(chips):
            bias_buf[:, d * used:(d + 1) * used] = rows_ref[d, :, :used]
    bias_copy = pltpu.make_async_copy(bias_buf, bias_ref, sems.at[0])
    bias_copy.start()
    total = energy_terms(rows_ref[0], used)
    for d in range(1, chips):
        total = total + energy_terms(rows_ref[d], used)
    energy_buf[...] = jnp.sum(total, axis=1, keepdims=True) * scale
    energy_copy = pltpu.make_async_copy(energy_buf, energy_ref, sems.at[1])
    energy_copy.start()
    bias_copy.wait()
    energy_copy.wait()


def finish(rows, used, scale):
    chips = rows.shape[0]
    shapes = [(1, chips * used), (1, 1)]
    force_bias, energy = pl.pallas_call(
        functools.partial(finish_kernel, used=used, scale=scale),
        in_specs=[VMEM],
        out_specs=[pl.BlockSpec(memory_space=pl.ANY)] * 2,
        out_shape=[jax.ShapeDtypeStruct(s, jnp.float32) for s in shapes],
        scratch_shapes=[pltpu.VMEM(s, jnp.float32) for s in shapes] + [pltpu.SemaphoreType.DMA((2,))],
        name="finish",
    )(rows)
    return force_bias, energy.reshape(1)


def body(theta, chol_tiles, screen, tile_list):
    groups = lax.axis_size("chol")
    chips = groups // CORES
    half = chips // 2
    _, occupied, _ = theta.shape
    vectors = chol_tiles.shape[2]
    used = CORES * vectors
    out_width = LANES * ((used + 8 + LANES - 1) // LANES)
    listing = tile_list.T

    def to_chip(x, offset):
        return lax.ppermute(x, "chol", [(i, i ^ (offset * CORES)) for i in range(groups)])

    def to_core(x):
        return lax.ppermute(x, "chol", [(i, i ^ 1) for i in range(groups)])

    far = to_chip(theta, half)
    near = [theta] + [to_chip(theta, offset) for offset in range(1, half)]
    own, own_turned = prepare_block(chol_tiles)
    near[2], far, near[1], own = lax.optimization_barrier((near[2], far, near[1], own))
    pieces = pick_tiles(listing, far, own.shape[1], half)
    beyond = [pieces[0]] + [to_chip(pieces[offset], offset) for offset in range(1, half)]
    other_chol, late_screen, near[-1] = lax.optimization_barrier((to_core(chol_tiles), screen, near[-1]))
    other, other_turned = prepare_block(other_chol)
    blocks = [own, own_turned, other, other_turned]

    scalars = [listing, screen, to_core(late_screen)]
    rows, masks = chip_terms(scalars, [], blocks, near, 0, NEAR, vectors, chips, out_width)
    rows, = chip_terms([], [masks, rows], blocks, beyond, half, BEYOND, vectors, chips, out_width)
    same_core = [list(range(core, groups, CORES)) for core in range(CORES)]
    back = lax.all_to_all(rows, "chol", split_axis=0, concat_axis=0, tiled=True, axis_index_groups=same_core)
    return finish(back, used, 1.0 / (2.0 * occupied * occupied))


def solution(mesh):
    in_specs = (
        P(("grp", "chol"), None, None),
        P("chol", None, None, None, None),
        P("chol", None),
        P(),
    )
    out_specs = (P(("grp", "chol"), None), P(("grp", "chol")))
    return jax.shard_map(body, mesh=mesh, in_specs=in_specs, out_specs=out_specs, check_vma=False)
```

```python
import functools

import jax
import jax.numpy as jnp
from jax import lax
from jax.experimental import pallas as pl
from jax.experimental.pallas import tpu as pltpu
from jax.sharding import PartitionSpec as P

LANES = 128
CORES = 2
VMEM_LIMIT = 32 * 1024 * 1024
NEAR = ((8, 4),)
BEYOND = ((8, 0),)
BATCH = 4
VMEM = pl.BlockSpec(memory_space=pltpu.VMEM)
SMEM = pl.BlockSpec(memory_space=pltpu.SMEM)
PARAMS = pltpu.CompilerParams(vmem_limit_bytes=VMEM_LIMIT)
SMALL = pl.CostEstimate(flops=0, bytes_accessed=0, transcendentals=0)
NT = (((1,), (1,)), ((), ()))
NN = (((1,), (0,)), ((), ()))


def prepare_kernel(chol_ref, block_ref, turned_ref):
    _, listed, vectors, occupied, width = chol_ref.shape
    for m in range(listed):
        tile = chol_ref[0, m].reshape(vectors * occupied, width)
        block_ref[:, m * width:(m + 1) * width] = tile
        turned_ref[m * width:(m + 1) * width, :] = tile.T


def prepare_block(chol_tiles):
    _, listed, vectors, occupied, width = chol_tiles.shape
    rows, depth = vectors * occupied, listed * width
    return pl.pallas_call(
        prepare_kernel,
        in_specs=[VMEM],
        out_specs=[VMEM, VMEM],
        out_shape=[
            jax.ShapeDtypeStruct((rows, depth), chol_tiles.dtype),
            jax.ShapeDtypeStruct((depth, rows), chol_tiles.dtype),
        ],
        compiler_params=PARAMS,
        cost_estimate=SMALL,
        name="prepare_block",
    )(chol_tiles)


def pick_kernel(list_ref, theta_ref, *out_refs):
    listed = list_ref.shape[0]
    width = out_refs[0].shape[2] // listed
    me = lax.axis_index("chol")
    for offset, out_ref in enumerate(out_refs):
        device = me ^ (offset * CORES)
        for b, group in enumerate((device, device ^ 1)):
            for m in range(listed):
                start = pl.multiple_of(list_ref[m, group] * width, width)
                out_ref[b, :, m * width:(m + 1) * width] = theta_ref[0, :, pl.ds(start, width)]


def pick_tiles(listing, theta, depth, count):
    piece = jax.ShapeDtypeStruct((CORES, theta.shape[1], depth), theta.dtype)
    return pl.pallas_call(
        pick_kernel,
        in_specs=[SMEM, VMEM],
        out_specs=[VMEM] * count,
        out_shape=[piece] * count,
        compiler_params=PARAMS,
        cost_estimate=SMALL,
        name="pick_tiles",
    )(listing, theta)


def fold_rows(blocks, sub):
    high = sub < 4
    pairs = []
    for i in range(4):
        a, b = blocks[i], blocks[i + 4]
        pairs.append(jnp.where(high, a, b) + pltpu.roll(jnp.where(high, b, a), 4, 0))
    for shift in (2, 1):
        first = sub % (2 * shift) < shift
        half = len(pairs) // 2
        pairs = [
            jnp.where(
                first,
                pairs[i] + pltpu.roll(pairs[i], 8 - shift, 0),
                pairs[i + half] + pltpu.roll(pairs[i + half], shift, 0),
            )
            for i in range(half)
        ]
    return pairs[0]


def chunk_products(block_ref, turned_ref, theta, occupied, k0, size, by_matmul):
    span = slice(k0 * occupied, (k0 + size) * occupied)
    inner_mat = lax.dot_general(block_ref[span, :], theta, NT, preferred_element_type=jnp.float32)
    if not by_matmul:
        return inner_mat, None
    turned = slice(k0 * occupied, (k0 + by_matmul) * occupied)
    return inner_mat, lax.dot_general(theta, turned_ref[:, turned], NN, preferred_element_type=jnp.float32)


def chunk_terms(inner_mat, flipped, cross, store_rows, occupied, k0, size, by_matmul):
    tiles = inner_mat.shape[1] // LANES

    low = lax.broadcasted_iota(jnp.int32, (occupied, LANES), 1) < occupied
    sub8 = lax.broadcasted_iota(jnp.int32, (8, LANES), 0)
    lane8 = lax.broadcasted_iota(jnp.int32, (8, LANES), 1)
    strip = (lane8 % occupied) // 8
    on_diag = lane8 % 8 == sub8

    def diagonal(block):
        merged = block[:8]
        for r in range(1, occupied // 8):
            merged = jnp.where(strip == r, block[8 * r:8 * r + 8], merged)
        return jnp.where(on_diag, merged, 0.0)

    for k8 in range(0, size, 8):
        for t in range(tiles):
            c0 = t * LANES
            diagonals = []
            for k in range(k8, k8 + 8, 2):
                r0 = k * occupied
                top = inner_mat[r0:r0 + occupied, c0:c0 + LANES]
                bottom = inner_mat[r0 + occupied:r0 + 2 * occupied, c0:c0 + LANES]
                if k < by_matmul:
                    other = flipped[c0:c0 + LANES, r0:r0 + LANES]
                else:
                    other = inner_mat[r0:r0 + LANES, c0:c0 + LANES].T
                f_top, f_bottom = other[:occupied], other[occupied:]
                swapped = pltpu.roll(jnp.where(low, f_bottom, f_top), occupied, 1)
                product = jnp.where(low, top, bottom) * jnp.where(low, f_top, f_bottom)
                product = product + jnp.where(low, bottom, top) * swapped
                cross[t] = cross[t] + jnp.sum(product.reshape(occupied // 8, 8, LANES), axis=0)
                diagonals.append(diagonal(top))
                diagonals.append(diagonal(bottom))
            store_rows(k0 + k8, t, fold_rows(diagonals, sub8))


def spread(place, count):
    return jnp.where(place == 1, 1, jnp.where(place == 2, count - 1, place - 1))


def mask_kernel_rows(screen_refs, listed, width):
    return [
        jnp.concatenate(
            [jnp.full((1, width), ref[0, m].astype(jnp.float32)) for m in range(listed)], axis=1
        )
        for ref in screen_refs
    ]


def terms_kernel(*refs, first, count, picked, chunks, vectors, batch):
    if picked:
        mask_ref, carried_ref, refs = refs[0], refs[1], refs[2:]
    else:
        list_ref, screen_refs, refs = refs[0], refs[1:3], refs[3:]
    block_refs, theta_refs, rest = refs[:4], refs[4:4 + count], refs[4 + count:]
    out_ref, picked_ref, rows_ref = rest[0], rest[-2], rest[-1]
    occupied = block_refs[0].shape[0] // vectors
    depth = block_refs[0].shape[1]
    used = CORES * vectors
    columns = batch * occupied
    tiles = columns // LANES
    me = lax.axis_index("chol")
    core = lax.rem(me, CORES)
    chip = me // CORES

    if picked:
        masks = [mask_ref[b:b + 1, :] for b in range(CORES)]
        out_ref[...] = carried_ref[...]
    else:
        listed = list_ref.shape[0]
        width = depth // listed
        masks = mask_kernel_rows(screen_refs, listed, width)
        mask_ref = rest[1]
        for b in range(CORES):
            mask_ref[b:b + 1, :] = masks[b]
        out_ref[...] = jnp.zeros(out_ref.shape, out_ref.dtype)
    for b, group in enumerate((me, me ^ 1)):
        mask = masks[b].astype(picked_ref.dtype)
        if picked:
            for i, ref in enumerate(theta_refs):
                picked_ref[b, i * occupied:(i + 1) * occupied, :] = ref[b] * mask
        else:
            for m in range(listed):
                start = pl.multiple_of(list_ref[m, group] * width, width)
                tile_mask = mask[:, m * width:(m + 1) * width]
                for i, ref in enumerate(theta_refs):
                    picked_ref[b, i * occupied:(i + 1) * occupied, m * width:(m + 1) * width] = (
                        ref[0, :, pl.ds(start, width)] * tile_mask
                    )

    def one_batch(index):
        start = index * occupied
        rows = pl.ds(start if isinstance(index, int) else pl.multiple_of(start, columns), columns)
        cross = [jnp.zeros((8, LANES), jnp.float32) for _ in range(tiles)]
        tasks = []
        for b in range(CORES):
            theta, k0 = picked_ref[b, rows, :], 0
            while k0 < vectors:
                for size, by_matmul in chunks:
                    tasks.append((b, theta, k0, size, by_matmul))
                    k0 += size

        def products(task):
            b, theta, k0, size, by_matmul = task
            return chunk_products(block_refs[2 * b], block_refs[2 * b + 1], theta, occupied, k0, size, by_matmul)

        ahead = products(tasks[0])
        for i, (b, _, k0, size, by_matmul) in enumerate(tasks):
            now, ahead = ahead, products(tasks[i + 1]) if i + 1 < len(tasks) else None
            place = (core ^ b) * vectors

            def store_rows(k, t, value, place=place):
                rows_ref[pl.ds(pl.multiple_of(place + k, 8), 8), t * LANES:(t + 1) * LANES] = value

            chunk_terms(*now, cross, store_rows, occupied, k0, size, by_matmul)
        for t in range(tiles):
            rows_ref[used:used + 8, t * LANES:(t + 1) * LANES] = cross[t]
        values = rows_ref[...]
        parts = []
        for _ in range(3):
            part = values.astype(jnp.bfloat16)
            parts.append(part)
            values = values - part.astype(jnp.float32)
        seg_row = lax.broadcasted_iota(jnp.int32, (8, columns), 0)
        seg_col = lax.broadcasted_iota(jnp.int32, (8, columns), 1)
        segment = jnp.where(seg_col // occupied == seg_row, 1.0, 0.0).astype(jnp.bfloat16)
        sums = sum(
            lax.dot_general(segment, part, NT, preferred_element_type=jnp.float32) for part in parts
        )
        for i in range(batch):
            place = jnp.int32(index + i)
            if picked:
                place = jnp.where(place == 0, 0, spread(place, count))
            owner = chip ^ (first + place)
            out_ref[pl.ds(owner, 1), 0, :used + 8] = sums[i:i + 1]

    if count == batch:
        one_batch(0)
    else:
        @pl.loop(0, count // batch)
        def _(step):
            one_batch(step * batch)


def chip_terms(scalars, so_far, blocks, thetas, first, chunks, vectors, chips, out_width):
    count = len(thetas)
    batch = min(count, BATCH)
    rows, depth = blocks[0].shape
    occupied = rows // vectors
    vector_operands = [*so_far, *blocks, *thetas]
    out_shape = [jax.ShapeDtypeStruct((chips, 1, out_width), jnp.float32)]
    if scalars:
        out_shape.append(jax.ShapeDtypeStruct((CORES, depth), jnp.float32))
    return pl.pallas_call(
        functools.partial(
            terms_kernel, first=first, count=count, picked=not scalars, chunks=chunks, vectors=vectors, batch=batch
        ),
        in_specs=[SMEM] * len(scalars) + [VMEM] * len(vector_operands),
        out_specs=[VMEM] * len(out_shape),
        out_shape=out_shape,
        scratch_shapes=[
            pltpu.VMEM((CORES, count * occupied, depth), thetas[0].dtype),
            pltpu.VMEM((CORES * vectors + 8, batch * occupied), jnp.float32),
        ],
        compiler_params=PARAMS,
        cost_estimate=SMALL,
        name="chip_terms",
    )(*scalars, *vector_operands)


def energy_terms(rows, used):
    lane = lax.broadcasted_iota(jnp.int32, rows.shape, 1)
    return jnp.where(lane < used, rows * rows, jnp.where(lane < used + 8, -rows, 0.0))


def finish_kernel(rows_ref, bias_ref, energy_ref, bias_buf, energy_buf, sems, *, used, scale):
    chips, _, width = rows_ref.shape
    fit = LANES // used if width == LANES else 0
    lane = lax.broadcasted_iota(jnp.int32, (1, width), 1)
    if fit and chips % fit == 0:
        for d in range(0, chips, fit):
            packed = rows_ref[d]
            for i in range(1, fit):
                packed = jnp.where(lane < i * used, packed, pltpu.roll(rows_ref[d + i], i * used, 1))
            bias_buf[:, d * used:(d + fit) * used] = packed
    else:
        for d in range(chips):
            bias_buf[:, d * used:(d + 1) * used] = rows_ref[d, :, :used]
    bias_copy = pltpu.make_async_copy(bias_buf, bias_ref, sems.at[0])
    bias_copy.start()
    total = energy_terms(rows_ref[0], used)
    for d in range(1, chips):
        total = total + energy_terms(rows_ref[d], used)
    energy_buf[...] = jnp.sum(total, axis=1, keepdims=True) * scale
    energy_copy = pltpu.make_async_copy(energy_buf, energy_ref, sems.at[1])
    energy_copy.start()
    bias_copy.wait()
    energy_copy.wait()


def finish(rows, used, scale):
    chips = rows.shape[0]
    shapes = [(1, chips * used), (1, 1)]
    force_bias, energy = pl.pallas_call(
        functools.partial(finish_kernel, used=used, scale=scale),
        in_specs=[VMEM],
        out_specs=[pl.BlockSpec(memory_space=pl.ANY)] * 2,
        out_shape=[jax.ShapeDtypeStruct(s, jnp.float32) for s in shapes],
        scratch_shapes=[pltpu.VMEM(s, jnp.float32) for s in shapes] + [pltpu.SemaphoreType.DMA((2,))],
        name="finish",
    )(rows)
    return force_bias, energy.reshape(1)


def body(theta, chol_tiles, screen, tile_list):
    groups = lax.axis_size("chol")
    chips = groups // CORES
    half = chips // 2
    _, occupied, _ = theta.shape
    vectors = chol_tiles.shape[2]
    used = CORES * vectors
    out_width = LANES * ((used + 8 + LANES - 1) // LANES)
    listing = tile_list.T

    def to_chip(x, offset):
        return lax.ppermute(x, "chol", [(i, i ^ (offset * CORES)) for i in range(groups)])

    def to_core(x):
        return lax.ppermute(x, "chol", [(i, i ^ 1) for i in range(groups)])

    far = to_chip(theta, half)
    near = [theta] + [to_chip(theta, offset) for offset in range(1, half)]
    own, own_turned = prepare_block(chol_tiles)
    near[2], far, near[1], own = lax.optimization_barrier((near[2], far, near[1], own))
    pieces = pick_tiles(listing, far, own.shape[1], half)
    beyond = [pieces[0]] + [to_chip(pieces[offset], offset) for offset in range(1, half)]
    other_chol, late_screen, near[-1] = lax.optimization_barrier((to_core(chol_tiles), screen, near[-1]))
    other, other_turned = prepare_block(other_chol)
    blocks = [own, own_turned, other, other_turned]

    scalars = [listing, screen, to_core(late_screen)]
    rows, masks = chip_terms(scalars, [], blocks, near, 0, NEAR, vectors, chips, out_width)
    beyond = beyond[:2] + beyond[:1:-1][:1] + beyond[2:-1]
    rows, = chip_terms([], [masks, rows], blocks, beyond, half, BEYOND, vectors, chips, out_width)
    same_core = [list(range(core, groups, CORES)) for core in range(CORES)]
    back = lax.all_to_all(rows, "chol", split_axis=0, concat_axis=0, tiled=True, axis_index_groups=same_core)
    return finish(back, used, 1.0 / (2.0 * occupied * occupied))


def solution(mesh):
    in_specs = (
        P(("grp", "chol"), None, None),
        P("chol", None, None, None, None),
        P("chol", None),
        P(),
    )
    out_specs = (P(("grp", "chol"), None), P(("grp", "chol")))
    return jax.shard_map(body, mesh=mesh, in_specs=in_specs, out_specs=out_specs, check_vma=False)
```

```python
import functools

import jax
import jax.numpy as jnp
from jax import lax
from jax.experimental import pallas as pl
from jax.experimental.pallas import tpu as pltpu
from jax.sharding import PartitionSpec as P

LANES = 128
CORES = 2
VMEM_LIMIT = 32 * 1024 * 1024
NEAR = ((8, 4),)
BEYOND = ((8, 8), (8, 0))
BATCH = 4
VMEM = pl.BlockSpec(memory_space=pltpu.VMEM)
SMEM = pl.BlockSpec(memory_space=pltpu.SMEM)
PARAMS = pltpu.CompilerParams(vmem_limit_bytes=VMEM_LIMIT)
SMALL = pl.CostEstimate(flops=0, bytes_accessed=0, transcendentals=0)
NT = (((1,), (1,)), ((), ()))
NN = (((1,), (0,)), ((), ()))


def prepare_kernel(chol_ref, block_ref, turned_ref):
    _, listed, vectors, occupied, width = chol_ref.shape
    for m in range(listed):
        tile = chol_ref[0, m].reshape(vectors * occupied, width)
        block_ref[:, m * width:(m + 1) * width] = tile
        turned_ref[m * width:(m + 1) * width, :] = tile.T


def prepare_block(chol_tiles):
    _, listed, vectors, occupied, width = chol_tiles.shape
    rows, depth = vectors * occupied, listed * width
    return pl.pallas_call(
        prepare_kernel,
        in_specs=[VMEM],
        out_specs=[VMEM, VMEM],
        out_shape=[
            jax.ShapeDtypeStruct((rows, depth), chol_tiles.dtype),
            jax.ShapeDtypeStruct((depth, rows), chol_tiles.dtype),
        ],
        compiler_params=PARAMS,
        cost_estimate=SMALL,
        name="prepare_block",
    )(chol_tiles)


def pick_kernel(list_ref, early_ref, late_ref, *out_refs, part):
    listed = list_ref.shape[0]
    width = out_refs[0].shape[2] // listed
    me = lax.axis_index("chol")
    early = lax.rem(me // (CORES * part), 2) == 1
    for offset, out_ref in enumerate(out_refs):
        device = me ^ (offset * CORES)
        for b, group in enumerate((device, device ^ 1)):
            for m in range(listed):
                start = pl.multiple_of(list_ref[m, group] * width, width)
                out_ref[b, :, m * width:(m + 1) * width] = jnp.where(
                    early, early_ref[0, :, pl.ds(start, width)], late_ref[0, :, pl.ds(start, width)]
                )


def pick_tiles(listing, early, late, depth, count, part):
    piece = jax.ShapeDtypeStruct((CORES, early.shape[1], depth), early.dtype)
    return pl.pallas_call(
        functools.partial(pick_kernel, part=part),
        in_specs=[SMEM, VMEM, VMEM],
        out_specs=[VMEM] * count,
        out_shape=[piece] * count,
        compiler_params=PARAMS,
        cost_estimate=SMALL,
        name="pick_tiles",
    )(listing, early, late)


def fold_rows(blocks, sub):
    high = sub < 4
    pairs = []
    for i in range(4):
        a, b = blocks[i], blocks[i + 4]
        pairs.append(jnp.where(high, a, b) + pltpu.roll(jnp.where(high, b, a), 4, 0))
    for shift in (2, 1):
        first = sub % (2 * shift) < shift
        half = len(pairs) // 2
        pairs = [
            jnp.where(
                first,
                pairs[i] + pltpu.roll(pairs[i], 8 - shift, 0),
                pairs[i + half] + pltpu.roll(pairs[i + half], shift, 0),
            )
            for i in range(half)
        ]
    return pairs[0]


def chunk_products(block_ref, turned_ref, theta, occupied, k0, size, by_matmul):
    span = slice(k0 * occupied, (k0 + size) * occupied)
    inner_mat = lax.dot_general(block_ref[span, :], theta, NT, preferred_element_type=jnp.float32)
    if not by_matmul:
        return inner_mat, None
    turned = slice(k0 * occupied, (k0 + by_matmul) * occupied)
    return inner_mat, lax.dot_general(theta, turned_ref[:, turned], NN, preferred_element_type=jnp.float32)


def chunk_terms(inner_mat, flipped, cross, store_rows, occupied, k0, size, by_matmul):
    tiles = inner_mat.shape[1] // LANES

    low = lax.broadcasted_iota(jnp.int32, (occupied, LANES), 1) < occupied
    sub8 = lax.broadcasted_iota(jnp.int32, (8, LANES), 0)
    lane8 = lax.broadcasted_iota(jnp.int32, (8, LANES), 1)
    strip = (lane8 % occupied) // 8
    on_diag = lane8 % 8 == sub8

    def diagonal(block):
        merged = block[:8]
        for r in range(1, occupied // 8):
            merged = jnp.where(strip == r, block[8 * r:8 * r + 8], merged)
        return jnp.where(on_diag, merged, 0.0)

    for k8 in range(0, size, 8):
        for t in range(tiles):
            c0 = t * LANES
            diagonals = []
            for k in range(k8, k8 + 8, 2):
                r0 = k * occupied
                top = inner_mat[r0:r0 + occupied, c0:c0 + LANES]
                bottom = inner_mat[r0 + occupied:r0 + 2 * occupied, c0:c0 + LANES]
                if k < by_matmul:
                    other = flipped[c0:c0 + LANES, r0:r0 + LANES]
                else:
                    other = inner_mat[r0:r0 + LANES, c0:c0 + LANES].T
                f_top, f_bottom = other[:occupied], other[occupied:]
                swapped = pltpu.roll(jnp.where(low, f_bottom, f_top), occupied, 1)
                product = jnp.where(low, top, bottom) * jnp.where(low, f_top, f_bottom)
                product = product + jnp.where(low, bottom, top) * swapped
                cross[t] = cross[t] + jnp.sum(product.reshape(occupied // 8, 8, LANES), axis=0)
                diagonals.append(diagonal(top))
                diagonals.append(diagonal(bottom))
            store_rows(k0 + k8, t, fold_rows(diagonals, sub8))


def mask_kernel_rows(screen_refs, listed, width):
    return [
        jnp.concatenate(
            [jnp.full((1, width), ref[0, m].astype(jnp.float32)) for m in range(listed)], axis=1
        )
        for ref in screen_refs
    ]


def terms_kernel(*refs, first, count, picked, chunks, vectors, batch):
    if picked:
        mask_ref, carried_ref, refs = refs[0], refs[1], refs[2:]
    else:
        list_ref, screen_refs, refs = refs[0], refs[1:3], refs[3:]
    block_refs, theta_refs, rest = refs[:4], refs[4:4 + count], refs[4 + count:]
    out_ref, picked_ref, rows_ref = rest[0], rest[-2], rest[-1]
    occupied = block_refs[0].shape[0] // vectors
    depth = block_refs[0].shape[1]
    used = CORES * vectors
    columns = batch * occupied
    tiles = columns // LANES
    me = lax.axis_index("chol")
    core = lax.rem(me, CORES)
    chip = me // CORES

    if picked:
        masks = [mask_ref[b:b + 1, :] for b in range(CORES)]
        out_ref[...] = carried_ref[...]
    else:
        listed = list_ref.shape[0]
        width = depth // listed
        masks = mask_kernel_rows(screen_refs, listed, width)
        mask_ref = rest[1]
        for b in range(CORES):
            mask_ref[b:b + 1, :] = masks[b]
        out_ref[...] = jnp.zeros(out_ref.shape, out_ref.dtype)
    for b, group in enumerate((me, me ^ 1)):
        mask = masks[b].astype(picked_ref.dtype)
        if picked:
            for i, ref in enumerate(theta_refs):
                picked_ref[b, i * occupied:(i + 1) * occupied, :] = ref[b] * mask
        else:
            for m in range(listed):
                start = pl.multiple_of(list_ref[m, group] * width, width)
                tile_mask = mask[:, m * width:(m + 1) * width]
                for i, ref in enumerate(theta_refs):
                    picked_ref[b, i * occupied:(i + 1) * occupied, m * width:(m + 1) * width] = (
                        ref[0, :, pl.ds(start, width)] * tile_mask
                    )

    def one_batch(index):
        start = index * occupied
        rows = pl.ds(start if isinstance(index, int) else pl.multiple_of(start, columns), columns)
        cross = [jnp.zeros((8, LANES), jnp.float32) for _ in range(tiles)]
        tasks = []
        for b in range(CORES):
            theta, k0 = picked_ref[b, rows, :], 0
            while k0 < vectors:
                for size, by_matmul in chunks:
                    tasks.append((b, theta, k0, size, by_matmul))
                    k0 += size

        def products(task):
            b, theta, k0, size, by_matmul = task
            return chunk_products(block_refs[2 * b], block_refs[2 * b + 1], theta, occupied, k0, size, by_matmul)

        ahead = products(tasks[0])
        for i, (b, _, k0, size, by_matmul) in enumerate(tasks):
            now, ahead = ahead, products(tasks[i + 1]) if i + 1 < len(tasks) else None
            place = (core ^ b) * vectors

            def store_rows(k, t, value, place=place):
                rows_ref[pl.ds(pl.multiple_of(place + k, 8), 8), t * LANES:(t + 1) * LANES] = value

            chunk_terms(*now, cross, store_rows, occupied, k0, size, by_matmul)
        for t in range(tiles):
            rows_ref[used:used + 8, t * LANES:(t + 1) * LANES] = cross[t]
        values = rows_ref[...]
        parts = []
        for _ in range(3):
            part = values.astype(jnp.bfloat16)
            parts.append(part)
            values = values - part.astype(jnp.float32)
        seg_row = lax.broadcasted_iota(jnp.int32, (8, columns), 0)
        seg_col = lax.broadcasted_iota(jnp.int32, (8, columns), 1)
        segment = jnp.where(seg_col // occupied == seg_row, 1.0, 0.0).astype(jnp.bfloat16)
        sums = sum(
            lax.dot_general(segment, part, NT, preferred_element_type=jnp.float32) for part in parts
        )
        for i in range(batch):
            owner = chip ^ (first + index + i)
            out_ref[pl.ds(owner, 1), 0, :used + 8] = sums[i:i + 1]

    if count == batch:
        one_batch(0)
    else:
        @pl.loop(0, count // batch)
        def _(step):
            one_batch(step * batch)


def chip_terms(scalars, so_far, blocks, thetas, first, chunks, vectors, chips, out_width):
    count = len(thetas)
    batch = min(count, BATCH)
    rows, depth = blocks[0].shape
    occupied = rows // vectors
    vector_operands = [*so_far, *blocks, *thetas]
    out_shape = [jax.ShapeDtypeStruct((chips, 1, out_width), jnp.float32)]
    if scalars:
        out_shape.append(jax.ShapeDtypeStruct((CORES, depth), jnp.float32))
    return pl.pallas_call(
        functools.partial(
            terms_kernel, first=first, count=count, picked=not scalars, chunks=chunks, vectors=vectors, batch=batch
        ),
        in_specs=[SMEM] * len(scalars) + [VMEM] * len(vector_operands),
        out_specs=[VMEM] * len(out_shape),
        out_shape=out_shape,
        scratch_shapes=[
            pltpu.VMEM((CORES, count * occupied, depth), thetas[0].dtype),
            pltpu.VMEM((CORES * vectors + 8, batch * occupied), jnp.float32),
        ],
        compiler_params=PARAMS,
        cost_estimate=SMALL,
        name="chip_terms",
    )(*scalars, *vector_operands)


def energy_terms(rows, used):
    lane = lax.broadcasted_iota(jnp.int32, rows.shape, 1)
    return jnp.where(lane < used, rows * rows, jnp.where(lane < used + 8, -rows, 0.0))


def finish_kernel(rows_ref, bias_ref, energy_ref, bias_buf, energy_buf, sems, *, used, scale):
    chips, _, width = rows_ref.shape
    fit = LANES // used if width == LANES else 0
    lane = lax.broadcasted_iota(jnp.int32, (1, width), 1)
    if fit and chips % fit == 0:
        for d in range(0, chips, fit):
            packed = rows_ref[d]
            for i in range(1, fit):
                packed = jnp.where(lane < i * used, packed, pltpu.roll(rows_ref[d + i], i * used, 1))
            bias_buf[:, d * used:(d + fit) * used] = packed
    else:
        for d in range(chips):
            bias_buf[:, d * used:(d + 1) * used] = rows_ref[d, :, :used]
    bias_copy = pltpu.make_async_copy(bias_buf, bias_ref, sems.at[0])
    bias_copy.start()
    total = energy_terms(rows_ref[0], used)
    for d in range(1, chips):
        total = total + energy_terms(rows_ref[d], used)
    energy_buf[...] = jnp.sum(total, axis=1, keepdims=True) * scale
    energy_copy = pltpu.make_async_copy(energy_buf, energy_ref, sems.at[1])
    energy_copy.start()
    bias_copy.wait()
    energy_copy.wait()


def finish(rows, used, scale):
    chips = rows.shape[0]
    shapes = [(1, chips * used), (1, 1)]
    force_bias, energy = pl.pallas_call(
        functools.partial(finish_kernel, used=used, scale=scale),
        in_specs=[VMEM],
        out_specs=[pl.BlockSpec(memory_space=pl.ANY)] * 2,
        out_shape=[jax.ShapeDtypeStruct(s, jnp.float32) for s in shapes],
        scratch_shapes=[pltpu.VMEM(s, jnp.float32) for s in shapes] + [pltpu.SemaphoreType.DMA((2,))],
        name="finish",
    )(rows)
    return force_bias, energy.reshape(1)


def body(theta, chol_tiles, screen, tile_list):
    groups = lax.axis_size("chol")
    chips = groups // CORES
    half = chips // 2
    _, occupied, _ = theta.shape
    vectors = chol_tiles.shape[2]
    used = CORES * vectors
    out_width = LANES * ((used + 8 + LANES - 1) // LANES)
    listing = tile_list.T

    def to_chip(x, offset):
        return lax.ppermute(x, "chol", [(i, i ^ (offset * CORES)) for i in range(groups)])

    def to_core(x):
        return lax.ppermute(x, "chol", [(i, i ^ 1) for i in range(groups)])

    part = half // 2

    def across(x, early):
        pairs = [(i, i ^ (half * CORES)) for i in range(groups) if bool((i // CORES) & part) == early]
        return lax.ppermute(x, "chol", pairs)

    first, second = across(theta, True), across(theta, False)
    near = [theta] + [to_chip(theta, offset) for offset in range(1, half - 1)]
    own, own_turned = prepare_block(chol_tiles)
    near[2], own, late_theta = lax.optimization_barrier((near[2], own, theta))
    near.append(to_chip(late_theta, half - 1))
    first, near[1], second = lax.optimization_barrier((first, near[1], second))
    pieces = pick_tiles(listing, first, second, own.shape[1], half, part)
    beyond = [pieces[0]] + [to_chip(pieces[offset], offset) for offset in range(1, half)]
    other_chol, late_screen, near[-1] = lax.optimization_barrier((to_core(chol_tiles), screen, near[-1]))
    other, other_turned = prepare_block(other_chol)
    blocks = [own, own_turned, other, other_turned]

    scalars = [listing, screen, to_core(late_screen)]
    rows, masks = chip_terms(scalars, [], blocks, near, 0, NEAR, vectors, chips, out_width)
    rows, = chip_terms([], [masks, rows], blocks, beyond, half, BEYOND, vectors, chips, out_width)
    same_core = [list(range(core, groups, CORES)) for core in range(CORES)]
    back = lax.all_to_all(rows, "chol", split_axis=0, concat_axis=0, tiled=True, axis_index_groups=same_core)
    return finish(back, used, 1.0 / (2.0 * occupied * occupied))


def solution(mesh):
    in_specs = (
        P(("grp", "chol"), None, None),
        P("chol", None, None, None, None),
        P("chol", None),
        P(),
    )
    out_specs = (P(("grp", "chol"), None), P(("grp", "chol")))
    return jax.shard_map(body, mesh=mesh, in_specs=in_specs, out_specs=out_specs, check_vma=False)
```

```python
import functools

import jax
import jax.numpy as jnp
from jax import lax
from jax.experimental import pallas as pl
from jax.experimental.pallas import tpu as pltpu
from jax.sharding import PartitionSpec as P

LANES = 128
CORES = 2
VMEM_LIMIT = 32 * 1024 * 1024
NEAR = ((8, 4),)
BEYOND = ((8, 8), (8, 0))
BATCH = 4
VMEM = pl.BlockSpec(memory_space=pltpu.VMEM)
SMEM = pl.BlockSpec(memory_space=pltpu.SMEM)
PARAMS = pltpu.CompilerParams(vmem_limit_bytes=VMEM_LIMIT)
SMALL = pl.CostEstimate(flops=0, bytes_accessed=0, transcendentals=0)
NT = (((1,), (1,)), ((), ()))
NN = (((1,), (0,)), ((), ()))


def prepare_kernel(chol_ref, block_ref, turned_ref):
    _, listed, vectors, occupied, width = chol_ref.shape
    for m in range(listed):
        tile = chol_ref[0, m].reshape(vectors * occupied, width)
        block_ref[:, m * width:(m + 1) * width] = tile
        turned_ref[m * width:(m + 1) * width, :] = tile.T


def prepare_block(chol_tiles):
    _, listed, vectors, occupied, width = chol_tiles.shape
    rows, depth = vectors * occupied, listed * width
    return pl.pallas_call(
        prepare_kernel,
        in_specs=[VMEM],
        out_specs=[VMEM, VMEM],
        out_shape=[
            jax.ShapeDtypeStruct((rows, depth), chol_tiles.dtype),
            jax.ShapeDtypeStruct((depth, rows), chol_tiles.dtype),
        ],
        compiler_params=PARAMS,
        cost_estimate=SMALL,
        name="prepare_block",
    )(chol_tiles)


def pick_kernel(list_ref, theta_ref, *out_refs):
    listed = list_ref.shape[0]
    width = out_refs[0].shape[2] // listed
    me = lax.axis_index("chol")
    for offset, out_ref in enumerate(out_refs):
        device = me ^ (offset * CORES)
        for b, group in enumerate((device, device ^ 1)):
            for m in range(listed):
                start = pl.multiple_of(list_ref[m, group] * width, width)
                out_ref[b, :, m * width:(m + 1) * width] = theta_ref[0, :, pl.ds(start, width)]


def pick_tiles(listing, theta, depth, count):
    piece = jax.ShapeDtypeStruct((CORES, theta.shape[1], depth), theta.dtype)
    return pl.pallas_call(
        pick_kernel,
        in_specs=[SMEM, VMEM],
        out_specs=[VMEM] * count,
        out_shape=[piece] * count,
        compiler_params=PARAMS,
        cost_estimate=SMALL,
        name="pick_tiles",
    )(listing, theta)


def fold_rows(blocks, sub):
    high = sub < 4
    pairs = []
    for i in range(4):
        a, b = blocks[i], blocks[i + 4]
        pairs.append(jnp.where(high, a, b) + pltpu.roll(jnp.where(high, b, a), 4, 0))
    for shift in (2, 1):
        first = sub % (2 * shift) < shift
        half = len(pairs) // 2
        pairs = [
            jnp.where(
                first,
                pairs[i] + pltpu.roll(pairs[i], 8 - shift, 0),
                pairs[i + half] + pltpu.roll(pairs[i + half], shift, 0),
            )
            for i in range(half)
        ]
    return pairs[0]


def chunk_products(block_ref, turned_ref, theta, occupied, k0, size, by_matmul):
    span = slice(k0 * occupied, (k0 + size) * occupied)
    inner_mat = lax.dot_general(block_ref[span, :], theta, NT, preferred_element_type=jnp.float32)
    if not by_matmul:
        return inner_mat, None
    turned = slice(k0 * occupied, (k0 + by_matmul) * occupied)
    return inner_mat, lax.dot_general(theta, turned_ref[:, turned], NN, preferred_element_type=jnp.float32)


def chunk_terms(inner_mat, flipped, cross, store_rows, occupied, k0, size, by_matmul):
    tiles = inner_mat.shape[1] // LANES

    low = lax.broadcasted_iota(jnp.int32, (occupied, LANES), 1) < occupied
    sub8 = lax.broadcasted_iota(jnp.int32, (8, LANES), 0)
    lane8 = lax.broadcasted_iota(jnp.int32, (8, LANES), 1)
    strip = (lane8 % occupied) // 8
    on_diag = lane8 % 8 == sub8

    def diagonal(block):
        merged = block[:8]
        for r in range(1, occupied // 8):
            merged = jnp.where(strip == r, block[8 * r:8 * r + 8], merged)
        return jnp.where(on_diag, merged, 0.0)

    for k8 in range(0, size, 8):
        for t in range(tiles):
            c0 = t * LANES
            diagonals = []
            for k in range(k8, k8 + 8, 2):
                r0 = k * occupied
                top = inner_mat[r0:r0 + occupied, c0:c0 + LANES]
                bottom = inner_mat[r0 + occupied:r0 + 2 * occupied, c0:c0 + LANES]
                if k < by_matmul:
                    other = flipped[c0:c0 + LANES, r0:r0 + LANES]
                else:
                    other = inner_mat[r0:r0 + LANES, c0:c0 + LANES].T
                f_top, f_bottom = other[:occupied], other[occupied:]
                swapped = pltpu.roll(jnp.where(low, f_bottom, f_top), occupied, 1)
                product = jnp.where(low, top, bottom) * jnp.where(low, f_top, f_bottom)
                product = product + jnp.where(low, bottom, top) * swapped
                cross[t] = cross[t] + jnp.sum(product.reshape(occupied // 8, 8, LANES), axis=0)
                diagonals.append(diagonal(top))
                diagonals.append(diagonal(bottom))
            store_rows(k0 + k8, t, fold_rows(diagonals, sub8))


def mask_kernel_rows(screen_refs, listed, width):
    return [
        jnp.concatenate(
            [jnp.full((1, width), ref[0, m].astype(jnp.float32)) for m in range(listed)], axis=1
        )
        for ref in screen_refs
    ]


def terms_kernel(*refs, first, count, screened, chunks, vectors, batch):
    if screened:
        screen_refs, refs = refs[:2], refs[2:]
    else:
        mask_ref, carried_ref, refs = refs[0], refs[1], refs[2:]
    block_refs, theta_refs, rest = refs[:4], refs[4:4 + count], refs[4 + count:]
    out_ref, picked_ref, rows_ref = rest[0], rest[-2], rest[-1]
    occupied = block_refs[0].shape[0] // vectors
    depth = block_refs[0].shape[1]
    used = CORES * vectors
    columns = batch * occupied
    tiles = columns // LANES
    me = lax.axis_index("chol")
    core = lax.rem(me, CORES)
    chip = me // CORES

    if screened:
        listed = screen_refs[0].shape[1]
        masks = mask_kernel_rows(screen_refs, listed, depth // listed)
        mask_ref = rest[1]
        for b in range(CORES):
            mask_ref[b:b + 1, :] = masks[b]
        out_ref[...] = jnp.zeros(out_ref.shape, out_ref.dtype)
    else:
        masks = [mask_ref[b:b + 1, :] for b in range(CORES)]
        out_ref[...] = carried_ref[...]
    for b in range(CORES):
        mask = masks[b].astype(picked_ref.dtype)
        for i, ref in enumerate(theta_refs):
            picked_ref[b, i * occupied:(i + 1) * occupied, :] = ref[b] * mask

    def one_batch(index):
        start = index * occupied
        rows = pl.ds(start if isinstance(index, int) else pl.multiple_of(start, columns), columns)
        cross = [jnp.zeros((8, LANES), jnp.float32) for _ in range(tiles)]
        tasks = []
        for b in range(CORES):
            theta, k0 = picked_ref[b, rows, :], 0
            while k0 < vectors:
                for size, by_matmul in chunks:
                    tasks.append((b, theta, k0, size, by_matmul))
                    k0 += size

        def products(task):
            b, theta, k0, size, by_matmul = task
            return chunk_products(block_refs[2 * b], block_refs[2 * b + 1], theta, occupied, k0, size, by_matmul)

        ahead = products(tasks[0])
        for i, (b, _, k0, size, by_matmul) in enumerate(tasks):
            now, ahead = ahead, products(tasks[i + 1]) if i + 1 < len(tasks) else None
            place = (core ^ b) * vectors

            def store_rows(k, t, value, place=place):
                rows_ref[pl.ds(pl.multiple_of(place + k, 8), 8), t * LANES:(t + 1) * LANES] = value

            chunk_terms(*now, cross, store_rows, occupied, k0, size, by_matmul)
        for t in range(tiles):
            rows_ref[used:used + 8, t * LANES:(t + 1) * LANES] = cross[t]
        values = rows_ref[...]
        parts = []
        for _ in range(3):
            part = values.astype(jnp.bfloat16)
            parts.append(part)
            values = values - part.astype(jnp.float32)
        seg_row = lax.broadcasted_iota(jnp.int32, (8, columns), 0)
        seg_col = lax.broadcasted_iota(jnp.int32, (8, columns), 1)
        segment = jnp.where(seg_col // occupied == seg_row, 1.0, 0.0).astype(jnp.bfloat16)
        sums = sum(
            lax.dot_general(segment, part, NT, preferred_element_type=jnp.float32) for part in parts
        )
        for i in range(batch):
            owner = chip ^ (first + index + i)
            out_ref[pl.ds(owner, 1), 0, :used + 8] = sums[i:i + 1]

    if count == batch:
        one_batch(0)
    else:
        @pl.loop(0, count // batch)
        def _(step):
            one_batch(step * batch)


def chip_terms(screens, so_far, blocks, thetas, first, chunks, vectors, chips, out_width):
    count = len(thetas)
    batch = min(count, BATCH)
    rows, depth = blocks[0].shape
    occupied = rows // vectors
    vector_operands = [*so_far, *blocks, *thetas]
    out_shape = [jax.ShapeDtypeStruct((chips, 1, out_width), jnp.float32)]
    if screens:
        out_shape.append(jax.ShapeDtypeStruct((CORES, depth), jnp.float32))
    return pl.pallas_call(
        functools.partial(
            terms_kernel, first=first, count=count, screened=bool(screens), chunks=chunks, vectors=vectors, batch=batch
        ),
        in_specs=[SMEM] * len(screens) + [VMEM] * len(vector_operands),
        out_specs=[VMEM] * len(out_shape),
        out_shape=out_shape,
        scratch_shapes=[
            pltpu.VMEM((CORES, count * occupied, depth), thetas[0].dtype),
            pltpu.VMEM((CORES * vectors + 8, batch * occupied), jnp.float32),
        ],
        compiler_params=PARAMS,
        cost_estimate=SMALL,
        name="chip_terms",
    )(*screens, *vector_operands)


def energy_terms(rows, used):
    lane = lax.broadcasted_iota(jnp.int32, rows.shape, 1)
    return jnp.where(lane < used, rows * rows, jnp.where(lane < used + 8, -rows, 0.0))


def finish_kernel(rows_ref, bias_ref, energy_ref, bias_buf, energy_buf, sems, *, used, scale):
    chips, _, width = rows_ref.shape
    fit = LANES // used if width == LANES else 0
    lane = lax.broadcasted_iota(jnp.int32, (1, width), 1)
    if fit and chips % fit == 0:
        for d in range(0, chips, fit):
            packed = rows_ref[d]
            for i in range(1, fit):
                packed = jnp.where(lane < i * used, packed, pltpu.roll(rows_ref[d + i], i * used, 1))
            bias_buf[:, d * used:(d + fit) * used] = packed
    else:
        for d in range(chips):
            bias_buf[:, d * used:(d + 1) * used] = rows_ref[d, :, :used]
    bias_copy = pltpu.make_async_copy(bias_buf, bias_ref, sems.at[0])
    bias_copy.start()
    total = energy_terms(rows_ref[0], used)
    for d in range(1, chips):
        total = total + energy_terms(rows_ref[d], used)
    energy_buf[...] = jnp.sum(total, axis=1, keepdims=True) * scale
    energy_copy = pltpu.make_async_copy(energy_buf, energy_ref, sems.at[1])
    energy_copy.start()
    bias_copy.wait()
    energy_copy.wait()


def finish(rows, used, scale):
    chips = rows.shape[0]
    shapes = [(1, chips * used), (1, 1)]
    force_bias, energy = pl.pallas_call(
        functools.partial(finish_kernel, used=used, scale=scale),
        in_specs=[VMEM],
        out_specs=[pl.BlockSpec(memory_space=pl.ANY)] * 2,
        out_shape=[jax.ShapeDtypeStruct(s, jnp.float32) for s in shapes],
        scratch_shapes=[pltpu.VMEM(s, jnp.float32) for s in shapes] + [pltpu.SemaphoreType.DMA((2,))],
        name="finish",
    )(rows)
    return force_bias, energy.reshape(1)


def body(theta, chol_tiles, screen, tile_list):
    groups = lax.axis_size("chol")
    chips = groups // CORES
    half = chips // 2
    _, occupied, _ = theta.shape
    vectors = chol_tiles.shape[2]
    used = CORES * vectors
    out_width = LANES * ((used + 8 + LANES - 1) // LANES)
    depth = chol_tiles.shape[1] * chol_tiles.shape[4]
    listing = tile_list.T

    def to_chip(x, offset):
        return lax.ppermute(x, "chol", [(i, i ^ (offset * CORES)) for i in range(groups)])

    def to_core(x):
        return lax.ppermute(x, "chol", [(i, i ^ 1) for i in range(groups)])

    far = to_chip(theta, half)

    def spread(walker):
        pieces = pick_tiles(listing, walker, depth, half)
        return [pieces[0]] + [to_chip(pieces[offset], offset) for offset in range(1, half)]

    near = spread(theta)
    own, own_turned = prepare_block(chol_tiles)
    far, near[1], near[2], own = lax.optimization_barrier((far, near[1], near[2], own))
    beyond = spread(far)
    other_chol, late_screen, near[-1] = lax.optimization_barrier((to_core(chol_tiles), screen, near[-1]))
    other, other_turned = prepare_block(other_chol)
    blocks = [own, own_turned, other, other_turned]

    screens = [screen, to_core(late_screen)]
    rows, masks = chip_terms(screens, [], blocks, near, 0, NEAR, vectors, chips, out_width)
    rows, = chip_terms([], [masks, rows], blocks, beyond, half, BEYOND, vectors, chips, out_width)
    same_core = [list(range(core, groups, CORES)) for core in range(CORES)]
    back = lax.all_to_all(rows, "chol", split_axis=0, concat_axis=0, tiled=True, axis_index_groups=same_core)
    return finish(back, used, 1.0 / (2.0 * occupied * occupied))


def solution(mesh):
    in_specs = (
        P(("grp", "chol"), None, None),
        P("chol", None, None, None, None),
        P("chol", None),
        P(),
    )
    out_specs = (P(("grp", "chol"), None), P(("grp", "chol")))
    return jax.shard_map(body, mesh=mesh, in_specs=in_specs, out_specs=out_specs, check_vma=False)
```

```python
import functools

import jax
import jax.numpy as jnp
from jax import lax
from jax.experimental import pallas as pl
from jax.experimental.pallas import tpu as pltpu
from jax.sharding import PartitionSpec as P

LANES = 128
CORES = 2
VMEM_LIMIT = 32 * 1024 * 1024
NEAR = ((8, 4),)
BEYOND = ((8, 8), (8, 0))
BATCH = 4
VMEM = pl.BlockSpec(memory_space=pltpu.VMEM)
SMEM = pl.BlockSpec(memory_space=pltpu.SMEM)
PARAMS = pltpu.CompilerParams(vmem_limit_bytes=VMEM_LIMIT)
SMALL = pl.CostEstimate(flops=0, bytes_accessed=0, transcendentals=0)
NT = (((1,), (1,)), ((), ()))
NN = (((1,), (0,)), ((), ()))


def prepare_kernel(chol_ref, block_ref, turned_ref):
    _, listed, vectors, occupied, width = chol_ref.shape
    for m in range(listed):
        tile = chol_ref[0, m].reshape(vectors * occupied, width)
        block_ref[:, m * width:(m + 1) * width] = tile
        turned_ref[m * width:(m + 1) * width, :] = tile.T


def prepare_block(chol_tiles):
    _, listed, vectors, occupied, width = chol_tiles.shape
    rows, depth = vectors * occupied, listed * width
    return pl.pallas_call(
        prepare_kernel,
        in_specs=[VMEM],
        out_specs=[VMEM, VMEM],
        out_shape=[
            jax.ShapeDtypeStruct((rows, depth), chol_tiles.dtype),
            jax.ShapeDtypeStruct((depth, rows), chol_tiles.dtype),
        ],
        compiler_params=PARAMS,
        cost_estimate=SMALL,
        name="prepare_block",
    )(chol_tiles)


def pick_kernel(list_ref, theta_ref, *out_refs):
    listed = list_ref.shape[0]
    width = out_refs[0].shape[2] // listed
    me = lax.axis_index("chol")
    for offset, out_ref in enumerate(out_refs):
        device = me ^ (offset * CORES)
        for b, group in enumerate((device, device ^ 1)):
            for m in range(listed):
                start = pl.multiple_of(list_ref[m, group] * width, width)
                out_ref[b, :, m * width:(m + 1) * width] = theta_ref[0, :, pl.ds(start, width)]


def pick_tiles(listing, theta, depth, count):
    piece = jax.ShapeDtypeStruct((CORES, theta.shape[1], depth), theta.dtype)
    return pl.pallas_call(
        pick_kernel,
        in_specs=[SMEM, VMEM],
        out_specs=[VMEM] * count,
        out_shape=[piece] * count,
        compiler_params=PARAMS,
        cost_estimate=SMALL,
        name="pick_tiles",
    )(listing, theta)


def fold_rows(blocks, sub):
    high = sub < 4
    pairs = []
    for i in range(4):
        a, b = blocks[i], blocks[i + 4]
        pairs.append(jnp.where(high, a, b) + pltpu.roll(jnp.where(high, b, a), 4, 0))
    for shift in (2, 1):
        first = sub % (2 * shift) < shift
        half = len(pairs) // 2
        pairs = [
            jnp.where(
                first,
                pairs[i] + pltpu.roll(pairs[i], 8 - shift, 0),
                pairs[i + half] + pltpu.roll(pairs[i + half], shift, 0),
            )
            for i in range(half)
        ]
    return pairs[0]


def chunk_products(block_ref, turned_ref, theta, occupied, k0, size, by_matmul):
    span = slice(k0 * occupied, (k0 + size) * occupied)
    inner_mat = lax.dot_general(block_ref[span, :], theta, NT, preferred_element_type=jnp.float32)
    if not by_matmul:
        return inner_mat, None
    turned = slice(k0 * occupied, (k0 + by_matmul) * occupied)
    return inner_mat, lax.dot_general(theta, turned_ref[:, turned], NN, preferred_element_type=jnp.float32)


def chunk_terms(inner_mat, flipped, cross, store_rows, occupied, k0, size, by_matmul):
    tiles = inner_mat.shape[1] // LANES

    low = lax.broadcasted_iota(jnp.int32, (occupied, LANES), 1) < occupied
    sub8 = lax.broadcasted_iota(jnp.int32, (8, LANES), 0)
    lane8 = lax.broadcasted_iota(jnp.int32, (8, LANES), 1)
    strip = (lane8 % occupied) // 8
    on_diag = lane8 % 8 == sub8

    def diagonal(block):
        merged = block[:8]
        for r in range(1, occupied // 8):
            merged = jnp.where(strip == r, block[8 * r:8 * r + 8], merged)
        return jnp.where(on_diag, merged, 0.0)

    for k8 in range(0, size, 8):
        for t in range(tiles):
            c0 = t * LANES
            diagonals = []
            for k in range(k8, k8 + 8, 2):
                r0 = k * occupied
                top = inner_mat[r0:r0 + occupied, c0:c0 + LANES]
                bottom = inner_mat[r0 + occupied:r0 + 2 * occupied, c0:c0 + LANES]
                if k < by_matmul:
                    other = flipped[c0:c0 + LANES, r0:r0 + LANES]
                else:
                    other = inner_mat[r0:r0 + LANES, c0:c0 + LANES].T
                f_top, f_bottom = other[:occupied], other[occupied:]
                swapped = pltpu.roll(jnp.where(low, f_bottom, f_top), occupied, 1)
                product = jnp.where(low, top, bottom) * jnp.where(low, f_top, f_bottom)
                product = product + jnp.where(low, bottom, top) * swapped
                cross[t] = cross[t] + jnp.sum(product.reshape(occupied // 8, 8, LANES), axis=0)
                diagonals.append(diagonal(top))
                diagonals.append(diagonal(bottom))
            store_rows(k0 + k8, t, fold_rows(diagonals, sub8))


def mask_kernel_rows(screen_refs, listed, width):
    return [
        jnp.concatenate(
            [jnp.full((1, width), ref[0, m].astype(jnp.float32)) for m in range(listed)], axis=1
        )
        for ref in screen_refs
    ]


def terms_kernel(*refs, first, count, screened, chunks, vectors, batch):
    if screened:
        screen_refs, refs = refs[:2], refs[2:]
    else:
        mask_ref, carried_ref, refs = refs[0], refs[1], refs[2:]
    block_refs, theta_refs, rest = refs[:4], refs[4:4 + count], refs[4 + count:]
    out_ref, picked_ref, rows_ref = rest[0], rest[-2], rest[-1]
    occupied = block_refs[0].shape[0] // vectors
    depth = block_refs[0].shape[1]
    used = CORES * vectors
    columns = batch * occupied
    tiles = columns // LANES
    me = lax.axis_index("chol")
    core = lax.rem(me, CORES)
    chip = me // CORES

    if screened:
        listed = screen_refs[0].shape[1]
        masks = mask_kernel_rows(screen_refs, listed, depth // listed)
        mask_ref = rest[1]
        for b in range(CORES):
            mask_ref[b:b + 1, :] = masks[b]
        out_ref[...] = jnp.zeros(out_ref.shape, out_ref.dtype)
    else:
        masks = [mask_ref[b:b + 1, :] for b in range(CORES)]
        out_ref[...] = carried_ref[...]
    for b in range(CORES):
        mask = masks[b].astype(picked_ref.dtype)
        for i, ref in enumerate(theta_refs):
            picked_ref[b, i * occupied:(i + 1) * occupied, :] = ref[b] * mask

    def one_batch(index):
        start = index * occupied
        rows = pl.ds(start if isinstance(index, int) else pl.multiple_of(start, columns), columns)
        cross = [jnp.zeros((8, LANES), jnp.float32) for _ in range(tiles)]
        tasks = []
        for b in range(CORES):
            theta, k0 = picked_ref[b, rows, :], 0
            while k0 < vectors:
                for size, by_matmul in chunks:
                    tasks.append((b, theta, k0, size, by_matmul))
                    k0 += size

        def products(task):
            b, theta, k0, size, by_matmul = task
            return chunk_products(block_refs[2 * b], block_refs[2 * b + 1], theta, occupied, k0, size, by_matmul)

        ahead = products(tasks[0])
        for i, (b, _, k0, size, by_matmul) in enumerate(tasks):
            now, ahead = ahead, products(tasks[i + 1]) if i + 1 < len(tasks) else None
            place = (core ^ b) * vectors

            def store_rows(k, t, value, place=place):
                rows_ref[pl.ds(pl.multiple_of(place + k, 8), 8), t * LANES:(t + 1) * LANES] = value

            chunk_terms(*now, cross, store_rows, occupied, k0, size, by_matmul)
        for t in range(tiles):
            rows_ref[used:used + 8, t * LANES:(t + 1) * LANES] = cross[t]
        values = rows_ref[...]
        parts = []
        for _ in range(3):
            part = values.astype(jnp.bfloat16)
            parts.append(part)
            values = values - part.astype(jnp.float32)
        seg_row = lax.broadcasted_iota(jnp.int32, (8, columns), 0)
        seg_col = lax.broadcasted_iota(jnp.int32, (8, columns), 1)
        segment = jnp.where(seg_col // occupied == seg_row, 1.0, 0.0).astype(jnp.bfloat16)
        sums = sum(
            lax.dot_general(segment, part, NT, preferred_element_type=jnp.float32) for part in parts
        )
        for i in range(batch):
            owner = chip ^ (first + index + i)
            out_ref[pl.ds(owner, 1), 0, :used + 8] = sums[i:i + 1]

    if count == batch:
        one_batch(0)
    else:
        @pl.loop(0, count // batch)
        def _(step):
            one_batch(step * batch)


def chip_terms(screens, so_far, blocks, thetas, first, chunks, vectors, chips, out_width):
    count = len(thetas)
    batch = min(count, BATCH)
    rows, depth = blocks[0].shape
    occupied = rows // vectors
    vector_operands = [*so_far, *blocks, *thetas]
    out_shape = [jax.ShapeDtypeStruct((chips, 1, out_width), jnp.float32)]
    if screens:
        out_shape.append(jax.ShapeDtypeStruct((CORES, depth), jnp.float32))
    return pl.pallas_call(
        functools.partial(
            terms_kernel, first=first, count=count, screened=bool(screens), chunks=chunks, vectors=vectors, batch=batch
        ),
        in_specs=[SMEM] * len(screens) + [VMEM] * len(vector_operands),
        out_specs=[VMEM] * len(out_shape),
        out_shape=out_shape,
        scratch_shapes=[
            pltpu.VMEM((CORES, count * occupied, depth), thetas[0].dtype),
            pltpu.VMEM((CORES * vectors + 8, batch * occupied), jnp.float32),
        ],
        compiler_params=PARAMS,
        cost_estimate=SMALL,
        name="chip_terms",
    )(*screens, *vector_operands)


def energy_terms(rows, used):
    lane = lax.broadcasted_iota(jnp.int32, rows.shape, 1)
    return jnp.where(lane < used, rows * rows, jnp.where(lane < used + 8, -rows, 0.0))


def finish_kernel(rows_ref, bias_ref, energy_ref, bias_buf, energy_buf, sems, *, used, scale):
    chips, _, width = rows_ref.shape
    fit = LANES // used if width == LANES else 0
    lane = lax.broadcasted_iota(jnp.int32, (1, width), 1)
    if fit and chips % fit == 0:
        for d in range(0, chips, fit):
            packed = rows_ref[d]
            for i in range(1, fit):
                packed = jnp.where(lane < i * used, packed, pltpu.roll(rows_ref[d + i], i * used, 1))
            bias_buf[:, d * used:(d + fit) * used] = packed
    else:
        for d in range(chips):
            bias_buf[:, d * used:(d + 1) * used] = rows_ref[d, :, :used]
    bias_copy = pltpu.make_async_copy(bias_buf, bias_ref, sems.at[0])
    bias_copy.start()
    total = energy_terms(rows_ref[0], used)
    for d in range(1, chips):
        total = total + energy_terms(rows_ref[d], used)
    energy_buf[...] = jnp.sum(total, axis=1, keepdims=True) * scale
    energy_copy = pltpu.make_async_copy(energy_buf, energy_ref, sems.at[1])
    energy_copy.start()
    bias_copy.wait()
    energy_copy.wait()


def finish(rows, used, scale):
    chips = rows.shape[0]
    shapes = [(1, chips * used), (1, 1)]
    force_bias, energy = pl.pallas_call(
        functools.partial(finish_kernel, used=used, scale=scale),
        in_specs=[VMEM],
        out_specs=[pl.BlockSpec(memory_space=pl.ANY)] * 2,
        out_shape=[jax.ShapeDtypeStruct(s, jnp.float32) for s in shapes],
        scratch_shapes=[pltpu.VMEM(s, jnp.float32) for s in shapes] + [pltpu.SemaphoreType.DMA((2,))],
        name="finish",
    )(rows)
    return force_bias, energy.reshape(1)


def body(theta, chol_tiles, screen, tile_list):
    groups = lax.axis_size("chol")
    chips = groups // CORES
    half = chips // 2
    _, occupied, _ = theta.shape
    vectors = chol_tiles.shape[2]
    used = CORES * vectors
    out_width = LANES * ((used + 8 + LANES - 1) // LANES)
    depth = chol_tiles.shape[1] * chol_tiles.shape[4]
    listing = tile_list.T

    def to_chip(x, offset):
        return lax.ppermute(x, "chol", [(i, i ^ (offset * CORES)) for i in range(groups)])

    def to_core(x):
        return lax.ppermute(x, "chol", [(i, i ^ 1) for i in range(groups)])

    far = to_chip(theta, half)

    def spread(walker):
        pieces = pick_tiles(listing, walker, depth, half)
        return [pieces[0]] + [to_chip(pieces[offset], offset) for offset in range(1, half)]

    near = spread(theta)
    own, own_turned = prepare_block(chol_tiles)
    other_chol = to_core(chol_tiles)
    far, near[1], other_chol, own = lax.optimization_barrier((far, near[1], other_chol, own))
    beyond = spread(far)
    other_chol, late_screen, near[-1] = lax.optimization_barrier((other_chol, screen, near[-1]))
    other, other_turned = prepare_block(other_chol)
    blocks = [own, own_turned, other, other_turned]

    screens = [screen, to_core(late_screen)]
    rows, masks = chip_terms(screens, [], blocks, near, 0, NEAR, vectors, chips, out_width)
    rows, = chip_terms([], [masks, rows], blocks, beyond, half, BEYOND, vectors, chips, out_width)
    same_core = [list(range(core, groups, CORES)) for core in range(CORES)]
    back = lax.all_to_all(rows, "chol", split_axis=0, concat_axis=0, tiled=True, axis_index_groups=same_core)
    return finish(back, used, 1.0 / (2.0 * occupied * occupied))


def solution(mesh):
    in_specs = (
        P(("grp", "chol"), None, None),
        P("chol", None, None, None, None),
        P("chol", None),
        P(),
    )
    out_specs = (P(("grp", "chol"), None), P(("grp", "chol")))
    return jax.shard_map(body, mesh=mesh, in_specs=in_specs, out_specs=out_specs, check_vma=False)
```

```python
import functools

import jax
import jax.numpy as jnp
from jax import lax
from jax.experimental import pallas as pl
from jax.experimental.pallas import tpu as pltpu
from jax.sharding import PartitionSpec as P

LANES = 128
CORES = 2
VMEM_LIMIT = 32 * 1024 * 1024
NEAR = ((8, 4),)
BEYOND = ((8, 8), (8, 0))
BATCH = 4
VMEM = pl.BlockSpec(memory_space=pltpu.VMEM)
SMEM = pl.BlockSpec(memory_space=pltpu.SMEM)
PARAMS = pltpu.CompilerParams(vmem_limit_bytes=VMEM_LIMIT)
SMALL = pl.CostEstimate(flops=0, bytes_accessed=0, transcendentals=0)
NT = (((1,), (1,)), ((), ()))
NN = (((1,), (0,)), ((), ()))


def prepare_kernel(chol_ref, block_ref, turned_ref):
    _, listed, vectors, occupied, width = chol_ref.shape
    for m in range(listed):
        tile = chol_ref[0, m].reshape(vectors * occupied, width)
        block_ref[:, m * width:(m + 1) * width] = tile
        turned_ref[m * width:(m + 1) * width, :] = tile.T


def prepare_block(chol_tiles):
    _, listed, vectors, occupied, width = chol_tiles.shape
    rows, depth = vectors * occupied, listed * width
    return pl.pallas_call(
        prepare_kernel,
        in_specs=[VMEM],
        out_specs=[VMEM, VMEM],
        out_shape=[
            jax.ShapeDtypeStruct((rows, depth), chol_tiles.dtype),
            jax.ShapeDtypeStruct((depth, rows), chol_tiles.dtype),
        ],
        compiler_params=PARAMS,
        cost_estimate=SMALL,
        name="prepare_block",
    )(chol_tiles)


def pick_kernel(list_ref, theta_ref, *out_refs):
    listed = list_ref.shape[0]
    width = out_refs[0].shape[2] // listed
    me = lax.axis_index("chol")
    for offset, out_ref in enumerate(out_refs):
        device = me ^ (offset * CORES)
        for b, group in enumerate((device, device ^ 1)):
            for m in range(listed):
                start = pl.multiple_of(list_ref[m, group] * width, width)
                out_ref[b, :, m * width:(m + 1) * width] = theta_ref[0, :, pl.ds(start, width)]


def pick_tiles(listing, theta, depth, count):
    piece = jax.ShapeDtypeStruct((CORES, theta.shape[1], depth), theta.dtype)
    return pl.pallas_call(
        pick_kernel,
        in_specs=[SMEM, VMEM],
        out_specs=[VMEM] * count,
        out_shape=[piece] * count,
        compiler_params=PARAMS,
        cost_estimate=SMALL,
        name="pick_tiles",
    )(listing, theta)


def fold_rows(blocks, sub):
    high = sub < 4
    pairs = []
    for i in range(4):
        a, b = blocks[i], blocks[i + 4]
        pairs.append(jnp.where(high, a, b) + pltpu.roll(jnp.where(high, b, a), 4, 0))
    for shift in (2, 1):
        first = sub % (2 * shift) < shift
        half = len(pairs) // 2
        pairs = [
            jnp.where(
                first,
                pairs[i] + pltpu.roll(pairs[i], 8 - shift, 0),
                pairs[i + half] + pltpu.roll(pairs[i + half], shift, 0),
            )
            for i in range(half)
        ]
    return pairs[0]


def chunk_products(block_ref, turned_ref, theta, occupied, k0, size, by_matmul):
    span = slice(k0 * occupied, (k0 + size) * occupied)
    inner_mat = lax.dot_general(block_ref[span, :], theta, NT, preferred_element_type=jnp.float32)
    if not by_matmul:
        return inner_mat, None
    turned = slice(k0 * occupied, (k0 + by_matmul) * occupied)
    return inner_mat, lax.dot_general(theta, turned_ref[:, turned], NN, preferred_element_type=jnp.float32)


def chunk_terms(inner_mat, flipped, cross, store_rows, occupied, k0, size, by_matmul):
    tiles = inner_mat.shape[1] // LANES

    low = lax.broadcasted_iota(jnp.int32, (occupied, LANES), 1) < occupied
    sub8 = lax.broadcasted_iota(jnp.int32, (8, LANES), 0)
    lane8 = lax.broadcasted_iota(jnp.int32, (8, LANES), 1)
    strip = (lane8 % occupied) // 8
    on_diag = lane8 % 8 == sub8

    def diagonal(block):
        merged = block[:8]
        for r in range(1, occupied // 8):
            merged = jnp.where(strip == r, block[8 * r:8 * r + 8], merged)
        return jnp.where(on_diag, merged, 0.0)

    for k8 in range(0, size, 8):
        for t in range(tiles):
            c0 = t * LANES
            diagonals = []
            for k in range(k8, k8 + 8, 2):
                r0 = k * occupied
                top = inner_mat[r0:r0 + occupied, c0:c0 + LANES]
                bottom = inner_mat[r0 + occupied:r0 + 2 * occupied, c0:c0 + LANES]
                if k < by_matmul:
                    other = flipped[c0:c0 + LANES, r0:r0 + LANES]
                else:
                    other = inner_mat[r0:r0 + LANES, c0:c0 + LANES].T
                f_top, f_bottom = other[:occupied], other[occupied:]
                swapped = pltpu.roll(jnp.where(low, f_bottom, f_top), occupied, 1)
                product = jnp.where(low, top, bottom) * jnp.where(low, f_top, f_bottom)
                product = product + jnp.where(low, bottom, top) * swapped
                cross[t] = cross[t] + jnp.sum(product.reshape(occupied // 8, 8, LANES), axis=0)
                diagonals.append(diagonal(top))
                diagonals.append(diagonal(bottom))
            store_rows(k0 + k8, t, fold_rows(diagonals, sub8))


def mask_kernel_rows(screen_refs, listed, width):
    return [
        jnp.concatenate(
            [jnp.full((1, width), ref[0, m].astype(jnp.float32)) for m in range(listed)], axis=1
        )
        for ref in screen_refs
    ]


def terms_kernel(*refs, first, count, screened, chunks, vectors, batch):
    if screened:
        screen_refs, refs = refs[:2], refs[2:]
    else:
        mask_ref, carried_ref, refs = refs[0], refs[1], refs[2:]
    block_refs, theta_refs, rest = refs[:4], refs[4:4 + count], refs[4 + count:]
    out_ref, picked_ref, rows_ref = rest[0], rest[-2], rest[-1]
    occupied = block_refs[0].shape[0] // vectors
    depth = block_refs[0].shape[1]
    used = CORES * vectors
    columns = batch * occupied
    tiles = columns // LANES
    me = lax.axis_index("chol")
    core = lax.rem(me, CORES)
    chip = me // CORES

    if screened:
        listed = screen_refs[0].shape[1]
        masks = mask_kernel_rows(screen_refs, listed, depth // listed)
        mask_ref = rest[1]
        for b in range(CORES):
            mask_ref[b:b + 1, :] = masks[b]
        out_ref[...] = jnp.zeros(out_ref.shape, out_ref.dtype)
    else:
        masks = [mask_ref[b:b + 1, :] for b in range(CORES)]
        out_ref[...] = carried_ref[...]
    for b in range(CORES):
        mask = masks[b].astype(picked_ref.dtype)
        for i, ref in enumerate(theta_refs):
            picked_ref[b, i * occupied:(i + 1) * occupied, :] = ref[b] * mask

    def one_batch(index):
        start = index * occupied
        rows = pl.ds(start if isinstance(index, int) else pl.multiple_of(start, columns), columns)
        cross = [jnp.zeros((8, LANES), jnp.float32) for _ in range(tiles)]
        tasks = []
        for b in range(CORES):
            theta, k0 = picked_ref[b, rows, :], 0
            while k0 < vectors:
                for size, by_matmul in chunks:
                    tasks.append((b, theta, k0, size, by_matmul))
                    k0 += size

        def products(task):
            b, theta, k0, size, by_matmul = task
            return chunk_products(block_refs[2 * b], block_refs[2 * b + 1], theta, occupied, k0, size, by_matmul)

        ahead = products(tasks[0])
        for i, (b, _, k0, size, by_matmul) in enumerate(tasks):
            now, ahead = ahead, products(tasks[i + 1]) if i + 1 < len(tasks) else None
            place = (core ^ b) * vectors

            def store_rows(k, t, value, place=place):
                rows_ref[pl.ds(pl.multiple_of(place + k, 8), 8), t * LANES:(t + 1) * LANES] = value

            chunk_terms(*now, cross, store_rows, occupied, k0, size, by_matmul)
        for t in range(tiles):
            rows_ref[used:used + 8, t * LANES:(t + 1) * LANES] = cross[t]
        values = rows_ref[...]
        parts = []
        for _ in range(3):
            part = values.astype(jnp.bfloat16)
            parts.append(part)
            values = values - part.astype(jnp.float32)
        seg_row = lax.broadcasted_iota(jnp.int32, (8, columns), 0)
        seg_col = lax.broadcasted_iota(jnp.int32, (8, columns), 1)
        segment = jnp.where(seg_col // occupied == seg_row, 1.0, 0.0).astype(jnp.bfloat16)
        sums = sum(
            lax.dot_general(segment, part, NT, preferred_element_type=jnp.float32) for part in parts
        )
        for i in range(batch):
            owner = chip ^ (first + index + i)
            out_ref[pl.ds(owner, 1), 0, :used + 8] = sums[i:i + 1]

    if count == batch:
        one_batch(0)
    else:
        @pl.loop(0, count // batch)
        def _(step):
            one_batch(step * batch)


def chip_terms(screens, so_far, blocks, thetas, first, chunks, vectors, chips, out_width):
    count = len(thetas)
    batch = min(count, BATCH)
    rows, depth = blocks[0].shape
    occupied = rows // vectors
    vector_operands = [*so_far, *blocks, *thetas]
    out_shape = [jax.ShapeDtypeStruct((chips, 1, out_width), jnp.float32)]
    if screens:
        out_shape.append(jax.ShapeDtypeStruct((CORES, depth), jnp.float32))
    return pl.pallas_call(
        functools.partial(
            terms_kernel, first=first, count=count, screened=bool(screens), chunks=chunks, vectors=vectors, batch=batch
        ),
        in_specs=[SMEM] * len(screens) + [VMEM] * len(vector_operands),
        out_specs=[VMEM] * len(out_shape),
        out_shape=out_shape,
        scratch_shapes=[
            pltpu.VMEM((CORES, count * occupied, depth), thetas[0].dtype),
            pltpu.VMEM((CORES * vectors + 8, batch * occupied), jnp.float32),
        ],
        compiler_params=PARAMS,
        cost_estimate=SMALL,
        name="chip_terms",
    )(*screens, *vector_operands)


def energy_terms(rows, used):
    lane = lax.broadcasted_iota(jnp.int32, rows.shape, 1)
    return jnp.where(lane < used, rows * rows, jnp.where(lane < used + 8, -rows, 0.0))


def finish_kernel(rows_ref, bias_ref, energy_ref, bias_buf, energy_buf, sems, *, used, scale):
    chips, _, width = rows_ref.shape
    fit = LANES // used if width == LANES else 0
    lane = lax.broadcasted_iota(jnp.int32, (1, width), 1)
    if fit and chips % fit == 0:
        for d in range(0, chips, fit):
            packed = rows_ref[d]
            for i in range(1, fit):
                packed = jnp.where(lane < i * used, packed, pltpu.roll(rows_ref[d + i], i * used, 1))
            bias_buf[:, d * used:(d + fit) * used] = packed
    else:
        for d in range(chips):
            bias_buf[:, d * used:(d + 1) * used] = rows_ref[d, :, :used]
    bias_copy = pltpu.make_async_copy(bias_buf, bias_ref, sems.at[0])
    bias_copy.start()
    total = energy_terms(rows_ref[0], used)
    for d in range(1, chips):
        total = total + energy_terms(rows_ref[d], used)
    energy_buf[...] = jnp.sum(total, axis=1, keepdims=True) * scale
    energy_copy = pltpu.make_async_copy(energy_buf, energy_ref, sems.at[1])
    energy_copy.start()
    bias_copy.wait()
    energy_copy.wait()


def finish(rows, used, scale):
    chips = rows.shape[0]
    shapes = [(1, chips * used), (1, 1)]
    force_bias, energy = pl.pallas_call(
        functools.partial(finish_kernel, used=used, scale=scale),
        in_specs=[VMEM],
        out_specs=[pl.BlockSpec(memory_space=pl.ANY)] * 2,
        out_shape=[jax.ShapeDtypeStruct(s, jnp.float32) for s in shapes],
        scratch_shapes=[pltpu.VMEM(s, jnp.float32) for s in shapes] + [pltpu.SemaphoreType.DMA((2,))],
        name="finish",
    )(rows)
    return force_bias, energy.reshape(1)


def body(theta, chol_tiles, screen, tile_list):
    groups = lax.axis_size("chol")
    chips = groups // CORES
    half = chips // 2
    _, occupied, _ = theta.shape
    vectors = chol_tiles.shape[2]
    used = CORES * vectors
    out_width = LANES * ((used + 8 + LANES - 1) // LANES)
    depth = chol_tiles.shape[1] * chol_tiles.shape[4]
    listing = tile_list.T

    def to_chip(x, offset):
        return lax.ppermute(x, "chol", [(i, i ^ (offset * CORES)) for i in range(groups)])

    def to_core(x):
        return lax.ppermute(x, "chol", [(i, i ^ 1) for i in range(groups)])

    far = to_chip(theta, half)

    def spread(walker):
        pieces = pick_tiles(listing, walker, depth, half)
        return [pieces[0]] + [to_chip(pieces[offset], offset) for offset in range(1, half)]

    near = spread(theta)
    own, own_turned = prepare_block(chol_tiles)
    other_chol = to_core(chol_tiles)
    far, near[1], other_chol, own = lax.optimization_barrier((far, near[1], other_chol, own))
    beyond = spread(far)
    other_chol, late_screen, near[-1] = lax.optimization_barrier((other_chol, screen, near[-1]))
    other, other_turned = prepare_block(other_chol)
    blocks = [own, own_turned, other, other_turned]

    screens = [screen, to_core(late_screen)]
    rows, masks = chip_terms(screens, [], blocks, near, 0, NEAR, vectors, chips, out_width)
    rows, = chip_terms([], [masks, rows], blocks, beyond[:half // 2], half, BEYOND, vectors, chips, out_width)
    rows, = chip_terms([], [masks, rows], blocks, beyond[half // 2:], half + half // 2, BEYOND, vectors, chips, out_width)
    same_core = [list(range(core, groups, CORES)) for core in range(CORES)]
    back = lax.all_to_all(rows, "chol", split_axis=0, concat_axis=0, tiled=True, axis_index_groups=same_core)
    return finish(back, used, 1.0 / (2.0 * occupied * occupied))


def solution(mesh):
    in_specs = (
        P(("grp", "chol"), None, None),
        P("chol", None, None, None, None),
        P("chol", None),
        P(),
    )
    out_specs = (P(("grp", "chol"), None), P(("grp", "chol")))
    return jax.shard_map(body, mesh=mesh, in_specs=in_specs, out_specs=out_specs, check_vma=False)
```

```python
import functools

import jax
import jax.numpy as jnp
from jax import lax
from jax.experimental import pallas as pl
from jax.experimental.pallas import tpu as pltpu
from jax.sharding import PartitionSpec as P

LANES = 128
CORES = 2
VMEM_LIMIT = 32 * 1024 * 1024
NEAR = ((8, 4),)
BEYOND = ((8, 8), (8, 0))
BATCH = 4
VMEM = pl.BlockSpec(memory_space=pltpu.VMEM)
SMEM = pl.BlockSpec(memory_space=pltpu.SMEM)
PARAMS = pltpu.CompilerParams(vmem_limit_bytes=VMEM_LIMIT)
SMALL = pl.CostEstimate(flops=0, bytes_accessed=0, transcendentals=0)
NT = (((1,), (1,)), ((), ()))
NN = (((1,), (0,)), ((), ()))


def prepare_kernel(chol_ref, block_ref, turned_ref):
    _, listed, vectors, occupied, width = chol_ref.shape
    for m in range(listed):
        tile = chol_ref[0, m].reshape(vectors * occupied, width)
        block_ref[:, m * width:(m + 1) * width] = tile
        turned_ref[m * width:(m + 1) * width, :] = tile.T


def prepare_block(chol_tiles):
    _, listed, vectors, occupied, width = chol_tiles.shape
    rows, depth = vectors * occupied, listed * width
    return pl.pallas_call(
        prepare_kernel,
        in_specs=[VMEM],
        out_specs=[VMEM, VMEM],
        out_shape=[
            jax.ShapeDtypeStruct((rows, depth), chol_tiles.dtype),
            jax.ShapeDtypeStruct((depth, rows), chol_tiles.dtype),
        ],
        compiler_params=PARAMS,
        cost_estimate=SMALL,
        name="prepare_block",
    )(chol_tiles)


def pick_kernel(list_ref, theta_ref, *out_refs):
    listed = list_ref.shape[0]
    width = out_refs[0].shape[2] // listed
    me = lax.axis_index("chol")
    for offset, out_ref in enumerate(out_refs):
        device = me ^ (offset * CORES)
        for b, group in enumerate((device, device ^ 1)):
            for m in range(listed):
                start = pl.multiple_of(list_ref[m, group] * width, width)
                out_ref[b, :, m * width:(m + 1) * width] = theta_ref[0, :, pl.ds(start, width)]


def pick_tiles(listing, theta, depth, count):
    piece = jax.ShapeDtypeStruct((CORES, theta.shape[1], depth), theta.dtype)
    return pl.pallas_call(
        pick_kernel,
        in_specs=[SMEM, VMEM],
        out_specs=[VMEM] * count,
        out_shape=[piece] * count,
        compiler_params=PARAMS,
        cost_estimate=SMALL,
        name="pick_tiles",
    )(listing, theta)


def fold_rows(blocks, sub):
    high = sub < 4
    pairs = []
    for i in range(4):
        a, b = blocks[i], blocks[i + 4]
        pairs.append(jnp.where(high, a, b) + pltpu.roll(jnp.where(high, b, a), 4, 0))
    for shift in (2, 1):
        first = sub % (2 * shift) < shift
        half = len(pairs) // 2
        pairs = [
            jnp.where(
                first,
                pairs[i] + pltpu.roll(pairs[i], 8 - shift, 0),
                pairs[i + half] + pltpu.roll(pairs[i + half], shift, 0),
            )
            for i in range(half)
        ]
    return pairs[0]


def chunk_products(block_ref, turned_ref, theta, occupied, k0, size, by_matmul):
    span = slice(k0 * occupied, (k0 + size) * occupied)
    inner_mat = lax.dot_general(block_ref[span, :], theta, NT, preferred_element_type=jnp.float32)
    if not by_matmul:
        return inner_mat, None
    turned = slice(k0 * occupied, (k0 + by_matmul) * occupied)
    return inner_mat, lax.dot_general(theta, turned_ref[:, turned], NN, preferred_element_type=jnp.float32)


def chunk_terms(inner_mat, flipped, cross, store_rows, occupied, k0, size, by_matmul):
    tiles = inner_mat.shape[1] // LANES

    low = lax.broadcasted_iota(jnp.int32, (occupied, LANES), 1) < occupied
    sub8 = lax.broadcasted_iota(jnp.int32, (8, LANES), 0)
    lane8 = lax.broadcasted_iota(jnp.int32, (8, LANES), 1)
    strip = (lane8 % occupied) // 8
    on_diag = lane8 % 8 == sub8

    def diagonal(block):
        merged = block[:8]
        for r in range(1, occupied // 8):
            merged = jnp.where(strip == r, block[8 * r:8 * r + 8], merged)
        return jnp.where(on_diag, merged, 0.0)

    for k8 in range(0, size, 8):
        for t in range(tiles):
            c0 = t * LANES
            diagonals = []
            for k in range(k8, k8 + 8, 2):
                r0 = k * occupied
                top = inner_mat[r0:r0 + occupied, c0:c0 + LANES]
                bottom = inner_mat[r0 + occupied:r0 + 2 * occupied, c0:c0 + LANES]
                if k < by_matmul:
                    other = flipped[c0:c0 + LANES, r0:r0 + LANES]
                else:
                    other = inner_mat[r0:r0 + LANES, c0:c0 + LANES].T
                f_top, f_bottom = other[:occupied], other[occupied:]
                swapped = pltpu.roll(jnp.where(low, f_bottom, f_top), occupied, 1)
                product = jnp.where(low, top, bottom) * jnp.where(low, f_top, f_bottom)
                product = product + jnp.where(low, bottom, top) * swapped
                cross[t] = cross[t] + jnp.sum(product.reshape(occupied // 8, 8, LANES), axis=0)
                diagonals.append(diagonal(top))
                diagonals.append(diagonal(bottom))
            store_rows(k0 + k8, t, fold_rows(diagonals, sub8))


def send_order(place, count):
    return jnp.where(place <= 1, place, jnp.where(place == 2, count - 1, place - 1))


def mask_kernel_rows(screen_refs, listed, width):
    return [
        jnp.concatenate(
            [jnp.full((1, width), ref[0, m].astype(jnp.float32)) for m in range(listed)], axis=1
        )
        for ref in screen_refs
    ]


def terms_kernel(*refs, first, count, screened, chunks, vectors, batch):
    if screened:
        screen_refs, refs = refs[:2], refs[2:]
    else:
        mask_ref, carried_ref, refs = refs[0], refs[1], refs[2:]
    block_refs, theta_refs, rest = refs[:4], refs[4:4 + count], refs[4 + count:]
    out_ref, picked_ref, rows_ref = rest[0], rest[-2], rest[-1]
    occupied = block_refs[0].shape[0] // vectors
    depth = block_refs[0].shape[1]
    used = CORES * vectors
    columns = batch * occupied
    tiles = columns // LANES
    me = lax.axis_index("chol")
    core = lax.rem(me, CORES)
    chip = me // CORES

    if screened:
        listed = screen_refs[0].shape[1]
        masks = mask_kernel_rows(screen_refs, listed, depth // listed)
        mask_ref = rest[1]
        for b in range(CORES):
            mask_ref[b:b + 1, :] = masks[b]
        out_ref[...] = jnp.zeros(out_ref.shape, out_ref.dtype)
    else:
        masks = [mask_ref[b:b + 1, :] for b in range(CORES)]
        out_ref[...] = carried_ref[...]
    for b in range(CORES):
        mask = masks[b].astype(picked_ref.dtype)
        for i, ref in enumerate(theta_refs):
            picked_ref[b, i * occupied:(i + 1) * occupied, :] = ref[b] * mask

    def one_batch(index):
        start = index * occupied
        rows = pl.ds(start if isinstance(index, int) else pl.multiple_of(start, columns), columns)
        cross = [jnp.zeros((8, LANES), jnp.float32) for _ in range(tiles)]
        tasks = []
        for b in range(CORES):
            theta, k0 = picked_ref[b, rows, :], 0
            while k0 < vectors:
                for size, by_matmul in chunks:
                    tasks.append((b, theta, k0, size, by_matmul))
                    k0 += size

        def products(task):
            b, theta, k0, size, by_matmul = task
            return chunk_products(block_refs[2 * b], block_refs[2 * b + 1], theta, occupied, k0, size, by_matmul)

        ahead = products(tasks[0])
        for i, (b, _, k0, size, by_matmul) in enumerate(tasks):
            now, ahead = ahead, products(tasks[i + 1]) if i + 1 < len(tasks) else None
            place = (core ^ b) * vectors

            def store_rows(k, t, value, place=place):
                rows_ref[pl.ds(pl.multiple_of(place + k, 8), 8), t * LANES:(t + 1) * LANES] = value

            chunk_terms(*now, cross, store_rows, occupied, k0, size, by_matmul)
        for t in range(tiles):
            rows_ref[used:used + 8, t * LANES:(t + 1) * LANES] = cross[t]
        values = rows_ref[...]
        parts = []
        for _ in range(3):
            part = values.astype(jnp.bfloat16)
            parts.append(part)
            values = values - part.astype(jnp.float32)
        seg_row = lax.broadcasted_iota(jnp.int32, (8, columns), 0)
        seg_col = lax.broadcasted_iota(jnp.int32, (8, columns), 1)
        segment = jnp.where(seg_col // occupied == seg_row, 1.0, 0.0).astype(jnp.bfloat16)
        sums = sum(
            lax.dot_general(segment, part, NT, preferred_element_type=jnp.float32) for part in parts
        )
        for i in range(batch):
            place = jnp.int32(index + i)
            if not screened:
                place = send_order(place, count)
            owner = chip ^ (first + place)
            out_ref[pl.ds(owner, 1), 0, :used + 8] = sums[i:i + 1]

    if count == batch:
        one_batch(0)
    else:
        @pl.loop(0, count // batch)
        def _(step):
            one_batch(step * batch)


def chip_terms(screens, so_far, blocks, thetas, first, chunks, vectors, chips, out_width):
    count = len(thetas)
    batch = min(count, BATCH)
    rows, depth = blocks[0].shape
    occupied = rows // vectors
    vector_operands = [*so_far, *blocks, *thetas]
    out_shape = [jax.ShapeDtypeStruct((chips, 1, out_width), jnp.float32)]
    if screens:
        out_shape.append(jax.ShapeDtypeStruct((CORES, depth), jnp.float32))
    return pl.pallas_call(
        functools.partial(
            terms_kernel, first=first, count=count, screened=bool(screens), chunks=chunks, vectors=vectors, batch=batch
        ),
        in_specs=[SMEM] * len(screens) + [VMEM] * len(vector_operands),
        out_specs=[VMEM] * len(out_shape),
        out_shape=out_shape,
        scratch_shapes=[
            pltpu.VMEM((CORES, count * occupied, depth), thetas[0].dtype),
            pltpu.VMEM((CORES * vectors + 8, batch * occupied), jnp.float32),
        ],
        compiler_params=PARAMS,
        cost_estimate=SMALL,
        name="chip_terms",
    )(*screens, *vector_operands)


def energy_terms(rows, used):
    lane = lax.broadcasted_iota(jnp.int32, rows.shape, 1)
    return jnp.where(lane < used, rows * rows, jnp.where(lane < used + 8, -rows, 0.0))


def finish_kernel(rows_ref, bias_ref, energy_ref, bias_buf, energy_buf, sems, *, used, scale):
    chips, _, width = rows_ref.shape
    fit = LANES // used if width == LANES else 0
    lane = lax.broadcasted_iota(jnp.int32, (1, width), 1)
    if fit and chips % fit == 0:
        for d in range(0, chips, fit):
            packed = rows_ref[d]
            for i in range(1, fit):
                packed = jnp.where(lane < i * used, packed, pltpu.roll(rows_ref[d + i], i * used, 1))
            bias_buf[:, d * used:(d + fit) * used] = packed
    else:
        for d in range(chips):
            bias_buf[:, d * used:(d + 1) * used] = rows_ref[d, :, :used]
    bias_copy = pltpu.make_async_copy(bias_buf, bias_ref, sems.at[0])
    bias_copy.start()
    total = energy_terms(rows_ref[0], used)
    for d in range(1, chips):
        total = total + energy_terms(rows_ref[d], used)
    energy_buf[...] = jnp.sum(total, axis=1, keepdims=True) * scale
    energy_copy = pltpu.make_async_copy(energy_buf, energy_ref, sems.at[1])
    energy_copy.start()
    bias_copy.wait()
    energy_copy.wait()


def finish(rows, used, scale):
    chips = rows.shape[0]
    shapes = [(1, chips * used), (1, 1)]
    force_bias, energy = pl.pallas_call(
        functools.partial(finish_kernel, used=used, scale=scale),
        in_specs=[VMEM],
        out_specs=[pl.BlockSpec(memory_space=pl.ANY)] * 2,
        out_shape=[jax.ShapeDtypeStruct(s, jnp.float32) for s in shapes],
        scratch_shapes=[pltpu.VMEM(s, jnp.float32) for s in shapes] + [pltpu.SemaphoreType.DMA((2,))],
        name="finish",
    )(rows)
    return force_bias, energy.reshape(1)


def body(theta, chol_tiles, screen, tile_list):
    groups = lax.axis_size("chol")
    chips = groups // CORES
    half = chips // 2
    _, occupied, _ = theta.shape
    vectors = chol_tiles.shape[2]
    used = CORES * vectors
    out_width = LANES * ((used + 8 + LANES - 1) // LANES)
    depth = chol_tiles.shape[1] * chol_tiles.shape[4]
    listing = tile_list.T

    def to_chip(x, offset):
        return lax.ppermute(x, "chol", [(i, i ^ (offset * CORES)) for i in range(groups)])

    def to_core(x):
        return lax.ppermute(x, "chol", [(i, i ^ 1) for i in range(groups)])

    far = to_chip(theta, half)

    def spread(walker, late=False):
        pieces = list(pick_tiles(listing, walker, depth, half))
        if late:
            pieces[-2], near[1] = lax.optimization_barrier((pieces[-2], near[1]))
        return [pieces[0]] + [to_chip(pieces[offset], offset) for offset in range(1, half)]

    near = spread(theta)
    own, own_turned = prepare_block(chol_tiles)
    other_chol = to_core(chol_tiles)
    far, other_chol, own = lax.optimization_barrier((far, other_chol, own))
    beyond = spread(far, True)
    beyond = beyond[:2] + beyond[-1:] + beyond[2:-1]
    other_chol, late_screen, near[-1] = lax.optimization_barrier((other_chol, screen, near[-1]))
    other, other_turned = prepare_block(other_chol)
    blocks = [own, own_turned, other, other_turned]

    screens = [screen, to_core(late_screen)]
    rows, masks = chip_terms(screens, [], blocks, near, 0, NEAR, vectors, chips, out_width)
    rows, = chip_terms([], [masks, rows], blocks, beyond, half, BEYOND, vectors, chips, out_width)
    same_core = [list(range(core, groups, CORES)) for core in range(CORES)]
    back = lax.all_to_all(rows, "chol", split_axis=0, concat_axis=0, tiled=True, axis_index_groups=same_core)
    return finish(back, used, 1.0 / (2.0 * occupied * occupied))


def solution(mesh):
    in_specs = (
        P(("grp", "chol"), None, None),
        P("chol", None, None, None, None),
        P("chol", None),
        P(),
    )
    out_specs = (P(("grp", "chol"), None), P(("grp", "chol")))
    return jax.shard_map(body, mesh=mesh, in_specs=in_specs, out_specs=out_specs, check_vma=False)
```

```python
import functools

import jax
import jax.numpy as jnp
from jax import lax
from jax.experimental import pallas as pl
from jax.experimental.pallas import tpu as pltpu
from jax.sharding import PartitionSpec as P

LANES = 128
CORES = 2
VMEM_LIMIT = 32 * 1024 * 1024
NEAR = ((8, 4),)
BEYOND = ((8, 8), (8, 0))
BATCH = 4
VMEM = pl.BlockSpec(memory_space=pltpu.VMEM)
SMEM = pl.BlockSpec(memory_space=pltpu.SMEM)
PARAMS = pltpu.CompilerParams(vmem_limit_bytes=VMEM_LIMIT)
SMALL = pl.CostEstimate(flops=0, bytes_accessed=0, transcendentals=0)
NT = (((1,), (1,)), ((), ()))
NN = (((1,), (0,)), ((), ()))


def prepare_kernel(chol_ref, block_ref, turned_ref):
    _, listed, vectors, occupied, width = chol_ref.shape
    for m in range(listed):
        tile = chol_ref[0, m].reshape(vectors * occupied, width)
        block_ref[:, m * width:(m + 1) * width] = tile
        turned_ref[m * width:(m + 1) * width, :] = tile.T


def prepare_block(chol_tiles):
    _, listed, vectors, occupied, width = chol_tiles.shape
    rows, depth = vectors * occupied, listed * width
    return pl.pallas_call(
        prepare_kernel,
        in_specs=[VMEM],
        out_specs=[VMEM, VMEM],
        out_shape=[
            jax.ShapeDtypeStruct((rows, depth), chol_tiles.dtype),
            jax.ShapeDtypeStruct((depth, rows), chol_tiles.dtype),
        ],
        compiler_params=PARAMS,
        cost_estimate=SMALL,
        name="prepare_block",
    )(chol_tiles)


def pick_kernel(list_ref, theta_ref, *out_refs):
    listed = list_ref.shape[0]
    width = out_refs[0].shape[2] // listed
    me = lax.axis_index("chol")
    for offset, out_ref in enumerate(out_refs):
        device = me ^ (offset * CORES)
        for b, group in enumerate((device, device ^ 1)):
            for m in range(listed):
                start = pl.multiple_of(list_ref[m, group] * width, width)
                out_ref[b, :, m * width:(m + 1) * width] = theta_ref[0, :, pl.ds(start, width)]


def pick_tiles(listing, theta, depth, count):
    piece = jax.ShapeDtypeStruct((CORES, theta.shape[1], depth), theta.dtype)
    return pl.pallas_call(
        pick_kernel,
        in_specs=[SMEM, VMEM],
        out_specs=[VMEM] * count,
        out_shape=[piece] * count,
        compiler_params=PARAMS,
        cost_estimate=SMALL,
        name="pick_tiles",
    )(listing, theta)


def fold_rows(blocks, sub):
    high = sub < 4
    pairs = []
    for i in range(4):
        a, b = blocks[i], blocks[i + 4]
        pairs.append(jnp.where(high, a, b) + pltpu.roll(jnp.where(high, b, a), 4, 0))
    for shift in (2, 1):
        first = sub % (2 * shift) < shift
        half = len(pairs) // 2
        pairs = [
            jnp.where(
                first,
                pairs[i] + pltpu.roll(pairs[i], 8 - shift, 0),
                pairs[i + half] + pltpu.roll(pairs[i + half], shift, 0),
            )
            for i in range(half)
        ]
    return pairs[0]


def chunk_products(block_ref, turned_ref, theta, occupied, k0, size, by_matmul):
    span = slice(k0 * occupied, (k0 + size) * occupied)
    inner_mat = lax.dot_general(block_ref[span, :], theta, NT, preferred_element_type=jnp.float32)
    if not by_matmul:
        return inner_mat, None
    turned = slice(k0 * occupied, (k0 + by_matmul) * occupied)
    return inner_mat, lax.dot_general(theta, turned_ref[:, turned], NN, preferred_element_type=jnp.float32)


def chunk_terms(inner_mat, flipped, cross, store_rows, occupied, k0, size, by_matmul):
    tiles = inner_mat.shape[1] // LANES

    low = lax.broadcasted_iota(jnp.int32, (occupied, LANES), 1) < occupied
    sub8 = lax.broadcasted_iota(jnp.int32, (8, LANES), 0)
    lane8 = lax.broadcasted_iota(jnp.int32, (8, LANES), 1)
    strip = (lane8 % occupied) // 8
    on_diag = lane8 % 8 == sub8

    def diagonal(block):
        merged = block[:8]
        for r in range(1, occupied // 8):
            merged = jnp.where(strip == r, block[8 * r:8 * r + 8], merged)
        return jnp.where(on_diag, merged, 0.0)

    for k8 in range(0, size, 8):
        for t in range(tiles):
            c0 = t * LANES
            diagonals = []
            for k in range(k8, k8 + 8, 2):
                r0 = k * occupied
                top = inner_mat[r0:r0 + occupied, c0:c0 + LANES]
                bottom = inner_mat[r0 + occupied:r0 + 2 * occupied, c0:c0 + LANES]
                if k < by_matmul:
                    other = flipped[c0:c0 + LANES, r0:r0 + LANES]
                else:
                    other = inner_mat[r0:r0 + LANES, c0:c0 + LANES].T
                f_top, f_bottom = other[:occupied], other[occupied:]
                swapped = pltpu.roll(jnp.where(low, f_bottom, f_top), occupied, 1)
                product = jnp.where(low, top, bottom) * jnp.where(low, f_top, f_bottom)
                product = product + jnp.where(low, bottom, top) * swapped
                cross[t] = cross[t] + jnp.sum(product.reshape(occupied // 8, 8, LANES), axis=0)
                diagonals.append(diagonal(top))
                diagonals.append(diagonal(bottom))
            store_rows(k0 + k8, t, fold_rows(diagonals, sub8))


def mask_kernel_rows(screen_refs, listed, width):
    return [
        jnp.concatenate(
            [jnp.full((1, width), ref[0, m].astype(jnp.float32)) for m in range(listed)], axis=1
        )
        for ref in screen_refs
    ]


def terms_kernel(*refs, first, count, screened, chunks, vectors, batch):
    if screened:
        screen_refs, refs = refs[:2], refs[2:]
    else:
        mask_ref, carried_ref, refs = refs[0], refs[1], refs[2:]
    block_refs, theta_refs, rest = refs[:4], refs[4:4 + count], refs[4 + count:]
    out_ref, picked_ref, rows_ref = rest[0], rest[-2], rest[-1]
    occupied = block_refs[0].shape[0] // vectors
    depth = block_refs[0].shape[1]
    used = CORES * vectors
    columns = batch * occupied
    tiles = columns // LANES
    me = lax.axis_index("chol")
    core = lax.rem(me, CORES)
    chip = me // CORES

    if screened:
        listed = screen_refs[0].shape[1]
        masks = mask_kernel_rows(screen_refs, listed, depth // listed)
        mask_ref = rest[1]
        for b in range(CORES):
            mask_ref[b:b + 1, :] = masks[b]
        out_ref[...] = jnp.zeros(out_ref.shape, out_ref.dtype)
    else:
        masks = [mask_ref[b:b + 1, :] for b in range(CORES)]
        out_ref[...] = carried_ref[...]
    for b in range(CORES):
        mask = masks[b].astype(picked_ref.dtype)
        for i, ref in enumerate(theta_refs):
            picked_ref[b, i * occupied:(i + 1) * occupied, :] = ref[b] * mask

    def one_batch(index):
        start = index * occupied
        rows = pl.ds(start if isinstance(index, int) else pl.multiple_of(start, columns), columns)
        cross = [jnp.zeros((8, LANES), jnp.float32) for _ in range(tiles)]
        tasks = []
        for b in range(CORES):
            theta, k0 = picked_ref[b, rows, :], 0
            while k0 < vectors:
                for size, by_matmul in chunks:
                    tasks.append((b, theta, k0, size, by_matmul))
                    k0 += size

        def products(task):
            b, theta, k0, size, by_matmul = task
            return chunk_products(block_refs[2 * b], block_refs[2 * b + 1], theta, occupied, k0, size, by_matmul)

        ahead = products(tasks[0])
        for i, (b, _, k0, size, by_matmul) in enumerate(tasks):
            now, ahead = ahead, products(tasks[i + 1]) if i + 1 < len(tasks) else None
            place = (core ^ b) * vectors

            def store_rows(k, t, value, place=place):
                rows_ref[pl.ds(pl.multiple_of(place + k, 8), 8), t * LANES:(t + 1) * LANES] = value

            chunk_terms(*now, cross, store_rows, occupied, k0, size, by_matmul)
        for t in range(tiles):
            rows_ref[used:used + 8, t * LANES:(t + 1) * LANES] = cross[t]
        values = rows_ref[...]
        parts = []
        for _ in range(3):
            part = values.astype(jnp.bfloat16)
            parts.append(part)
            values = values - part.astype(jnp.float32)
        seg_row = lax.broadcasted_iota(jnp.int32, (8, columns), 0)
        seg_col = lax.broadcasted_iota(jnp.int32, (8, columns), 1)
        segment = jnp.where(seg_col // occupied == seg_row, 1.0, 0.0).astype(jnp.bfloat16)
        sums = sum(
            lax.dot_general(segment, part, NT, preferred_element_type=jnp.float32) for part in parts
        )
        for i in range(batch):
            owner = chip ^ (first + index + i)
            out_ref[pl.ds(owner, 1), 0, :used + 8] = sums[i:i + 1]

    if count == batch:
        one_batch(0)
    else:
        @pl.loop(0, count // batch)
        def _(step):
            one_batch(step * batch)


def chip_terms(screens, so_far, blocks, thetas, first, chunks, vectors, chips, out_width):
    count = len(thetas)
    batch = min(count, BATCH)
    rows, depth = blocks[0].shape
    occupied = rows // vectors
    vector_operands = [*so_far, *blocks, *thetas]
    out_shape = [jax.ShapeDtypeStruct((chips, 1, out_width), jnp.float32)]
    if screens:
        out_shape.append(jax.ShapeDtypeStruct((CORES, depth), jnp.float32))
    return pl.pallas_call(
        functools.partial(
            terms_kernel, first=first, count=count, screened=bool(screens), chunks=chunks, vectors=vectors, batch=batch
        ),
        in_specs=[SMEM] * len(screens) + [VMEM] * len(vector_operands),
        out_specs=[VMEM] * len(out_shape),
        out_shape=out_shape,
        scratch_shapes=[
            pltpu.VMEM((CORES, count * occupied, depth), thetas[0].dtype),
            pltpu.VMEM((CORES * vectors + 8, batch * occupied), jnp.float32),
        ],
        compiler_params=PARAMS,
        cost_estimate=SMALL,
        name="chip_terms",
    )(*screens, *vector_operands)


def energy_terms(rows, used):
    lane = lax.broadcasted_iota(jnp.int32, rows.shape, 1)
    return jnp.where(lane < used, rows * rows, jnp.where(lane < used + 8, -rows, 0.0))


def finish_kernel(rows_ref, bias_ref, energy_ref, bias_buf, energy_buf, sems, *, used, scale):
    chips, _, width = rows_ref.shape
    fit = LANES // used if width == LANES else 0
    lane = lax.broadcasted_iota(jnp.int32, (1, width), 1)
    if fit and chips % fit == 0:
        for d in range(0, chips, fit):
            packed = rows_ref[d]
            for i in range(1, fit):
                packed = jnp.where(lane < i * used, packed, pltpu.roll(rows_ref[d + i], i * used, 1))
            bias_buf[:, d * used:(d + fit) * used] = packed
    else:
        for d in range(chips):
            bias_buf[:, d * used:(d + 1) * used] = rows_ref[d, :, :used]
    bias_copy = pltpu.make_async_copy(bias_buf, bias_ref, sems.at[0])
    bias_copy.start()
    total = energy_terms(rows_ref[0], used)
    for d in range(1, chips):
        total = total + energy_terms(rows_ref[d], used)
    energy_buf[...] = jnp.sum(total, axis=1, keepdims=True) * scale
    energy_copy = pltpu.make_async_copy(energy_buf, energy_ref, sems.at[1])
    energy_copy.start(priority=1)
    bias_copy.wait()
    energy_copy.wait()


def finish(rows, used, scale):
    chips = rows.shape[0]
    shapes = [(1, chips * used), (1, 1)]
    force_bias, energy = pl.pallas_call(
        functools.partial(finish_kernel, used=used, scale=scale),
        in_specs=[VMEM],
        out_specs=[pl.BlockSpec(memory_space=pl.ANY)] * 2,
        out_shape=[jax.ShapeDtypeStruct(s, jnp.float32) for s in shapes],
        scratch_shapes=[pltpu.VMEM(s, jnp.float32) for s in shapes] + [pltpu.SemaphoreType.DMA((2,))],
        name="finish",
    )(rows)
    return force_bias, energy.reshape(1)


def body(theta, chol_tiles, screen, tile_list):
    groups = lax.axis_size("chol")
    chips = groups // CORES
    half = chips // 2
    _, occupied, _ = theta.shape
    vectors = chol_tiles.shape[2]
    used = CORES * vectors
    out_width = LANES * ((used + 8 + LANES - 1) // LANES)
    depth = chol_tiles.shape[1] * chol_tiles.shape[4]
    listing = tile_list.T

    def to_chip(x, offset):
        return lax.ppermute(x, "chol", [(i, i ^ (offset * CORES)) for i in range(groups)])

    def to_core(x):
        return lax.ppermute(x, "chol", [(i, i ^ 1) for i in range(groups)])

    far = to_chip(theta, half)

    def spread(walker):
        pieces = pick_tiles(listing, walker, depth, half)
        return [pieces[0]] + [to_chip(pieces[offset], offset) for offset in range(1, half)]

    near = spread(theta)
    own, own_turned = prepare_block(chol_tiles)
    other_chol = to_core(chol_tiles)
    far, near[1], other_chol, own = lax.optimization_barrier((far, near[1], other_chol, own))
    beyond = spread(far)
    other_chol, late_screen, near[-1] = lax.optimization_barrier((other_chol, screen, near[-1]))
    other, other_turned = prepare_block(other_chol)
    blocks = [own, own_turned, other, other_turned]

    screens = [screen, to_core(late_screen)]
    rows, masks = chip_terms(screens, [], blocks, near, 0, NEAR, vectors, chips, out_width)
    rows, = chip_terms([], [masks, rows], blocks, beyond, half, BEYOND, vectors, chips, out_width)
    same_core = [list(range(core, groups, CORES)) for core in range(CORES)]
    back = lax.all_to_all(rows, "chol", split_axis=0, concat_axis=0, tiled=True, axis_index_groups=same_core)
    return finish(back, used, 1.0 / (2.0 * occupied * occupied))


def solution(mesh):
    in_specs = (
        P(("grp", "chol"), None, None),
        P("chol", None, None, None, None),
        P("chol", None),
        P(),
    )
    out_specs = (P(("grp", "chol"), None), P(("grp", "chol")))
    return jax.shard_map(body, mesh=mesh, in_specs=in_specs, out_specs=out_specs, check_vma=False)
```

```python
import functools

import jax
import jax.numpy as jnp
from jax import lax
from jax.experimental import pallas as pl
from jax.experimental.pallas import tpu as pltpu
from jax.sharding import PartitionSpec as P

LANES = 128
CORES = 2
VMEM_LIMIT = 32 * 1024 * 1024
NEAR = ((8, 4),)
BEYOND = ((8, 8), (8, 0))
BATCH = 4
VMEM = pl.BlockSpec(memory_space=pltpu.VMEM)
SMEM = pl.BlockSpec(memory_space=pltpu.SMEM)
PARAMS = pltpu.CompilerParams(vmem_limit_bytes=VMEM_LIMIT)
SMALL = pl.CostEstimate(flops=0, bytes_accessed=0, transcendentals=0)
NT = (((1,), (1,)), ((), ()))
NN = (((1,), (0,)), ((), ()))


def prepare_kernel(chol_ref, block_ref, turned_ref):
    _, listed, vectors, occupied, width = chol_ref.shape
    for m in range(listed):
        tile = chol_ref[0, m].reshape(vectors * occupied, width)
        block_ref[:, m * width:(m + 1) * width] = tile
        turned_ref[m * width:(m + 1) * width, :] = tile.T


def prepare_block(chol_tiles):
    _, listed, vectors, occupied, width = chol_tiles.shape
    rows, depth = vectors * occupied, listed * width
    return pl.pallas_call(
        prepare_kernel,
        in_specs=[VMEM],
        out_specs=[VMEM, VMEM],
        out_shape=[
            jax.ShapeDtypeStruct((rows, depth), chol_tiles.dtype),
            jax.ShapeDtypeStruct((depth, rows), chol_tiles.dtype),
        ],
        compiler_params=PARAMS,
        cost_estimate=SMALL,
        name="prepare_block",
    )(chol_tiles)


def pick_kernel(list_ref, theta_ref, *out_refs):
    listed = list_ref.shape[0]
    width = out_refs[0].shape[2] // listed
    me = lax.axis_index("chol")
    for offset, out_ref in enumerate(out_refs):
        device = me ^ (offset * CORES)
        for b, group in enumerate((device, device ^ 1)):
            for m in range(listed):
                start = pl.multiple_of(list_ref[m, group] * width, width)
                out_ref[b, :, m * width:(m + 1) * width] = theta_ref[0, :, pl.ds(start, width)]


def pick_tiles(listing, theta, depth, count):
    piece = jax.ShapeDtypeStruct((CORES, theta.shape[1], depth), theta.dtype)
    return pl.pallas_call(
        pick_kernel,
        in_specs=[SMEM, VMEM],
        out_specs=[VMEM] * count,
        out_shape=[piece] * count,
        compiler_params=PARAMS,
        cost_estimate=SMALL,
        name="pick_tiles",
    )(listing, theta)


def fold_rows(blocks, sub):
    high = sub < 4
    pairs = []
    for i in range(4):
        a, b = blocks[i], blocks[i + 4]
        pairs.append(jnp.where(high, a, b) + pltpu.roll(jnp.where(high, b, a), 4, 0))
    for shift in (2, 1):
        first = sub % (2 * shift) < shift
        half = len(pairs) // 2
        pairs = [
            jnp.where(
                first,
                pairs[i] + pltpu.roll(pairs[i], 8 - shift, 0),
                pairs[i + half] + pltpu.roll(pairs[i + half], shift, 0),
            )
            for i in range(half)
        ]
    return pairs[0]


def chunk_products(block_ref, turned_ref, theta, theta_turned, occupied, k0, size, by_matmul):
    span = slice(k0 * occupied, (k0 + size) * occupied)
    inner_mat = lax.dot_general(block_ref[span, :], theta_turned, NN, preferred_element_type=jnp.float32)
    if not by_matmul:
        return inner_mat, None
    turned = slice(k0 * occupied, (k0 + by_matmul) * occupied)
    return inner_mat, lax.dot_general(theta, turned_ref[:, turned], NN, preferred_element_type=jnp.float32)


def chunk_terms(inner_mat, flipped, cross, store_rows, occupied, k0, size, by_matmul):
    tiles = inner_mat.shape[1] // LANES

    low = lax.broadcasted_iota(jnp.int32, (occupied, LANES), 1) < occupied
    sub8 = lax.broadcasted_iota(jnp.int32, (8, LANES), 0)
    lane8 = lax.broadcasted_iota(jnp.int32, (8, LANES), 1)
    strip = (lane8 % occupied) // 8
    on_diag = lane8 % 8 == sub8

    def diagonal(block):
        merged = block[:8]
        for r in range(1, occupied // 8):
            merged = jnp.where(strip == r, block[8 * r:8 * r + 8], merged)
        return jnp.where(on_diag, merged, 0.0)

    for k8 in range(0, size, 8):
        for t in range(tiles):
            c0 = t * LANES
            diagonals = []
            for k in range(k8, k8 + 8, 2):
                r0 = k * occupied
                top = inner_mat[r0:r0 + occupied, c0:c0 + LANES]
                bottom = inner_mat[r0 + occupied:r0 + 2 * occupied, c0:c0 + LANES]
                if k < by_matmul:
                    other = flipped[c0:c0 + LANES, r0:r0 + LANES]
                else:
                    other = inner_mat[r0:r0 + LANES, c0:c0 + LANES].T
                f_top, f_bottom = other[:occupied], other[occupied:]
                swapped = pltpu.roll(jnp.where(low, f_bottom, f_top), occupied, 1)
                product = jnp.where(low, top, bottom) * jnp.where(low, f_top, f_bottom)
                product = product + jnp.where(low, bottom, top) * swapped
                cross[t] = cross[t] + jnp.sum(product.reshape(occupied // 8, 8, LANES), axis=0)
                diagonals.append(diagonal(top))
                diagonals.append(diagonal(bottom))
            store_rows(k0 + k8, t, fold_rows(diagonals, sub8))


def mask_kernel_rows(screen_refs, listed, width):
    return [
        jnp.concatenate(
            [jnp.full((1, width), ref[0, m].astype(jnp.float32)) for m in range(listed)], axis=1
        )
        for ref in screen_refs
    ]


def terms_kernel(*refs, first, count, screened, chunks, vectors, batch):
    if screened:
        screen_refs, refs = refs[:2], refs[2:]
    else:
        mask_ref, carried_ref, refs = refs[0], refs[1], refs[2:]
    block_refs, theta_refs, rest = refs[:4], refs[4:4 + count], refs[4 + count:]
    out_ref, picked_ref, rows_ref = rest[0], rest[-2], rest[-1]
    occupied = block_refs[0].shape[0] // vectors
    depth = block_refs[0].shape[1]
    used = CORES * vectors
    columns = batch * occupied
    tiles = columns // LANES
    me = lax.axis_index("chol")
    core = lax.rem(me, CORES)
    chip = me // CORES

    if screened:
        listed = screen_refs[0].shape[1]
        masks = mask_kernel_rows(screen_refs, listed, depth // listed)
        mask_ref = rest[1]
        for b in range(CORES):
            mask_ref[b:b + 1, :] = masks[b]
        out_ref[...] = jnp.zeros(out_ref.shape, out_ref.dtype)
    else:
        masks = [mask_ref[b:b + 1, :] for b in range(CORES)]
        out_ref[...] = carried_ref[...]
    for b in range(CORES):
        mask = masks[b].astype(picked_ref.dtype)
        for i, ref in enumerate(theta_refs):
            picked_ref[b, i * occupied:(i + 1) * occupied, :] = ref[b] * mask

    def one_batch(index):
        start = index * occupied
        rows = pl.ds(start if isinstance(index, int) else pl.multiple_of(start, columns), columns)
        cross = [jnp.zeros((8, LANES), jnp.float32) for _ in range(tiles)]
        tasks = []
        for b in range(CORES):
            theta, k0 = picked_ref[b, rows, :], 0
            walkers = (theta, theta.T)
            while k0 < vectors:
                for size, by_matmul in chunks:
                    tasks.append((b, walkers, k0, size, by_matmul))
                    k0 += size

        def products(task):
            b, walkers, k0, size, by_matmul = task
            return chunk_products(block_refs[2 * b], block_refs[2 * b + 1], *walkers, occupied, k0, size, by_matmul)

        ahead = products(tasks[0])
        for i, (b, _, k0, size, by_matmul) in enumerate(tasks):
            now, ahead = ahead, products(tasks[i + 1]) if i + 1 < len(tasks) else None
            place = (core ^ b) * vectors

            def store_rows(k, t, value, place=place):
                rows_ref[pl.ds(pl.multiple_of(place + k, 8), 8), t * LANES:(t + 1) * LANES] = value

            chunk_terms(*now, cross, store_rows, occupied, k0, size, by_matmul)
        for t in range(tiles):
            rows_ref[used:used + 8, t * LANES:(t + 1) * LANES] = cross[t]
        values = rows_ref[...]
        parts = []
        for _ in range(3):
            part = values.astype(jnp.bfloat16)
            parts.append(part)
            values = values - part.astype(jnp.float32)
        seg_row = lax.broadcasted_iota(jnp.int32, (8, columns), 0)
        seg_col = lax.broadcasted_iota(jnp.int32, (8, columns), 1)
        segment = jnp.where(seg_col // occupied == seg_row, 1.0, 0.0).astype(jnp.bfloat16)
        sums = sum(
            lax.dot_general(segment, part, NT, preferred_element_type=jnp.float32) for part in parts
        )
        for i in range(batch):
            owner = chip ^ (first + index + i)
            out_ref[pl.ds(owner, 1), 0, :used + 8] = sums[i:i + 1]

    if count == batch:
        one_batch(0)
    else:
        @pl.loop(0, count // batch)
        def _(step):
            one_batch(step * batch)


def chip_terms(screens, so_far, blocks, thetas, first, chunks, vectors, chips, out_width):
    count = len(thetas)
    batch = min(count, BATCH)
    rows, depth = blocks[0].shape
    occupied = rows // vectors
    vector_operands = [*so_far, *blocks, *thetas]
    out_shape = [jax.ShapeDtypeStruct((chips, 1, out_width), jnp.float32)]
    if screens:
        out_shape.append(jax.ShapeDtypeStruct((CORES, depth), jnp.float32))
    return pl.pallas_call(
        functools.partial(
            terms_kernel, first=first, count=count, screened=bool(screens), chunks=chunks, vectors=vectors, batch=batch
        ),
        in_specs=[SMEM] * len(screens) + [VMEM] * len(vector_operands),
        out_specs=[VMEM] * len(out_shape),
        out_shape=out_shape,
        scratch_shapes=[
            pltpu.VMEM((CORES, count * occupied, depth), thetas[0].dtype),
            pltpu.VMEM((CORES * vectors + 8, batch * occupied), jnp.float32),
        ],
        compiler_params=PARAMS,
        cost_estimate=SMALL,
        name="chip_terms",
    )(*screens, *vector_operands)


def energy_terms(rows, used):
    lane = lax.broadcasted_iota(jnp.int32, rows.shape, 1)
    return jnp.where(lane < used, rows * rows, jnp.where(lane < used + 8, -rows, 0.0))


def finish_kernel(rows_ref, bias_ref, energy_ref, bias_buf, energy_buf, sems, *, used, scale):
    chips, _, width = rows_ref.shape
    fit = LANES // used if width == LANES else 0
    lane = lax.broadcasted_iota(jnp.int32, (1, width), 1)
    if fit and chips % fit == 0:
        for d in range(0, chips, fit):
            packed = rows_ref[d]
            for i in range(1, fit):
                packed = jnp.where(lane < i * used, packed, pltpu.roll(rows_ref[d + i], i * used, 1))
            bias_buf[:, d * used:(d + fit) * used] = packed
    else:
        for d in range(chips):
            bias_buf[:, d * used:(d + 1) * used] = rows_ref[d, :, :used]
    bias_copy = pltpu.make_async_copy(bias_buf, bias_ref, sems.at[0])
    bias_copy.start()
    total = energy_terms(rows_ref[0], used)
    for d in range(1, chips):
        total = total + energy_terms(rows_ref[d], used)
    energy_buf[...] = jnp.sum(total, axis=1, keepdims=True) * scale
    energy_copy = pltpu.make_async_copy(energy_buf, energy_ref, sems.at[1])
    energy_copy.start()
    bias_copy.wait()
    energy_copy.wait()


def finish(rows, used, scale):
    chips = rows.shape[0]
    shapes = [(1, chips * used), (1, 1)]
    force_bias, energy = pl.pallas_call(
        functools.partial(finish_kernel, used=used, scale=scale),
        in_specs=[VMEM],
        out_specs=[pl.BlockSpec(memory_space=pl.ANY)] * 2,
        out_shape=[jax.ShapeDtypeStruct(s, jnp.float32) for s in shapes],
        scratch_shapes=[pltpu.VMEM(s, jnp.float32) for s in shapes] + [pltpu.SemaphoreType.DMA((2,))],
        name="finish",
    )(rows)
    return force_bias, energy.reshape(1)


def body(theta, chol_tiles, screen, tile_list):
    groups = lax.axis_size("chol")
    chips = groups // CORES
    half = chips // 2
    _, occupied, _ = theta.shape
    vectors = chol_tiles.shape[2]
    used = CORES * vectors
    out_width = LANES * ((used + 8 + LANES - 1) // LANES)
    depth = chol_tiles.shape[1] * chol_tiles.shape[4]
    listing = tile_list.T

    def to_chip(x, offset):
        return lax.ppermute(x, "chol", [(i, i ^ (offset * CORES)) for i in range(groups)])

    def to_core(x):
        return lax.ppermute(x, "chol", [(i, i ^ 1) for i in range(groups)])

    far = to_chip(theta, half)

    def spread(walker):
        pieces = pick_tiles(listing, walker, depth, half)
        return [pieces[0]] + [to_chip(pieces[offset], offset) for offset in range(1, half)]

    near = spread(theta)
    own, own_turned = prepare_block(chol_tiles)
    other_chol = to_core(chol_tiles)
    far, near[1], other_chol, own = lax.optimization_barrier((far, near[1], other_chol, own))
    beyond = spread(far)
    other_chol, late_screen, near[-1] = lax.optimization_barrier((other_chol, screen, near[-1]))
    other, other_turned = prepare_block(other_chol)
    blocks = [own, own_turned, other, other_turned]

    screens = [screen, to_core(late_screen)]
    rows, masks = chip_terms(screens, [], blocks, near, 0, NEAR, vectors, chips, out_width)
    rows, = chip_terms([], [masks, rows], blocks, beyond, half, BEYOND, vectors, chips, out_width)
    same_core = [list(range(core, groups, CORES)) for core in range(CORES)]
    back = lax.all_to_all(rows, "chol", split_axis=0, concat_axis=0, tiled=True, axis_index_groups=same_core)
    return finish(back, used, 1.0 / (2.0 * occupied * occupied))


def solution(mesh):
    in_specs = (
        P(("grp", "chol"), None, None),
        P("chol", None, None, None, None),
        P("chol", None),
        P(),
    )
    out_specs = (P(("grp", "chol"), None), P(("grp", "chol")))
    return jax.shard_map(body, mesh=mesh, in_specs=in_specs, out_specs=out_specs, check_vma=False)
```

```python
import functools

import jax
import jax.numpy as jnp
from jax import lax
from jax.experimental import pallas as pl
from jax.experimental.pallas import tpu as pltpu
from jax.sharding import PartitionSpec as P

LANES = 128
CORES = 2
VMEM_LIMIT = 32 * 1024 * 1024
NEAR = ((8, 4),)
BEYOND = ((8, 8), (8, 0))
BATCH = 4
VMEM = pl.BlockSpec(memory_space=pltpu.VMEM)
SMEM = pl.BlockSpec(memory_space=pltpu.SMEM)
PARAMS = pltpu.CompilerParams(vmem_limit_bytes=VMEM_LIMIT)
SMALL = pl.CostEstimate(flops=0, bytes_accessed=0, transcendentals=0)
NT = (((1,), (1,)), ((), ()))
NN = (((1,), (0,)), ((), ()))


def prepare_kernel(chol_ref, block_ref, turned_ref):
    _, listed, vectors, occupied, width = chol_ref.shape
    for m in range(listed):
        tile = chol_ref[0, m].reshape(vectors * occupied, width)
        block_ref[:, m * width:(m + 1) * width] = tile
        turned_ref[m * width:(m + 1) * width, :] = tile.T


def prepare_block(chol_tiles):
    _, listed, vectors, occupied, width = chol_tiles.shape
    rows, depth = vectors * occupied, listed * width
    return pl.pallas_call(
        prepare_kernel,
        in_specs=[VMEM],
        out_specs=[VMEM, VMEM],
        out_shape=[
            jax.ShapeDtypeStruct((rows, depth), chol_tiles.dtype),
            jax.ShapeDtypeStruct((depth, rows), chol_tiles.dtype),
        ],
        compiler_params=PARAMS,
        cost_estimate=SMALL,
        name="prepare_block",
    )(chol_tiles)


def pick_kernel(list_ref, theta_ref, *out_refs):
    listed = list_ref.shape[0]
    width = out_refs[0].shape[2] // listed
    me = lax.axis_index("chol")
    for offset, out_ref in enumerate(out_refs):
        device = me ^ (offset * CORES)
        for b, group in enumerate((device, device ^ 1)):
            for m in range(listed):
                start = pl.multiple_of(list_ref[m, group] * width, width)
                out_ref[b, :, m * width:(m + 1) * width] = theta_ref[0, :, pl.ds(start, width)]


def pick_tiles(listing, theta, depth, count):
    piece = jax.ShapeDtypeStruct((CORES, theta.shape[1], depth), theta.dtype)
    return pl.pallas_call(
        pick_kernel,
        in_specs=[SMEM, VMEM],
        out_specs=[VMEM] * count,
        out_shape=[piece] * count,
        compiler_params=PARAMS,
        cost_estimate=SMALL,
        name="pick_tiles",
    )(listing, theta)


def fold_rows(blocks, sub):
    high = sub < 4
    pairs = []
    for i in range(4):
        a, b = blocks[i], blocks[i + 4]
        pairs.append(jnp.where(high, a, b) + pltpu.roll(jnp.where(high, b, a), 4, 0))
    for shift in (2, 1):
        first = sub % (2 * shift) < shift
        half = len(pairs) // 2
        pairs = [
            jnp.where(
                first,
                pairs[i] + pltpu.roll(pairs[i], 8 - shift, 0),
                pairs[i + half] + pltpu.roll(pairs[i + half], shift, 0),
            )
            for i in range(half)
        ]
    return pairs[0]


def chunk_products(block_ref, turned_ref, theta, theta_turned, occupied, k0, size, by_matmul):
    span = slice(k0 * occupied, (k0 + size) * occupied)
    inner_mat = lax.dot_general(block_ref[span, :], theta_turned, NN, preferred_element_type=jnp.float32)
    if not by_matmul:
        return inner_mat, None
    turned = slice(k0 * occupied, (k0 + by_matmul) * occupied)
    return inner_mat, lax.dot_general(theta, turned_ref[:, turned], NN, preferred_element_type=jnp.float32)


def chunk_terms(inner_mat, flipped, cross, store_rows, occupied, k0, size, by_matmul):
    tiles = inner_mat.shape[1] // LANES

    low = lax.broadcasted_iota(jnp.int32, (occupied, LANES), 1) < occupied
    sub8 = lax.broadcasted_iota(jnp.int32, (8, LANES), 0)
    lane8 = lax.broadcasted_iota(jnp.int32, (8, LANES), 1)
    strip = (lane8 % occupied) // 8
    on_diag = lane8 % 8 == sub8

    def diagonal(block):
        merged = block[:8]
        for r in range(1, occupied // 8):
            merged = jnp.where(strip == r, block[8 * r:8 * r + 8], merged)
        return jnp.where(on_diag, merged, 0.0)

    for k8 in range(0, size, 8):
        for t in range(tiles):
            c0 = t * LANES
            diagonals = []
            for k in range(k8, k8 + 8, 2):
                r0 = k * occupied
                top = inner_mat[r0:r0 + occupied, c0:c0 + LANES]
                bottom = inner_mat[r0 + occupied:r0 + 2 * occupied, c0:c0 + LANES]
                if k < by_matmul:
                    other = flipped[c0:c0 + LANES, r0:r0 + LANES]
                else:
                    other = inner_mat[r0:r0 + LANES, c0:c0 + LANES].T
                f_top, f_bottom = other[:occupied], other[occupied:]
                swapped = pltpu.roll(jnp.where(low, f_bottom, f_top), occupied, 1)
                product = jnp.where(low, top, bottom) * jnp.where(low, f_top, f_bottom)
                product = product + jnp.where(low, bottom, top) * swapped
                cross[t] = cross[t] + jnp.sum(product.reshape(occupied // 8, 8, LANES), axis=0)
                diagonals.append(diagonal(top))
                diagonals.append(diagonal(bottom))
            store_rows(k0 + k8, t, fold_rows(diagonals, sub8))


def mask_kernel_rows(screen_refs, listed, width):
    return [
        jnp.concatenate(
            [jnp.full((1, width), ref[0, m].astype(jnp.float32)) for m in range(listed)], axis=1
        )
        for ref in screen_refs
    ]


def terms_kernel(*refs, first, count, screened, chunks, vectors, batch):
    if screened:
        screen_refs, refs = refs[:2], refs[2:]
    else:
        mask_ref, carried_ref, refs = refs[0], refs[1], refs[2:]
    block_refs, theta_refs, rest = refs[:4], refs[4:4 + count], refs[4 + count:]
    out_ref, picked_ref, rows_ref = rest[0], rest[-2], rest[-1]
    occupied = block_refs[0].shape[0] // vectors
    depth = block_refs[0].shape[1]
    used = CORES * vectors
    columns = batch * occupied
    tiles = columns // LANES
    me = lax.axis_index("chol")
    core = lax.rem(me, CORES)
    chip = me // CORES

    if screened:
        listed = screen_refs[0].shape[1]
        masks = mask_kernel_rows(screen_refs, listed, depth // listed)
        mask_ref = rest[1]
        for b in range(CORES):
            mask_ref[b:b + 1, :] = masks[b]
        out_ref[...] = jnp.zeros(out_ref.shape, out_ref.dtype)
    else:
        masks = [mask_ref[b:b + 1, :] for b in range(CORES)]
        out_ref[...] = carried_ref[...]
    for b in range(CORES):
        mask = masks[b].astype(picked_ref.dtype)
        for i, ref in enumerate(theta_refs):
            picked_ref[b, i * occupied:(i + 1) * occupied, :] = ref[b] * mask

    def one_batch(index):
        start = index * occupied
        rows = pl.ds(start if isinstance(index, int) else pl.multiple_of(start, columns), columns)
        cross = [jnp.zeros((8, LANES), jnp.float32) for _ in range(tiles)]
        tasks = []
        for b in range(CORES):
            theta, k0 = picked_ref[b, rows, :], 0
            walkers = (theta, theta.T)
            while k0 < vectors:
                for size, by_matmul in chunks:
                    tasks.append((b, walkers, k0, size, by_matmul))
                    k0 += size

        def products(task):
            b, walkers, k0, size, by_matmul = task
            return chunk_products(block_refs[2 * b], block_refs[2 * b + 1], *walkers, occupied, k0, size, by_matmul)

        ahead = products(tasks[0])
        for i, (b, _, k0, size, by_matmul) in enumerate(tasks):
            now, ahead = ahead, products(tasks[i + 1]) if i + 1 < len(tasks) else None
            place = (core ^ b) * vectors

            def store_rows(k, t, value, place=place):
                rows_ref[pl.ds(pl.multiple_of(place + k, 8), 8), t * LANES:(t + 1) * LANES] = value

            chunk_terms(*now, cross, store_rows, occupied, k0, size, by_matmul)
        for t in range(tiles):
            rows_ref[used:used + 8, t * LANES:(t + 1) * LANES] = cross[t]
        values = rows_ref[...]
        parts = []
        for _ in range(3):
            part = values.astype(jnp.bfloat16)
            parts.append(part)
            values = values - part.astype(jnp.float32)
        seg_row = lax.broadcasted_iota(jnp.int32, (8, columns), 0)
        seg_col = lax.broadcasted_iota(jnp.int32, (8, columns), 1)
        segment = jnp.where(seg_col // occupied == seg_row, 1.0, 0.0).astype(jnp.bfloat16)
        sums = sum(
            lax.dot_general(segment, part, NT, preferred_element_type=jnp.float32) for part in parts
        )
        for i in range(batch):
            owner = chip ^ (first + index + i) ^ (out_ref.shape[0] // 2)
            out_ref[pl.ds(owner, 1), 0, :used + 8] = sums[i:i + 1]

    if count == batch:
        one_batch(0)
    else:
        @pl.loop(0, count // batch)
        def _(step):
            one_batch(step * batch)


def chip_terms(screens, so_far, blocks, thetas, first, chunks, vectors, chips, out_width):
    count = len(thetas)
    batch = min(count, BATCH)
    rows, depth = blocks[0].shape
    occupied = rows // vectors
    vector_operands = [*so_far, *blocks, *thetas]
    out_shape = [jax.ShapeDtypeStruct((chips, 1, out_width), jnp.float32)]
    if screens:
        out_shape.append(jax.ShapeDtypeStruct((CORES, depth), jnp.float32))
    return pl.pallas_call(
        functools.partial(
            terms_kernel, first=first, count=count, screened=bool(screens), chunks=chunks, vectors=vectors, batch=batch
        ),
        in_specs=[SMEM] * len(screens) + [VMEM] * len(vector_operands),
        out_specs=[VMEM] * len(out_shape),
        out_shape=out_shape,
        scratch_shapes=[
            pltpu.VMEM((CORES, count * occupied, depth), thetas[0].dtype),
            pltpu.VMEM((CORES * vectors + 8, batch * occupied), jnp.float32),
        ],
        compiler_params=PARAMS,
        cost_estimate=SMALL,
        name="chip_terms",
    )(*screens, *vector_operands)


def energy_terms(rows, used):
    lane = lax.broadcasted_iota(jnp.int32, rows.shape, 1)
    return jnp.where(lane < used, rows * rows, jnp.where(lane < used + 8, -rows, 0.0))


def finish_kernel(rows_ref, bias_ref, energy_ref, bias_buf, energy_buf, sems, *, used, scale):
    chips, _, width = rows_ref.shape
    half = chips // 2
    fit = LANES // used if width == LANES else 0
    lane = lax.broadcasted_iota(jnp.int32, (1, width), 1)
    if fit and chips % fit == 0:
        for d in range(0, chips, fit):
            packed = rows_ref[d ^ half]
            for i in range(1, fit):
                packed = jnp.where(lane < i * used, packed, pltpu.roll(rows_ref[(d + i) ^ half], i * used, 1))
            bias_buf[:, d * used:(d + fit) * used] = packed
    else:
        for d in range(chips):
            bias_buf[:, d * used:(d + 1) * used] = rows_ref[d ^ half, :, :used]
    bias_copy = pltpu.make_async_copy(bias_buf, bias_ref, sems.at[0])
    bias_copy.start()
    total = energy_terms(rows_ref[0], used)
    for d in range(1, chips):
        total = total + energy_terms(rows_ref[d], used)
    energy_buf[...] = jnp.sum(total, axis=1, keepdims=True) * scale
    energy_copy = pltpu.make_async_copy(energy_buf, energy_ref, sems.at[1])
    energy_copy.start()
    bias_copy.wait()
    energy_copy.wait()


def finish(rows, used, scale):
    chips = rows.shape[0]
    shapes = [(1, chips * used), (1, 1)]
    force_bias, energy = pl.pallas_call(
        functools.partial(finish_kernel, used=used, scale=scale),
        in_specs=[VMEM],
        out_specs=[pl.BlockSpec(memory_space=pl.ANY)] * 2,
        out_shape=[jax.ShapeDtypeStruct(s, jnp.float32) for s in shapes],
        scratch_shapes=[pltpu.VMEM(s, jnp.float32) for s in shapes] + [pltpu.SemaphoreType.DMA((2,))],
        name="finish",
    )(rows)
    return force_bias, energy.reshape(1)


def body(theta, chol_tiles, screen, tile_list):
    groups = lax.axis_size("chol")
    chips = groups // CORES
    half = chips // 2
    _, occupied, _ = theta.shape
    vectors = chol_tiles.shape[2]
    used = CORES * vectors
    out_width = LANES * ((used + 8 + LANES - 1) // LANES)
    depth = chol_tiles.shape[1] * chol_tiles.shape[4]
    listing = tile_list.T

    def to_chip(x, offset):
        return lax.ppermute(x, "chol", [(i, i ^ (offset * CORES)) for i in range(groups)])

    def to_core(x):
        return lax.ppermute(x, "chol", [(i, i ^ 1) for i in range(groups)])

    far = to_chip(theta, half)

    def spread(walker):
        pieces = pick_tiles(listing, walker, depth, half)
        return [pieces[0]] + [to_chip(pieces[offset], offset) for offset in range(1, half)]

    near = spread(theta)
    own, own_turned = prepare_block(chol_tiles)
    other_chol = to_core(chol_tiles)
    far, near[1], other_chol, own = lax.optimization_barrier((far, near[1], other_chol, own))
    beyond = spread(far)
    other_chol, late_screen, near[-1] = lax.optimization_barrier((other_chol, screen, near[-1]))
    other, other_turned = prepare_block(other_chol)
    blocks = [own, own_turned, other, other_turned]

    screens = [screen, to_core(late_screen)]
    rows, masks = chip_terms(screens, [], blocks, near, 0, NEAR, vectors, chips, out_width)
    rows, = chip_terms([], [masks, rows], blocks, beyond, half, BEYOND, vectors, chips, out_width)
    same_core = [[(rank ^ half) * CORES + core for rank in range(chips)] for core in range(CORES)]
    back = lax.all_to_all(rows, "chol", split_axis=0, concat_axis=0, tiled=True, axis_index_groups=same_core)
    return finish(back, used, 1.0 / (2.0 * occupied * occupied))


def solution(mesh):
    in_specs = (
        P(("grp", "chol"), None, None),
        P("chol", None, None, None, None),
        P("chol", None),
        P(),
    )
    out_specs = (P(("grp", "chol"), None), P(("grp", "chol")))
    return jax.shard_map(body, mesh=mesh, in_specs=in_specs, out_specs=out_specs, check_vma=False)
```

```python
import functools

import jax
import jax.numpy as jnp
from jax import lax
from jax.experimental import pallas as pl
from jax.experimental.pallas import tpu as pltpu
from jax.sharding import PartitionSpec as P

LANES = 128
CORES = 2
VMEM_LIMIT = 32 * 1024 * 1024
NEAR = ((8, 4),)
BEYOND = ((8, 8), (8, 0))
BATCH = 4
VMEM = pl.BlockSpec(memory_space=pltpu.VMEM)
SMEM = pl.BlockSpec(memory_space=pltpu.SMEM)
PARAMS = pltpu.CompilerParams(vmem_limit_bytes=VMEM_LIMIT)
SMALL = pl.CostEstimate(flops=0, bytes_accessed=0, transcendentals=0)
NT = (((1,), (1,)), ((), ()))
NN = (((1,), (0,)), ((), ()))


def prepare_kernel(chol_ref, block_ref, turned_ref):
    _, listed, vectors, occupied, width = chol_ref.shape
    for m in range(listed):
        tile = chol_ref[0, m].reshape(vectors * occupied, width)
        block_ref[:, m * width:(m + 1) * width] = tile
        turned_ref[m * width:(m + 1) * width, :] = tile.T


def prepare_block(chol_tiles):
    _, listed, vectors, occupied, width = chol_tiles.shape
    rows, depth = vectors * occupied, listed * width
    return pl.pallas_call(
        prepare_kernel,
        in_specs=[VMEM],
        out_specs=[VMEM, VMEM],
        out_shape=[
            jax.ShapeDtypeStruct((rows, depth), chol_tiles.dtype),
            jax.ShapeDtypeStruct((depth, rows), chol_tiles.dtype),
        ],
        compiler_params=PARAMS,
        cost_estimate=SMALL,
        name="prepare_block",
    )(chol_tiles)


def pick_kernel(list_ref, theta_ref, *out_refs):
    listed = list_ref.shape[0]
    width = out_refs[0].shape[2] // listed
    me = lax.axis_index("chol")
    for offset, out_ref in enumerate(out_refs):
        device = me ^ (offset * CORES)
        for b, group in enumerate((device, device ^ 1)):
            for m in range(listed):
                start = pl.multiple_of(list_ref[m, group] * width, width)
                out_ref[b, :, m * width:(m + 1) * width] = theta_ref[0, :, pl.ds(start, width)]


def pick_tiles(listing, theta, depth, count):
    piece = jax.ShapeDtypeStruct((CORES, theta.shape[1], depth), theta.dtype)
    return pl.pallas_call(
        pick_kernel,
        in_specs=[SMEM, VMEM],
        out_specs=[VMEM] * count,
        out_shape=[piece] * count,
        compiler_params=PARAMS,
        cost_estimate=SMALL,
        name="pick_tiles",
    )(listing, theta)


def fold_rows(blocks, sub):
    high = sub < 4
    pairs = []
    for i in range(4):
        a, b = blocks[i], blocks[i + 4]
        pairs.append(jnp.where(high, a, b) + pltpu.roll(jnp.where(high, b, a), 4, 0))
    for shift in (2, 1):
        first = sub % (2 * shift) < shift
        half = len(pairs) // 2
        pairs = [
            jnp.where(
                first,
                pairs[i] + pltpu.roll(pairs[i], 8 - shift, 0),
                pairs[i + half] + pltpu.roll(pairs[i + half], shift, 0),
            )
            for i in range(half)
        ]
    return pairs[0]


def chunk_products(block_ref, turned_ref, theta, theta_turned, occupied, k0, size, by_matmul):
    span = slice(k0 * occupied, (k0 + size) * occupied)
    inner_mat = lax.dot_general(block_ref[span, :], theta_turned, NN, preferred_element_type=jnp.float32)
    if not by_matmul:
        return inner_mat, None
    turned = slice(k0 * occupied, (k0 + by_matmul) * occupied)
    return inner_mat, lax.dot_general(theta, turned_ref[:, turned], NN, preferred_element_type=jnp.float32)


def chunk_terms(inner_mat, flipped, cross, store_rows, occupied, k0, size, by_matmul):
    tiles = inner_mat.shape[1] // LANES

    low = lax.broadcasted_iota(jnp.int32, (occupied, LANES), 1) < occupied
    sub8 = lax.broadcasted_iota(jnp.int32, (8, LANES), 0)
    lane8 = lax.broadcasted_iota(jnp.int32, (8, LANES), 1)
    strip = (lane8 % occupied) // 8
    on_diag = lane8 % 8 == sub8

    def diagonal(block):
        merged = block[:8]
        for r in range(1, occupied // 8):
            merged = jnp.where(strip == r, block[8 * r:8 * r + 8], merged)
        return jnp.where(on_diag, merged, 0.0)

    for k8 in range(0, size, 8):
        for t in range(tiles):
            c0 = t * LANES
            diagonals = []
            for k in range(k8, k8 + 8, 2):
                r0 = k * occupied
                top = inner_mat[r0:r0 + occupied, c0:c0 + LANES]
                bottom = inner_mat[r0 + occupied:r0 + 2 * occupied, c0:c0 + LANES]
                if k < by_matmul:
                    other = flipped[c0:c0 + LANES, r0:r0 + LANES]
                else:
                    other = inner_mat[r0:r0 + LANES, c0:c0 + LANES].T
                f_top, f_bottom = other[:occupied], other[occupied:]
                swapped = pltpu.roll(jnp.where(low, f_bottom, f_top), occupied, 1)
                product = jnp.where(low, top, bottom) * jnp.where(low, f_top, f_bottom)
                product = product + jnp.where(low, bottom, top) * swapped
                cross[t] = cross[t] + jnp.sum(product.reshape(occupied // 8, 8, LANES), axis=0)
                diagonals.append(diagonal(top))
                diagonals.append(diagonal(bottom))
            store_rows(k0 + k8, t, fold_rows(diagonals, sub8))


def send_order(place, count):
    return jnp.where(place == 0, 0, jnp.where(place == count - 1, 1, place + 1))


def mask_kernel_rows(screen_refs, listed, width):
    return [
        jnp.concatenate(
            [jnp.full((1, width), ref[0, m].astype(jnp.float32)) for m in range(listed)], axis=1
        )
        for ref in screen_refs
    ]


def terms_kernel(*refs, first, count, screened, chunks, vectors, batch):
    if screened:
        screen_refs, refs = refs[:2], refs[2:]
    else:
        mask_ref, carried_ref, refs = refs[0], refs[1], refs[2:]
    block_refs, theta_refs, rest = refs[:4], refs[4:4 + count], refs[4 + count:]
    out_ref, picked_ref, rows_ref = rest[0], rest[-2], rest[-1]
    occupied = block_refs[0].shape[0] // vectors
    depth = block_refs[0].shape[1]
    used = CORES * vectors
    columns = batch * occupied
    tiles = columns // LANES
    me = lax.axis_index("chol")
    core = lax.rem(me, CORES)
    chip = me // CORES

    if screened:
        listed = screen_refs[0].shape[1]
        masks = mask_kernel_rows(screen_refs, listed, depth // listed)
        mask_ref = rest[1]
        for b in range(CORES):
            mask_ref[b:b + 1, :] = masks[b]
        out_ref[...] = jnp.zeros(out_ref.shape, out_ref.dtype)
    else:
        masks = [mask_ref[b:b + 1, :] for b in range(CORES)]
        out_ref[...] = carried_ref[...]
    for b in range(CORES):
        mask = masks[b].astype(picked_ref.dtype)
        for i, ref in enumerate(theta_refs):
            picked_ref[b, i * occupied:(i + 1) * occupied, :] = ref[b] * mask

    def one_batch(index):
        start = index * occupied
        rows = pl.ds(start if isinstance(index, int) else pl.multiple_of(start, columns), columns)
        cross = [jnp.zeros((8, LANES), jnp.float32) for _ in range(tiles)]
        tasks = []
        for b in range(CORES):
            theta, k0 = picked_ref[b, rows, :], 0
            walkers = (theta, theta.T)
            while k0 < vectors:
                for size, by_matmul in chunks:
                    tasks.append((b, walkers, k0, size, by_matmul))
                    k0 += size

        def products(task):
            b, walkers, k0, size, by_matmul = task
            return chunk_products(block_refs[2 * b], block_refs[2 * b + 1], *walkers, occupied, k0, size, by_matmul)

        ahead = products(tasks[0])
        for i, (b, _, k0, size, by_matmul) in enumerate(tasks):
            now, ahead = ahead, products(tasks[i + 1]) if i + 1 < len(tasks) else None
            place = (core ^ b) * vectors

            def store_rows(k, t, value, place=place):
                rows_ref[pl.ds(pl.multiple_of(place + k, 8), 8), t * LANES:(t + 1) * LANES] = value

            chunk_terms(*now, cross, store_rows, occupied, k0, size, by_matmul)
        for t in range(tiles):
            rows_ref[used:used + 8, t * LANES:(t + 1) * LANES] = cross[t]
        values = rows_ref[...]
        parts = []
        for _ in range(3):
            part = values.astype(jnp.bfloat16)
            parts.append(part)
            values = values - part.astype(jnp.float32)
        seg_row = lax.broadcasted_iota(jnp.int32, (8, columns), 0)
        seg_col = lax.broadcasted_iota(jnp.int32, (8, columns), 1)
        segment = jnp.where(seg_col // occupied == seg_row, 1.0, 0.0).astype(jnp.bfloat16)
        sums = sum(
            lax.dot_general(segment, part, NT, preferred_element_type=jnp.float32) for part in parts
        )
        for i in range(batch):
            place = jnp.int32(index + i)
            if not screened:
                place = send_order(place, count)
            owner = chip ^ (first + place) ^ (out_ref.shape[0] // 2)
            out_ref[pl.ds(owner, 1), 0, :used + 8] = sums[i:i + 1]

    if count == batch:
        one_batch(0)
    else:
        @pl.loop(0, count // batch)
        def _(step):
            one_batch(step * batch)


def chip_terms(screens, so_far, blocks, thetas, first, chunks, vectors, chips, out_width):
    count = len(thetas)
    batch = min(count, BATCH)
    rows, depth = blocks[0].shape
    occupied = rows // vectors
    vector_operands = [*so_far, *blocks, *thetas]
    out_shape = [jax.ShapeDtypeStruct((chips, 1, out_width), jnp.float32)]
    if screens:
        out_shape.append(jax.ShapeDtypeStruct((CORES, depth), jnp.float32))
    return pl.pallas_call(
        functools.partial(
            terms_kernel, first=first, count=count, screened=bool(screens), chunks=chunks, vectors=vectors, batch=batch
        ),
        in_specs=[SMEM] * len(screens) + [VMEM] * len(vector_operands),
        out_specs=[VMEM] * len(out_shape),
        out_shape=out_shape,
        scratch_shapes=[
            pltpu.VMEM((CORES, count * occupied, depth), thetas[0].dtype),
            pltpu.VMEM((CORES * vectors + 8, batch * occupied), jnp.float32),
        ],
        compiler_params=PARAMS,
        cost_estimate=SMALL,
        name="chip_terms",
    )(*screens, *vector_operands)


def energy_terms(rows, used):
    lane = lax.broadcasted_iota(jnp.int32, rows.shape, 1)
    return jnp.where(lane < used, rows * rows, jnp.where(lane < used + 8, -rows, 0.0))


def finish_kernel(rows_ref, bias_ref, energy_ref, bias_buf, energy_buf, sems, *, used, scale):
    chips, _, width = rows_ref.shape
    half = chips // 2
    fit = LANES // used if width == LANES else 0
    lane = lax.broadcasted_iota(jnp.int32, (1, width), 1)
    if fit and chips % fit == 0:
        for d in range(0, chips, fit):
            packed = rows_ref[d ^ half]
            for i in range(1, fit):
                packed = jnp.where(lane < i * used, packed, pltpu.roll(rows_ref[(d + i) ^ half], i * used, 1))
            bias_buf[:, d * used:(d + fit) * used] = packed
    else:
        for d in range(chips):
            bias_buf[:, d * used:(d + 1) * used] = rows_ref[d ^ half, :, :used]
    bias_copy = pltpu.make_async_copy(bias_buf, bias_ref, sems.at[0])
    bias_copy.start()
    total = energy_terms(rows_ref[0], used)
    for d in range(1, chips):
        total = total + energy_terms(rows_ref[d], used)
    energy_buf[...] = jnp.sum(total, axis=1, keepdims=True) * scale
    energy_copy = pltpu.make_async_copy(energy_buf, energy_ref, sems.at[1])
    energy_copy.start()
    bias_copy.wait()
    energy_copy.wait()


def finish(rows, used, scale):
    chips = rows.shape[0]
    shapes = [(1, chips * used), (1, 1)]
    force_bias, energy = pl.pallas_call(
        functools.partial(finish_kernel, used=used, scale=scale),
        in_specs=[VMEM],
        out_specs=[pl.BlockSpec(memory_space=pl.ANY)] * 2,
        out_shape=[jax.ShapeDtypeStruct(s, jnp.float32) for s in shapes],
        scratch_shapes=[pltpu.VMEM(s, jnp.float32) for s in shapes] + [pltpu.SemaphoreType.DMA((2,))],
        name="finish",
    )(rows)
    return force_bias, energy.reshape(1)


def body(theta, chol_tiles, screen, tile_list):
    groups = lax.axis_size("chol")
    chips = groups // CORES
    half = chips // 2
    _, occupied, _ = theta.shape
    vectors = chol_tiles.shape[2]
    used = CORES * vectors
    out_width = LANES * ((used + 8 + LANES - 1) // LANES)
    depth = chol_tiles.shape[1] * chol_tiles.shape[4]
    listing = tile_list.T

    def to_chip(x, offset):
        return lax.ppermute(x, "chol", [(i, i ^ (offset * CORES)) for i in range(groups)])

    def to_core(x):
        return lax.ppermute(x, "chol", [(i, i ^ 1) for i in range(groups)])

    far = to_chip(theta, half)

    def spread(walker, late=False):
        pieces = list(pick_tiles(listing, walker, depth, half))
        if late:
            pieces[1], near[1] = lax.optimization_barrier((pieces[1], near[1]))
        return [pieces[0]] + [to_chip(pieces[offset], offset) for offset in range(1, half)]

    near = spread(theta)
    own, own_turned = prepare_block(chol_tiles)
    other_chol = to_core(chol_tiles)
    far, other_chol, own = lax.optimization_barrier((far, other_chol, own))
    beyond = spread(far, True)
    beyond = beyond[:1] + beyond[2:] + beyond[1:2]
    other_chol, late_screen, near[-1] = lax.optimization_barrier((other_chol, screen, near[-1]))
    other, other_turned = prepare_block(other_chol)
    blocks = [own, own_turned, other, other_turned]

    screens = [screen, to_core(late_screen)]
    rows, masks = chip_terms(screens, [], blocks, near, 0, NEAR, vectors, chips, out_width)
    rows, = chip_terms([], [masks, rows], blocks, beyond, half, BEYOND, vectors, chips, out_width)
    same_core = [[(rank ^ half) * CORES + core for rank in range(chips)] for core in range(CORES)]
    back = lax.all_to_all(rows, "chol", split_axis=0, concat_axis=0, tiled=True, axis_index_groups=same_core)
    return finish(back, used, 1.0 / (2.0 * occupied * occupied))


def solution(mesh):
    in_specs = (
        P(("grp", "chol"), None, None),
        P("chol", None, None, None, None),
        P("chol", None),
        P(),
    )
    out_specs = (P(("grp", "chol"), None), P(("grp", "chol")))
    return jax.shard_map(body, mesh=mesh, in_specs=in_specs, out_specs=out_specs, check_vma=False)
```

```python
import functools

import jax
import jax.numpy as jnp
from jax import lax
from jax.experimental import pallas as pl
from jax.experimental.pallas import tpu as pltpu
from jax.sharding import PartitionSpec as P

LANES = 128
CORES = 2
VMEM_LIMIT = 32 * 1024 * 1024
NEAR = ((8, 4),)
BEYOND = ((8, 8), (8, 0))
BATCH = 4
VMEM = pl.BlockSpec(memory_space=pltpu.VMEM)
SMEM = pl.BlockSpec(memory_space=pltpu.SMEM)
PARAMS = pltpu.CompilerParams(vmem_limit_bytes=VMEM_LIMIT)
SMALL = pl.CostEstimate(flops=0, bytes_accessed=0, transcendentals=0)
NT = (((1,), (1,)), ((), ()))
NN = (((1,), (0,)), ((), ()))


def prepare_kernel(chol_ref, block_ref, turned_ref):
    _, listed, vectors, occupied, width = chol_ref.shape
    for m in range(listed):
        tile = chol_ref[0, m].reshape(vectors * occupied, width)
        block_ref[:, m * width:(m + 1) * width] = tile
        turned_ref[m * width:(m + 1) * width, :] = tile.T


def prepare_block(chol_tiles):
    _, listed, vectors, occupied, width = chol_tiles.shape
    rows, depth = vectors * occupied, listed * width
    return pl.pallas_call(
        prepare_kernel,
        in_specs=[VMEM],
        out_specs=[VMEM, VMEM],
        out_shape=[
            jax.ShapeDtypeStruct((rows, depth), chol_tiles.dtype),
            jax.ShapeDtypeStruct((depth, rows), chol_tiles.dtype),
        ],
        compiler_params=PARAMS,
        cost_estimate=SMALL,
        name="prepare_block",
    )(chol_tiles)


def pick_kernel(list_ref, theta_ref, *out_refs):
    listed = list_ref.shape[0]
    width = out_refs[0].shape[2] // listed
    me = lax.axis_index("chol")
    for offset, out_ref in enumerate(out_refs):
        device = me ^ (offset * CORES)
        for b, group in enumerate((device, device ^ 1)):
            for m in range(listed):
                start = pl.multiple_of(list_ref[m, group] * width, width)
                out_ref[b, :, m * width:(m + 1) * width] = theta_ref[0, :, pl.ds(start, width)]


def pick_tiles(listing, theta, depth, count):
    piece = jax.ShapeDtypeStruct((CORES, theta.shape[1], depth), theta.dtype)
    return pl.pallas_call(
        pick_kernel,
        in_specs=[SMEM, VMEM],
        out_specs=[VMEM] * count,
        out_shape=[piece] * count,
        compiler_params=PARAMS,
        cost_estimate=SMALL,
        name="pick_tiles",
    )(listing, theta)


def fold_rows(blocks, sub):
    high = sub < 4
    pairs = []
    for i in range(4):
        a, b = blocks[i], blocks[i + 4]
        pairs.append(jnp.where(high, a, b) + pltpu.roll(jnp.where(high, b, a), 4, 0))
    for shift in (2, 1):
        first = sub % (2 * shift) < shift
        half = len(pairs) // 2
        pairs = [
            jnp.where(
                first,
                pairs[i] + pltpu.roll(pairs[i], 8 - shift, 0),
                pairs[i + half] + pltpu.roll(pairs[i + half], shift, 0),
            )
            for i in range(half)
        ]
    return pairs[0]


def chunk_products(block_ref, turned_ref, theta, theta_turned, occupied, k0, size, by_matmul):
    span = slice(k0 * occupied, (k0 + size) * occupied)
    inner_mat = lax.dot_general(block_ref[span, :], theta_turned, NN, preferred_element_type=jnp.float32)
    if not by_matmul:
        return inner_mat, None
    turned = slice(k0 * occupied, (k0 + by_matmul) * occupied)
    return inner_mat, lax.dot_general(theta, turned_ref[:, turned], NN, preferred_element_type=jnp.float32)


def chunk_terms(inner_mat, flipped, cross, store_rows, occupied, k0, size, by_matmul):
    tiles = inner_mat.shape[1] // LANES

    low = lax.broadcasted_iota(jnp.int32, (occupied, LANES), 1) < occupied
    sub8 = lax.broadcasted_iota(jnp.int32, (8, LANES), 0)
    lane8 = lax.broadcasted_iota(jnp.int32, (8, LANES), 1)
    strip = (lane8 % occupied) // 8
    on_diag = lane8 % 8 == sub8

    def diagonal(block):
        merged = block[:8]
        for r in range(1, occupied // 8):
            merged = jnp.where(strip == r, block[8 * r:8 * r + 8], merged)
        return jnp.where(on_diag, merged, 0.0)

    for k8 in range(0, size, 8):
        for t in range(tiles):
            c0 = t * LANES
            diagonals = []
            for k in range(k8, k8 + 8, 2):
                r0 = k * occupied
                top = inner_mat[r0:r0 + occupied, c0:c0 + LANES]
                bottom = inner_mat[r0 + occupied:r0 + 2 * occupied, c0:c0 + LANES]
                if k < by_matmul:
                    other = flipped[c0:c0 + LANES, r0:r0 + LANES]
                else:
                    other = inner_mat[r0:r0 + LANES, c0:c0 + LANES].T
                f_top, f_bottom = other[:occupied], other[occupied:]
                swapped = pltpu.roll(jnp.where(low, f_bottom, f_top), occupied, 1)
                product = jnp.where(low, top, bottom) * jnp.where(low, f_top, f_bottom)
                product = product + jnp.where(low, bottom, top) * swapped
                cross[t] = cross[t] + jnp.sum(product.reshape(occupied // 8, 8, LANES), axis=0)
                diagonals.append(diagonal(top))
                diagonals.append(diagonal(bottom))
            store_rows(k0 + k8, t, fold_rows(diagonals, sub8))


def mask_kernel_rows(screen_refs, listed, width):
    return [
        jnp.concatenate(
            [jnp.full((1, width), ref[0, m].astype(jnp.float32)) for m in range(listed)], axis=1
        )
        for ref in screen_refs
    ]


def terms_kernel(*refs, first, count, screened, chunks, vectors, batch):
    if screened:
        screen_refs, refs = refs[:2], refs[2:]
    else:
        mask_ref, carried_ref, refs = refs[0], refs[1], refs[2:]
    block_refs, theta_refs, rest = refs[:4], refs[4:4 + count], refs[4 + count:]
    out_ref, picked_ref, rows_ref = rest[0], rest[-2], rest[-1]
    occupied = block_refs[0].shape[0] // vectors
    depth = block_refs[0].shape[1]
    used = CORES * vectors
    columns = batch * occupied
    tiles = columns // LANES
    me = lax.axis_index("chol")
    core = lax.rem(me, CORES)
    chip = me // CORES

    if screened:
        listed = screen_refs[0].shape[1]
        masks = mask_kernel_rows(screen_refs, listed, depth // listed)
        mask_ref = rest[1]
        for b in range(CORES):
            mask_ref[b:b + 1, :] = masks[b]
        out_ref[...] = jnp.zeros(out_ref.shape, out_ref.dtype)
    else:
        masks = [mask_ref[b:b + 1, :] for b in range(CORES)]
        out_ref[...] = carried_ref[...]
    for b in range(CORES):
        mask = masks[b].astype(picked_ref.dtype)
        for i, ref in enumerate(theta_refs):
            picked_ref[b, i * occupied:(i + 1) * occupied, :] = ref[b] * mask

    def one_batch(index):
        start = index * occupied
        rows = pl.ds(start if isinstance(index, int) else pl.multiple_of(start, columns), columns)
        cross = [jnp.zeros((8, LANES), jnp.float32) for _ in range(tiles)]
        tasks = []
        for b in range(CORES):
            theta, k0 = picked_ref[b, rows, :], 0
            walkers = (theta, theta.T)
            while k0 < vectors:
                for size, by_matmul in chunks:
                    tasks.append((b, walkers, k0, size, by_matmul))
                    k0 += size

        def products(task):
            b, walkers, k0, size, by_matmul = task
            return chunk_products(block_refs[2 * b], block_refs[2 * b + 1], *walkers, occupied, k0, size, by_matmul)

        ahead = products(tasks[0])
        for i, (b, _, k0, size, by_matmul) in enumerate(tasks):
            now, ahead = ahead, products(tasks[i + 1]) if i + 1 < len(tasks) else None
            place = (core ^ b) * vectors

            def store_rows(k, t, value, place=place):
                rows_ref[pl.ds(pl.multiple_of(place + k, 8), 8), t * LANES:(t + 1) * LANES] = value

            chunk_terms(*now, cross, store_rows, occupied, k0, size, by_matmul)
        for t in range(tiles):
            rows_ref[used:used + 8, t * LANES:(t + 1) * LANES] = cross[t]
        values = rows_ref[...]
        parts = []
        for _ in range(3):
            part = values.astype(jnp.bfloat16)
            parts.append(part)
            values = values - part.astype(jnp.float32)
        seg_row = lax.broadcasted_iota(jnp.int32, (8, columns), 0)
        seg_col = lax.broadcasted_iota(jnp.int32, (8, columns), 1)
        segment = jnp.where(seg_col // occupied == seg_row, 1.0, 0.0).astype(jnp.bfloat16)
        sums = sum(
            lax.dot_general(segment, part, NT, preferred_element_type=jnp.float32) for part in parts
        )
        for i in range(batch):
            owner = chip ^ (first + index + i) ^ (out_ref.shape[0] // 2 + 1)
            out_ref[pl.ds(owner, 1), 0, :used + 8] = sums[i:i + 1]

    if count == batch:
        one_batch(0)
    else:
        @pl.loop(0, count // batch)
        def _(step):
            one_batch(step * batch)


def chip_terms(screens, so_far, blocks, thetas, first, chunks, vectors, chips, out_width):
    count = len(thetas)
    batch = min(count, BATCH)
    rows, depth = blocks[0].shape
    occupied = rows // vectors
    vector_operands = [*so_far, *blocks, *thetas]
    out_shape = [jax.ShapeDtypeStruct((chips, 1, out_width), jnp.float32)]
    if screens:
        out_shape.append(jax.ShapeDtypeStruct((CORES, depth), jnp.float32))
    return pl.pallas_call(
        functools.partial(
            terms_kernel, first=first, count=count, screened=bool(screens), chunks=chunks, vectors=vectors, batch=batch
        ),
        in_specs=[SMEM] * len(screens) + [VMEM] * len(vector_operands),
        out_specs=[VMEM] * len(out_shape),
        out_shape=out_shape,
        scratch_shapes=[
            pltpu.VMEM((CORES, count * occupied, depth), thetas[0].dtype),
            pltpu.VMEM((CORES * vectors + 8, batch * occupied), jnp.float32),
        ],
        compiler_params=PARAMS,
        cost_estimate=SMALL,
        name="chip_terms",
    )(*screens, *vector_operands)


def energy_terms(rows, used):
    lane = lax.broadcasted_iota(jnp.int32, rows.shape, 1)
    return jnp.where(lane < used, rows * rows, jnp.where(lane < used + 8, -rows, 0.0))


def finish_kernel(rows_ref, bias_ref, energy_ref, bias_buf, energy_buf, sems, *, used, scale):
    chips, _, width = rows_ref.shape
    turn = chips // 2 + 1
    fit = LANES // used if width == LANES else 0
    lane = lax.broadcasted_iota(jnp.int32, (1, width), 1)
    if fit and chips % fit == 0:
        for d in range(0, chips, fit):
            packed = rows_ref[d ^ turn]
            for i in range(1, fit):
                packed = jnp.where(lane < i * used, packed, pltpu.roll(rows_ref[(d + i) ^ turn], i * used, 1))
            bias_buf[:, d * used:(d + fit) * used] = packed
    else:
        for d in range(chips):
            bias_buf[:, d * used:(d + 1) * used] = rows_ref[d ^ turn, :, :used]
    bias_copy = pltpu.make_async_copy(bias_buf, bias_ref, sems.at[0])
    bias_copy.start()
    total = energy_terms(rows_ref[0], used)
    for d in range(1, chips):
        total = total + energy_terms(rows_ref[d], used)
    energy_buf[...] = jnp.sum(total, axis=1, keepdims=True) * scale
    energy_copy = pltpu.make_async_copy(energy_buf, energy_ref, sems.at[1])
    energy_copy.start()
    bias_copy.wait()
    energy_copy.wait()


def finish(rows, used, scale):
    chips = rows.shape[0]
    shapes = [(1, chips * used), (1, 1)]
    force_bias, energy = pl.pallas_call(
        functools.partial(finish_kernel, used=used, scale=scale),
        in_specs=[VMEM],
        out_specs=[pl.BlockSpec(memory_space=pl.ANY)] * 2,
        out_shape=[jax.ShapeDtypeStruct(s, jnp.float32) for s in shapes],
        scratch_shapes=[pltpu.VMEM(s, jnp.float32) for s in shapes] + [pltpu.SemaphoreType.DMA((2,))],
        name="finish",
    )(rows)
    return force_bias, energy.reshape(1)


def body(theta, chol_tiles, screen, tile_list):
    groups = lax.axis_size("chol")
    chips = groups // CORES
    half = chips // 2
    _, occupied, _ = theta.shape
    vectors = chol_tiles.shape[2]
    used = CORES * vectors
    out_width = LANES * ((used + 8 + LANES - 1) // LANES)
    depth = chol_tiles.shape[1] * chol_tiles.shape[4]
    listing = tile_list.T

    def to_chip(x, offset):
        return lax.ppermute(x, "chol", [(i, i ^ (offset * CORES)) for i in range(groups)])

    def to_core(x):
        return lax.ppermute(x, "chol", [(i, i ^ 1) for i in range(groups)])

    far = to_chip(theta, half)

    def spread(walker):
        pieces = pick_tiles(listing, walker, depth, half)
        return [pieces[0]] + [to_chip(pieces[offset], offset) for offset in range(1, half)]

    near = spread(theta)
    own, own_turned = prepare_block(chol_tiles)
    other_chol = to_core(chol_tiles)
    far, near[1], other_chol, own = lax.optimization_barrier((far, near[1], other_chol, own))
    beyond = spread(far)
    other_chol, late_screen, near[-1] = lax.optimization_barrier((other_chol, screen, near[-1]))
    other, other_turned = prepare_block(other_chol)
    blocks = [own, own_turned, other, other_turned]

    screens = [screen, to_core(late_screen)]
    rows, masks = chip_terms(screens, [], blocks, near, 0, NEAR, vectors, chips, out_width)
    rows, = chip_terms([], [masks, rows], blocks, beyond, half, BEYOND, vectors, chips, out_width)
    same_core = [[(rank ^ (half + 1)) * CORES + core for rank in range(chips)] for core in range(CORES)]
    back = lax.all_to_all(rows, "chol", split_axis=0, concat_axis=0, tiled=True, axis_index_groups=same_core)
    return finish(back, used, 1.0 / (2.0 * occupied * occupied))


def solution(mesh):
    in_specs = (
        P(("grp", "chol"), None, None),
        P("chol", None, None, None, None),
        P("chol", None),
        P(),
    )
    out_specs = (P(("grp", "chol"), None), P(("grp", "chol")))
    return jax.shard_map(body, mesh=mesh, in_specs=in_specs, out_specs=out_specs, check_vma=False)
```

```python
import functools

import jax
import jax.numpy as jnp
from jax import lax
from jax.experimental import pallas as pl
from jax.experimental.pallas import tpu as pltpu
from jax.sharding import PartitionSpec as P

LANES = 128
CORES = 2
VMEM_LIMIT = 32 * 1024 * 1024
NEAR = ((8, 4),)
BEYOND = ((8, 8), (8, 0))
BATCH = 4
VMEM = pl.BlockSpec(memory_space=pltpu.VMEM)
SMEM = pl.BlockSpec(memory_space=pltpu.SMEM)
PARAMS = pltpu.CompilerParams(vmem_limit_bytes=VMEM_LIMIT)
SMALL = pl.CostEstimate(flops=0, bytes_accessed=0, transcendentals=0)
NT = (((1,), (1,)), ((), ()))
NN = (((1,), (0,)), ((), ()))


def prepare_kernel(chol_ref, block_ref, turned_ref):
    _, listed, vectors, occupied, width = chol_ref.shape
    for m in range(listed):
        tile = chol_ref[0, m].reshape(vectors * occupied, width)
        block_ref[:, m * width:(m + 1) * width] = tile
        turned_ref[m * width:(m + 1) * width, :] = tile.T


def prepare_block(chol_tiles):
    _, listed, vectors, occupied, width = chol_tiles.shape
    rows, depth = vectors * occupied, listed * width
    return pl.pallas_call(
        prepare_kernel,
        in_specs=[VMEM],
        out_specs=[VMEM, VMEM],
        out_shape=[
            jax.ShapeDtypeStruct((rows, depth), chol_tiles.dtype),
            jax.ShapeDtypeStruct((depth, rows), chol_tiles.dtype),
        ],
        compiler_params=PARAMS,
        cost_estimate=SMALL,
        name="prepare_block",
    )(chol_tiles)


def pick_kernel(list_ref, theta_ref, *out_refs):
    listed = list_ref.shape[0]
    width = out_refs[0].shape[2] // listed
    me = lax.axis_index("chol")
    for offset, out_ref in enumerate(out_refs):
        device = me ^ (offset * CORES)
        for b, group in enumerate((device, device ^ 1)):
            for m in range(listed):
                start = pl.multiple_of(list_ref[m, group] * width, width)
                out_ref[b, :, m * width:(m + 1) * width] = theta_ref[0, :, pl.ds(start, width)]


def pick_tiles(listing, theta, depth, count):
    piece = jax.ShapeDtypeStruct((CORES, theta.shape[1], depth), theta.dtype)
    return pl.pallas_call(
        pick_kernel,
        in_specs=[SMEM, VMEM],
        out_specs=[VMEM] * count,
        out_shape=[piece] * count,
        compiler_params=PARAMS,
        cost_estimate=SMALL,
        name="pick_tiles",
    )(listing, theta)


def fold_rows(blocks, sub):
    high = sub < 4
    pairs = []
    for i in range(4):
        a, b = blocks[i], blocks[i + 4]
        pairs.append(jnp.where(high, a, b) + pltpu.roll(jnp.where(high, b, a), 4, 0))
    for shift in (2, 1):
        first = sub % (2 * shift) < shift
        half = len(pairs) // 2
        pairs = [
            jnp.where(
                first,
                pairs[i] + pltpu.roll(pairs[i], 8 - shift, 0),
                pairs[i + half] + pltpu.roll(pairs[i + half], shift, 0),
            )
            for i in range(half)
        ]
    return pairs[0]


def chunk_products(block_ref, turned_ref, theta, theta_turned, occupied, k0, size, by_matmul):
    span = slice(k0 * occupied, (k0 + size) * occupied)
    inner_mat = lax.dot_general(block_ref[span, :], theta_turned, NN, preferred_element_type=jnp.float32)
    if not by_matmul:
        return inner_mat, None
    turned = slice(k0 * occupied, (k0 + by_matmul) * occupied)
    return inner_mat, lax.dot_general(theta, turned_ref[:, turned], NN, preferred_element_type=jnp.float32)


def chunk_terms(inner_mat, flipped, cross, store_rows, occupied, k0, size, by_matmul):
    tiles = inner_mat.shape[1] // LANES

    low = lax.broadcasted_iota(jnp.int32, (occupied, LANES), 1) < occupied
    sub8 = lax.broadcasted_iota(jnp.int32, (8, LANES), 0)
    lane8 = lax.broadcasted_iota(jnp.int32, (8, LANES), 1)
    strip = (lane8 % occupied) // 8
    on_diag = lane8 % 8 == sub8

    def diagonal(block):
        merged = block[:8]
        for r in range(1, occupied // 8):
            merged = jnp.where(strip == r, block[8 * r:8 * r + 8], merged)
        return jnp.where(on_diag, merged, 0.0)

    for k8 in range(0, size, 8):
        for t in range(tiles):
            c0 = t * LANES
            diagonals = []
            for k in range(k8, k8 + 8, 2):
                r0 = k * occupied
                top = inner_mat[r0:r0 + occupied, c0:c0 + LANES]
                bottom = inner_mat[r0 + occupied:r0 + 2 * occupied, c0:c0 + LANES]
                if k < by_matmul:
                    other = flipped[c0:c0 + LANES, r0:r0 + LANES]
                else:
                    other = inner_mat[r0:r0 + LANES, c0:c0 + LANES].T
                f_top, f_bottom = other[:occupied], other[occupied:]
                swapped = pltpu.roll(jnp.where(low, f_bottom, f_top), occupied, 1)
                product = jnp.where(low, top, bottom) * jnp.where(low, f_top, f_bottom)
                product = product + jnp.where(low, bottom, top) * swapped
                cross[t] = cross[t] + jnp.sum(product.reshape(occupied // 8, 8, LANES), axis=0)
                diagonals.append(diagonal(top))
                diagonals.append(diagonal(bottom))
            store_rows(k0 + k8, t, fold_rows(diagonals, sub8))


def mask_kernel_rows(screen_refs, listed, width):
    return [
        jnp.concatenate(
            [jnp.full((1, width), ref[0, m].astype(jnp.float32)) for m in range(listed)], axis=1
        )
        for ref in screen_refs
    ]


def terms_kernel(*refs, first, count, screened, chunks, vectors, batch):
    if screened:
        screen_refs, refs = refs[:2], refs[2:]
    else:
        mask_ref, carried_ref, refs = refs[0], refs[1], refs[2:]
    block_refs, theta_refs, rest = refs[:4], refs[4:4 + count], refs[4 + count:]
    out_ref, picked_ref, rows_ref = rest[0], rest[-2], rest[-1]
    occupied = block_refs[0].shape[0] // vectors
    depth = block_refs[0].shape[1]
    used = CORES * vectors
    columns = batch * occupied
    tiles = columns // LANES
    me = lax.axis_index("chol")
    core = lax.rem(me, CORES)
    chip = me // CORES

    if screened:
        listed = screen_refs[0].shape[1]
        masks = mask_kernel_rows(screen_refs, listed, depth // listed)
        mask_ref = rest[1]
        for b in range(CORES):
            mask_ref[b:b + 1, :] = masks[b]
        out_ref[...] = jnp.zeros(out_ref.shape, out_ref.dtype)
    else:
        masks = [mask_ref[b:b + 1, :] for b in range(CORES)]
        out_ref[...] = carried_ref[...]
    for b in range(CORES):
        mask = masks[b].astype(picked_ref.dtype)
        for i, ref in enumerate(theta_refs):
            picked_ref[b, i * occupied:(i + 1) * occupied, :] = ref[b] * mask

    def one_batch(index):
        start = index * occupied
        rows = pl.ds(start if isinstance(index, int) else pl.multiple_of(start, columns), columns)
        cross = [jnp.zeros((8, LANES), jnp.float32) for _ in range(tiles)]
        tasks = []
        for b in range(CORES):
            theta, k0 = picked_ref[b, rows, :], 0
            walkers = (theta, theta.T)
            while k0 < vectors:
                for size, by_matmul in chunks:
                    tasks.append((b, walkers, k0, size, by_matmul))
                    k0 += size

        def products(task):
            b, walkers, k0, size, by_matmul = task
            return chunk_products(block_refs[2 * b], block_refs[2 * b + 1], *walkers, occupied, k0, size, by_matmul)

        ahead = products(tasks[0])
        for i, (b, _, k0, size, by_matmul) in enumerate(tasks):
            now, ahead = ahead, products(tasks[i + 1]) if i + 1 < len(tasks) else None
            place = (core ^ b) * vectors

            def store_rows(k, t, value, place=place):
                rows_ref[pl.ds(pl.multiple_of(place + k, 8), 8), t * LANES:(t + 1) * LANES] = value

            chunk_terms(*now, cross, store_rows, occupied, k0, size, by_matmul)
        for t in range(tiles):
            rows_ref[used:used + 8, t * LANES:(t + 1) * LANES] = cross[t]
        values = rows_ref[...]
        parts = []
        for _ in range(3):
            part = values.astype(jnp.bfloat16)
            parts.append(part)
            values = values - part.astype(jnp.float32)
        seg_row = lax.broadcasted_iota(jnp.int32, (8, columns), 0)
        seg_col = lax.broadcasted_iota(jnp.int32, (8, columns), 1)
        segment = jnp.where(seg_col // occupied == seg_row, 1.0, 0.0).astype(jnp.bfloat16)
        sums = sum(
            lax.dot_general(segment, part, NT, preferred_element_type=jnp.float32) for part in parts
        )
        for i in range(batch):
            owner = chip ^ (first + index + i) ^ (out_ref.shape[0] // 4 + 1)
            out_ref[pl.ds(owner, 1), 0, :used + 8] = sums[i:i + 1]

    if count == batch:
        one_batch(0)
    else:
        @pl.loop(0, count // batch)
        def _(step):
            one_batch(step * batch)


def chip_terms(screens, so_far, blocks, thetas, first, chunks, vectors, chips, out_width):
    count = len(thetas)
    batch = min(count, BATCH)
    rows, depth = blocks[0].shape
    occupied = rows // vectors
    vector_operands = [*so_far, *blocks, *thetas]
    out_shape = [jax.ShapeDtypeStruct((chips, 1, out_width), jnp.float32)]
    if screens:
        out_shape.append(jax.ShapeDtypeStruct((CORES, depth), jnp.float32))
    return pl.pallas_call(
        functools.partial(
            terms_kernel, first=first, count=count, screened=bool(screens), chunks=chunks, vectors=vectors, batch=batch
        ),
        in_specs=[SMEM] * len(screens) + [VMEM] * len(vector_operands),
        out_specs=[VMEM] * len(out_shape),
        out_shape=out_shape,
        scratch_shapes=[
            pltpu.VMEM((CORES, count * occupied, depth), thetas[0].dtype),
            pltpu.VMEM((CORES * vectors + 8, batch * occupied), jnp.float32),
        ],
        compiler_params=PARAMS,
        cost_estimate=SMALL,
        name="chip_terms",
    )(*screens, *vector_operands)


def energy_terms(rows, used):
    lane = lax.broadcasted_iota(jnp.int32, rows.shape, 1)
    return jnp.where(lane < used, rows * rows, jnp.where(lane < used + 8, -rows, 0.0))


def finish_kernel(rows_ref, bias_ref, energy_ref, bias_buf, energy_buf, sems, *, used, scale):
    chips, _, width = rows_ref.shape
    turn = chips // 4 + 1
    fit = LANES // used if width == LANES else 0
    lane = lax.broadcasted_iota(jnp.int32, (1, width), 1)
    if fit and chips % fit == 0:
        for d in range(0, chips, fit):
            packed = rows_ref[d ^ turn]
            for i in range(1, fit):
                packed = jnp.where(lane < i * used, packed, pltpu.roll(rows_ref[(d + i) ^ turn], i * used, 1))
            bias_buf[:, d * used:(d + fit) * used] = packed
    else:
        for d in range(chips):
            bias_buf[:, d * used:(d + 1) * used] = rows_ref[d ^ turn, :, :used]
    bias_copy = pltpu.make_async_copy(bias_buf, bias_ref, sems.at[0])
    bias_copy.start()
    total = energy_terms(rows_ref[0], used)
    for d in range(1, chips):
        total = total + energy_terms(rows_ref[d], used)
    energy_buf[...] = jnp.sum(total, axis=1, keepdims=True) * scale
    energy_copy = pltpu.make_async_copy(energy_buf, energy_ref, sems.at[1])
    energy_copy.start()
    bias_copy.wait()
    energy_copy.wait()


def finish(rows, used, scale):
    chips = rows.shape[0]
    shapes = [(1, chips * used), (1, 1)]
    force_bias, energy = pl.pallas_call(
        functools.partial(finish_kernel, used=used, scale=scale),
        in_specs=[VMEM],
        out_specs=[pl.BlockSpec(memory_space=pl.ANY)] * 2,
        out_shape=[jax.ShapeDtypeStruct(s, jnp.float32) for s in shapes],
        scratch_shapes=[pltpu.VMEM(s, jnp.float32) for s in shapes] + [pltpu.SemaphoreType.DMA((2,))],
        name="finish",
    )(rows)
    return force_bias, energy.reshape(1)


def body(theta, chol_tiles, screen, tile_list):
    groups = lax.axis_size("chol")
    chips = groups // CORES
    half = chips // 2
    _, occupied, _ = theta.shape
    vectors = chol_tiles.shape[2]
    used = CORES * vectors
    out_width = LANES * ((used + 8 + LANES - 1) // LANES)
    depth = chol_tiles.shape[1] * chol_tiles.shape[4]
    listing = tile_list.T

    def to_chip(x, offset):
        return lax.ppermute(x, "chol", [(i, i ^ (offset * CORES)) for i in range(groups)])

    def to_core(x):
        return lax.ppermute(x, "chol", [(i, i ^ 1) for i in range(groups)])

    far = to_chip(theta, half)

    def spread(walker):
        pieces = pick_tiles(listing, walker, depth, half)
        return [pieces[0]] + [to_chip(pieces[offset], offset) for offset in range(1, half)]

    near = spread(theta)
    own, own_turned = prepare_block(chol_tiles)
    other_chol = to_core(chol_tiles)
    far, near[1], other_chol, own = lax.optimization_barrier((far, near[1], other_chol, own))
    beyond = spread(far)
    other_chol, late_screen, near[-1] = lax.optimization_barrier((other_chol, screen, near[-1]))
    other, other_turned = prepare_block(other_chol)
    blocks = [own, own_turned, other, other_turned]

    screens = [screen, to_core(late_screen)]
    rows, masks = chip_terms(screens, [], blocks, near, 0, NEAR, vectors, chips, out_width)
    rows, = chip_terms([], [masks, rows], blocks, beyond, half, BEYOND, vectors, chips, out_width)
    same_core = [[(rank ^ (half // 2 + 1)) * CORES + core for rank in range(chips)] for core in range(CORES)]
    back = lax.all_to_all(rows, "chol", split_axis=0, concat_axis=0, tiled=True, axis_index_groups=same_core)
    return finish(back, used, 1.0 / (2.0 * occupied * occupied))


def solution(mesh):
    in_specs = (
        P(("grp", "chol"), None, None),
        P("chol", None, None, None, None),
        P("chol", None),
        P(),
    )
    out_specs = (P(("grp", "chol"), None), P(("grp", "chol")))
    return jax.shard_map(body, mesh=mesh, in_specs=in_specs, out_specs=out_specs, check_vma=False)
```

```python
import functools

import jax
import jax.numpy as jnp
from jax import lax
from jax.experimental import pallas as pl
from jax.experimental.pallas import tpu as pltpu
from jax.sharding import PartitionSpec as P

LANES = 128
CORES = 2
VMEM_LIMIT = 32 * 1024 * 1024
NEAR = ((8, 4),)
BEYOND = ((8, 8), (8, 0))
BATCH = 4
VMEM = pl.BlockSpec(memory_space=pltpu.VMEM)
SMEM = pl.BlockSpec(memory_space=pltpu.SMEM)
PARAMS = pltpu.CompilerParams(vmem_limit_bytes=VMEM_LIMIT)
SMALL = pl.CostEstimate(flops=0, bytes_accessed=0, transcendentals=0)
NT = (((1,), (1,)), ((), ()))
NN = (((1,), (0,)), ((), ()))


def prepare_kernel(chol_ref, block_ref, turned_ref):
    _, listed, vectors, occupied, width = chol_ref.shape
    for m in range(listed):
        tile = chol_ref[0, m].reshape(vectors * occupied, width)
        block_ref[:, m * width:(m + 1) * width] = tile
        turned_ref[m * width:(m + 1) * width, :] = tile.T


def prepare_block(chol_tiles):
    _, listed, vectors, occupied, width = chol_tiles.shape
    rows, depth = vectors * occupied, listed * width
    return pl.pallas_call(
        prepare_kernel,
        in_specs=[VMEM],
        out_specs=[VMEM, VMEM],
        out_shape=[
            jax.ShapeDtypeStruct((rows, depth), chol_tiles.dtype),
            jax.ShapeDtypeStruct((depth, rows), chol_tiles.dtype),
        ],
        compiler_params=PARAMS,
        cost_estimate=SMALL,
        name="prepare_block",
    )(chol_tiles)


def pick_kernel(list_ref, theta_ref, *out_refs):
    listed = list_ref.shape[0]
    width = out_refs[0].shape[2] // listed
    me = lax.axis_index("chol")
    for offset, out_ref in enumerate(out_refs):
        device = me ^ (offset * CORES)
        for b, group in enumerate((device, device ^ 1)):
            for m in range(listed):
                start = pl.multiple_of(list_ref[m, group] * width, width)
                out_ref[b, :, m * width:(m + 1) * width] = theta_ref[0, :, pl.ds(start, width)]


def pick_tiles(listing, theta, depth, count):
    piece = jax.ShapeDtypeStruct((CORES, theta.shape[1], depth), theta.dtype)
    return pl.pallas_call(
        pick_kernel,
        in_specs=[SMEM, VMEM],
        out_specs=[VMEM] * count,
        out_shape=[piece] * count,
        compiler_params=PARAMS,
        cost_estimate=SMALL,
        name="pick_tiles",
    )(listing, theta)


def fold_rows(blocks, sub):
    high = sub < 4
    pairs = []
    for i in range(4):
        a, b = blocks[i], blocks[i + 4]
        pairs.append(jnp.where(high, a, b) + pltpu.roll(jnp.where(high, b, a), 4, 0))
    for shift in (2, 1):
        first = sub % (2 * shift) < shift
        half = len(pairs) // 2
        pairs = [
            jnp.where(
                first,
                pairs[i] + pltpu.roll(pairs[i], 8 - shift, 0),
                pairs[i + half] + pltpu.roll(pairs[i + half], shift, 0),
            )
            for i in range(half)
        ]
    return pairs[0]


def chunk_products(block_ref, turned_ref, theta, theta_turned, occupied, k0, size, by_matmul):
    span = slice(k0 * occupied, (k0 + size) * occupied)
    inner_mat = lax.dot_general(block_ref[span, :], theta_turned, NN, preferred_element_type=jnp.float32)
    if not by_matmul:
        return inner_mat, None
    turned = slice(k0 * occupied, (k0 + by_matmul) * occupied)
    return inner_mat, lax.dot_general(theta, turned_ref[:, turned], NN, preferred_element_type=jnp.float32)


def chunk_terms(inner_mat, flipped, cross, store_rows, occupied, k0, size, by_matmul):
    tiles = inner_mat.shape[1] // LANES

    low = lax.broadcasted_iota(jnp.int32, (occupied, LANES), 1) < occupied
    sub8 = lax.broadcasted_iota(jnp.int32, (8, LANES), 0)
    lane8 = lax.broadcasted_iota(jnp.int32, (8, LANES), 1)
    strip = (lane8 % occupied) // 8
    on_diag = lane8 % 8 == sub8

    def diagonal(block):
        merged = block[:8]
        for r in range(1, occupied // 8):
            merged = jnp.where(strip == r, block[8 * r:8 * r + 8], merged)
        return jnp.where(on_diag, merged, 0.0)

    for k8 in range(0, size, 8):
        for t in range(tiles):
            c0 = t * LANES
            diagonals = []
            for k in range(k8, k8 + 8, 2):
                r0 = k * occupied
                top = inner_mat[r0:r0 + occupied, c0:c0 + LANES]
                bottom = inner_mat[r0 + occupied:r0 + 2 * occupied, c0:c0 + LANES]
                if k < by_matmul:
                    other = flipped[c0:c0 + LANES, r0:r0 + LANES]
                else:
                    other = inner_mat[r0:r0 + LANES, c0:c0 + LANES].T
                f_top, f_bottom = other[:occupied], other[occupied:]
                swapped = pltpu.roll(jnp.where(low, f_bottom, f_top), occupied, 1)
                product = jnp.where(low, top, bottom) * jnp.where(low, f_top, f_bottom)
                product = product + jnp.where(low, bottom, top) * swapped
                cross[t] = cross[t] + jnp.sum(product.reshape(occupied // 8, 8, LANES), axis=0)
                diagonals.append(diagonal(top))
                diagonals.append(diagonal(bottom))
            store_rows(k0 + k8, t, fold_rows(diagonals, sub8))


def mask_kernel_rows(screen_refs, listed, width):
    return [
        jnp.concatenate(
            [jnp.full((1, width), ref[0, m].astype(jnp.float32)) for m in range(listed)], axis=1
        )
        for ref in screen_refs
    ]


def terms_kernel(*refs, first, count, screened, chunks, vectors, batch):
    if screened:
        screen_refs, refs = refs[:2], refs[2:]
    else:
        mask_ref, carried_ref, refs = refs[0], refs[1], refs[2:]
    block_refs, theta_refs, rest = refs[:4], refs[4:4 + count], refs[4 + count:]
    out_ref, picked_ref, rows_ref = rest[0], rest[-2], rest[-1]
    occupied = block_refs[0].shape[0] // vectors
    depth = block_refs[0].shape[1]
    used = CORES * vectors
    columns = batch * occupied
    tiles = columns // LANES
    me = lax.axis_index("chol")
    core = lax.rem(me, CORES)
    chip = me // CORES

    if screened:
        listed = screen_refs[0].shape[1]
        masks = mask_kernel_rows(screen_refs, listed, depth // listed)
        mask_ref = rest[1]
        for b in range(CORES):
            mask_ref[b:b + 1, :] = masks[b]
        out_ref[...] = jnp.zeros(out_ref.shape, out_ref.dtype)
    else:
        masks = [mask_ref[b:b + 1, :] for b in range(CORES)]
        out_ref[...] = carried_ref[...]
    for b in range(CORES):
        mask = masks[b].astype(picked_ref.dtype)
        for i, ref in enumerate(theta_refs):
            picked_ref[b, i * occupied:(i + 1) * occupied, :] = ref[b] * mask

    def one_batch(index):
        start = index * occupied
        rows = pl.ds(start if isinstance(index, int) else pl.multiple_of(start, columns), columns)
        cross = [jnp.zeros((8, LANES), jnp.float32) for _ in range(tiles)]
        tasks = []
        for b in range(CORES):
            theta, k0 = picked_ref[b, rows, :], 0
            walkers = (theta, theta.T)
            while k0 < vectors:
                for size, by_matmul in chunks:
                    tasks.append((b, walkers, k0, size, by_matmul))
                    k0 += size

        def products(task):
            b, walkers, k0, size, by_matmul = task
            return chunk_products(block_refs[2 * b], block_refs[2 * b + 1], *walkers, occupied, k0, size, by_matmul)

        ahead = products(tasks[0])
        for i, (b, _, k0, size, by_matmul) in enumerate(tasks):
            now, ahead = ahead, products(tasks[i + 1]) if i + 1 < len(tasks) else None
            place = (core ^ b) * vectors

            def store_rows(k, t, value, place=place):
                rows_ref[pl.ds(pl.multiple_of(place + k, 8), 8), t * LANES:(t + 1) * LANES] = value

            chunk_terms(*now, cross, store_rows, occupied, k0, size, by_matmul)
        for t in range(tiles):
            rows_ref[used:used + 8, t * LANES:(t + 1) * LANES] = cross[t]
        values = rows_ref[...]
        parts = []
        for _ in range(3):
            part = values.astype(jnp.bfloat16)
            parts.append(part)
            values = values - part.astype(jnp.float32)
        seg_row = lax.broadcasted_iota(jnp.int32, (8, columns), 0)
        seg_col = lax.broadcasted_iota(jnp.int32, (8, columns), 1)
        segment = jnp.where(seg_col // occupied == seg_row, 1.0, 0.0).astype(jnp.bfloat16)
        sums = sum(
            lax.dot_general(segment, part, NT, preferred_element_type=jnp.float32) for part in parts
        )
        for i in range(batch):
            owner = chip ^ (first + index + i) ^ (out_ref.shape[0] * 3 // 4 + 1)
            out_ref[pl.ds(owner, 1), 0, :used + 8] = sums[i:i + 1]

    if count == batch:
        one_batch(0)
    else:
        @pl.loop(0, count // batch)
        def _(step):
            one_batch(step * batch)


def chip_terms(screens, so_far, blocks, thetas, first, chunks, vectors, chips, out_width):
    count = len(thetas)
    batch = min(count, BATCH)
    rows, depth = blocks[0].shape
    occupied = rows // vectors
    vector_operands = [*so_far, *blocks, *thetas]
    out_shape = [jax.ShapeDtypeStruct((chips, 1, out_width), jnp.float32)]
    if screens:
        out_shape.append(jax.ShapeDtypeStruct((CORES, depth), jnp.float32))
    return pl.pallas_call(
        functools.partial(
            terms_kernel, first=first, count=count, screened=bool(screens), chunks=chunks, vectors=vectors, batch=batch
        ),
        in_specs=[SMEM] * len(screens) + [VMEM] * len(vector_operands),
        out_specs=[VMEM] * len(out_shape),
        out_shape=out_shape,
        scratch_shapes=[
            pltpu.VMEM((CORES, count * occupied, depth), thetas[0].dtype),
            pltpu.VMEM((CORES * vectors + 8, batch * occupied), jnp.float32),
        ],
        compiler_params=PARAMS,
        cost_estimate=SMALL,
        name="chip_terms",
    )(*screens, *vector_operands)


def energy_terms(rows, used):
    lane = lax.broadcasted_iota(jnp.int32, rows.shape, 1)
    return jnp.where(lane < used, rows * rows, jnp.where(lane < used + 8, -rows, 0.0))


def finish_kernel(rows_ref, bias_ref, energy_ref, bias_buf, energy_buf, sems, *, used, scale):
    chips, _, width = rows_ref.shape
    turn = chips * 3 // 4 + 1
    fit = LANES // used if width == LANES else 0
    lane = lax.broadcasted_iota(jnp.int32, (1, width), 1)
    if fit and chips % fit == 0:
        for d in range(0, chips, fit):
            packed = rows_ref[d ^ turn]
            for i in range(1, fit):
                packed = jnp.where(lane < i * used, packed, pltpu.roll(rows_ref[(d + i) ^ turn], i * used, 1))
            bias_buf[:, d * used:(d + fit) * used] = packed
    else:
        for d in range(chips):
            bias_buf[:, d * used:(d + 1) * used] = rows_ref[d ^ turn, :, :used]
    bias_copy = pltpu.make_async_copy(bias_buf, bias_ref, sems.at[0])
    bias_copy.start()
    total = energy_terms(rows_ref[0], used)
    for d in range(1, chips):
        total = total + energy_terms(rows_ref[d], used)
    energy_buf[...] = jnp.sum(total, axis=1, keepdims=True) * scale
    energy_copy = pltpu.make_async_copy(energy_buf, energy_ref, sems.at[1])
    energy_copy.start()
    bias_copy.wait()
    energy_copy.wait()


def finish(rows, used, scale):
    chips = rows.shape[0]
    shapes = [(1, chips * used), (1, 1)]
    force_bias, energy = pl.pallas_call(
        functools.partial(finish_kernel, used=used, scale=scale),
        in_specs=[VMEM],
        out_specs=[pl.BlockSpec(memory_space=pl.ANY)] * 2,
        out_shape=[jax.ShapeDtypeStruct(s, jnp.float32) for s in shapes],
        scratch_shapes=[pltpu.VMEM(s, jnp.float32) for s in shapes] + [pltpu.SemaphoreType.DMA((2,))],
        name="finish",
    )(rows)
    return force_bias, energy.reshape(1)


def body(theta, chol_tiles, screen, tile_list):
    groups = lax.axis_size("chol")
    chips = groups // CORES
    half = chips // 2
    _, occupied, _ = theta.shape
    vectors = chol_tiles.shape[2]
    used = CORES * vectors
    out_width = LANES * ((used + 8 + LANES - 1) // LANES)
    depth = chol_tiles.shape[1] * chol_tiles.shape[4]
    listing = tile_list.T

    def to_chip(x, offset):
        return lax.ppermute(x, "chol", [(i, i ^ (offset * CORES)) for i in range(groups)])

    def to_core(x):
        return lax.ppermute(x, "chol", [(i, i ^ 1) for i in range(groups)])

    far = to_chip(theta, half)

    def spread(walker):
        pieces = pick_tiles(listing, walker, depth, half)
        return [pieces[0]] + [to_chip(pieces[offset], offset) for offset in range(1, half)]

    near = spread(theta)
    own, own_turned = prepare_block(chol_tiles)
    other_chol = to_core(chol_tiles)
    far, near[1], other_chol, own = lax.optimization_barrier((far, near[1], other_chol, own))
    beyond = spread(far)
    other_chol, late_screen, near[-1] = lax.optimization_barrier((other_chol, screen, near[-1]))
    other, other_turned = prepare_block(other_chol)
    blocks = [own, own_turned, other, other_turned]

    screens = [screen, to_core(late_screen)]
    rows, masks = chip_terms(screens, [], blocks, near, 0, NEAR, vectors, chips, out_width)
    rows, = chip_terms([], [masks, rows], blocks, beyond, half, BEYOND, vectors, chips, out_width)
    same_core = [[(rank ^ (half * 3 // 2 + 1)) * CORES + core for rank in range(chips)] for core in range(CORES)]
    back = lax.all_to_all(rows, "chol", split_axis=0, concat_axis=0, tiled=True, axis_index_groups=same_core)
    return finish(back, used, 1.0 / (2.0 * occupied * occupied))


def solution(mesh):
    in_specs = (
        P(("grp", "chol"), None, None),
        P("chol", None, None, None, None),
        P("chol", None),
        P(),
    )
    out_specs = (P(("grp", "chol"), None), P(("grp", "chol")))
    return jax.shard_map(body, mesh=mesh, in_specs=in_specs, out_specs=out_specs, check_vma=False)
```
